512 devices in a mesh: dp: 32 (over z, x), chan: 16 (over y, core).
Axes of the slice: x: 4, y: 8, z: 8, core: 2. Of those that a mesh axis runs over, the one named last changes fastest.
Arguments:
- tokens: bfloat16 [4096, 2560], P('dp', 'chan'), may hold values from -6 to 6
- norm_gain: float32 [2560], replicated, may hold values from 0.5 to 1.5
- in_weight: bfloat16 [2560, 2, 5120], P(None, None, 'chan'), may hold values from -0.125 to 0.125
- conv_weight: float32 [4, 5120], P(None, 'chan'), may hold values from -3 to 3
- conv_bias: float32 [5120], P('chan'), may hold values from -3 to 3
- proj_weight: bfloat16 [5120, 192], P('chan'), may hold values from -0.078125 to 0.078125
- dt_weight: bfloat16 [160, 5120], P(None, 'chan'), may hold values from -0.5 to 0.5
- dt_bias: float32 [5120], P('chan'), may hold values from -6 to -2
- decay_rate: float32 [5120, 16], P('chan'), may hold values from 1e-05 to 8
- skip_gain: float32 [5120], P('chan'), may hold values from 0.5 to 1.5
- doc_starts: int32 [4096], P('dp'), may hold values from 0 to 1, as said below
- group_target: int32 [512], P('dp'), may hold values from 0 to 511, as said below
Outputs:
- mixed: bfloat16 [4096, 5120], P('dp', 'chan')
The draws below stay inside these ranges and needn't reach their ends.
Inputs may be any that keep to these rules, and one draw needn't show every extreme that they name: doc_starts is 1 at the first byte of each document; its entry 0 is 1. group_target is a permutation of the group positions; every device receives 16 groups; every device sends its 16 groups to 16 distinct devices, exactly 1 group to each of them.
All inputs are finite; a program needn't handle non-finite values.
Results may differ from the reference program's by a relative error of at most 0.014.
Values may be sent and summed in bfloat16 or wider, within the bound.
No kernel may reach another device: no remote copies, remote signals or barrier semaphores. Data moves between devices by JAX's collectives and lax.ppermute only.
A program may use at most 64 MiB of HBM per device.

```python
import math
import jax
import jax.numpy as jnp
from jax import lax

D = 2560
DI = 5120
N = 16
R = 160
KCONV = 4
CH_DEV = 16
CAP = 1
TOK_DEV = 128
TOKENS = 4096
N_DP = 32


def draw_doc_starts(key, part):
    key = jax.random.fold_in(key, 11)
    level_key, value_key = jax.random.split(key)
    device_blocks = TOKENS // TOK_DEV
    levels = jax.random.randint(level_key, (device_blocks,), 0, 11)
    limits = jnp.repeat(jnp.left_shift(jnp.ones((device_blocks,), jnp.int32), levels), TOK_DEV)
    values = jax.random.randint(value_key, (TOKENS,), 0, 64 * TOK_DEV)
    starts = (values < limits).astype(jnp.int32)
    return starts.at[0].set(1)


def draw_group_target(key, part):
    key = jax.random.fold_in(key, 23)
    keys = jax.random.split(key, 6)
    spread_count = CH_DEV // CAP
    placement = jax.random.permutation(keys[0], N_DP)
    relabel = jax.random.permutation(keys[1], N_DP)
    slot_order = jax.random.permutation(keys[3], CH_DEV)
    slot_shift = jax.random.randint(keys[4], (N_DP,), 0, CH_DEV)
    group_shift = jax.random.randint(keys[5], (N_DP,), 0, CH_DEV)
    sender = jnp.arange(N_DP, dtype=jnp.int32)[:, None]
    local = jnp.arange(CH_DEV, dtype=jnp.int32)[None, :]
    turn = (local + group_shift[:, None]) % CH_DEV
    offset = turn % spread_count
    target_dev = relabel[(placement[sender] + offset) % N_DP]
    target_slot = (slot_order[turn] + slot_shift[target_dev]) % CH_DEV
    return (target_dev * CH_DEV + target_slot).reshape(-1).astype(jnp.int32)


def block_scale(stream_key, extent, shards, low, top_value):
    def one(dim, shards_of):
        draws = jax.random.uniform(jax.random.fold_in(jax.random.fold_in(stream_key, 6), dim), (shards_of,), jnp.float32, low / len(shards), top_value / len(shards))
        return jnp.repeat(jnp.exp(draws), extent[dim] // shards_of).reshape((-1,) + (1,) * (len(extent) - dim - 1))

    level = one(*shards[0])
    for cut in shards[1:]:
        level = level * one(*cut)
    return level


def scatter_about(key, shape, scale, most, cuts=(), kind=jnp.bfloat16):
    factor_of = block_scale(key, shape, cuts, -0.22, 0.18) if cuts else 1.0
    entries = jax.random.normal(key, shape, jnp.float32) * scale * factor_of
    return jnp.minimum(jnp.maximum(entries, -most), most).astype(kind)


def setup_inputs(seed: int = 0) -> dict:
    key_of = jax.random.split(jax.random.key(seed), 13)
    return {
        "tokens": scatter_about(key_of[0], (TOKENS, D), 1.0, 6.0, ((0, 32), (1, 16))),
        "norm_gain": jnp.clip(1.0 + 0.1 * jax.random.normal(key_of[1], (D,), jnp.float32), 0.5, 1.5),
        "in_weight": scatter_about(key_of[2], (D, 2, DI), D ** -0.5, 0.125, ((2, 16),)),
        "conv_weight": scatter_about(key_of[3], (KCONV, DI), KCONV ** -0.5, 3.0, ((1, 16),), jnp.float32),
        "conv_bias": scatter_about(key_of[4], (DI,), 0.5, 3.0, ((0, 16),), jnp.float32),
        "proj_weight": scatter_about(key_of[5], (DI, R + 2 * N), DI ** -0.5, 0.078125, ((0, 16),)),
        "dt_weight": scatter_about(key_of[6], (R, DI), R ** -0.5, 0.5, ((1, 16),)),
        "dt_bias": jnp.clip(-6.0 + 4.0 * jax.random.uniform(key_of[7], (DI,), jnp.float32) ** block_scale(key_of[7], (DI,), ((0, 16),), -0.2, 0.2), -6.0, -2.0),
        "decay_rate": jnp.clip(jnp.exp(math.log(8.0) - 13.592367 * jax.random.uniform(key_of[8], (DI, N), jnp.float32) ** block_scale(key_of[8], (DI, N), ((0, 16),), -0.2, 0.2)), 9.999999747378752e-06, 8.0),
        "skip_gain": jnp.clip(0.5 + 1.0 * jax.random.uniform(key_of[9], (DI,), jnp.float32) ** block_scale(key_of[9], (DI,), ((0, 16),), -0.2, 0.2), 0.5, 1.5),
        "doc_starts": draw_doc_starts(jax.random.fold_in(key_of[12], 71), 0),
        "group_target": draw_group_target(jax.random.fold_in(key_of[12], 71), 0),
    }


epsilon = 1e-05

def reference(tokens, norm_gain, in_weight, conv_weight, conv_bias, proj_weight, dt_weight, dt_bias, decay_rate, skip_gain, doc_starts, group_target):
    total_groups = group_target.shape[0]
    row_total = tokens.shape[0]
    width = tokens.shape[1]
    group_rows = row_total // total_groups
    channels = in_weight.shape[2]
    kernel = conv_weight.shape[0]
    rank = dt_weight.shape[0]
    states = decay_rate.shape[1]
    source = jnp.zeros((total_groups,), jnp.int32).at[group_target].set(jnp.arange(total_groups, dtype=jnp.int32))
    ordered = jnp.take(tokens.reshape(total_groups, group_rows, width), source, axis=0).reshape(row_total, width)
    positions = jnp.arange(row_total, dtype=jnp.int32)
    since = positions - lax.cummax(jnp.where(doc_starts == 1, positions, 0), axis=0)
    keep = (1 - doc_starts).astype(jnp.float32)
    flat = in_weight.reshape(width, 2 * channels)
    block = math.gcd(row_total, 1024)

    def one_row(hidden, row):
        size_row, keep_row, in_row, out_row, act_row = row
        decay = jnp.exp(-size_row[:, None] * decay_rate) * keep_row
        hidden = decay * hidden + (size_row * act_row)[:, None] * in_row[None, :]
        return (hidden, lax.optimization_barrier(jnp.sum(hidden * out_row[None, :], axis=1)))

    def one_block(carried, index):
        state, tail = carried
        first = index * block
        rows_in = lax.dynamic_slice_in_dim(ordered, first, block, 0).astype(jnp.float32)
        scale = lax.rsqrt(lax.optimization_barrier(jnp.mean(rows_in * rows_in, axis=1, keepdims=True)) + epsilon)
        normed = (rows_in * scale * norm_gain[None, :]).astype(jnp.bfloat16)
        inner = jnp.dot(normed, flat, preferred_element_type=jnp.float32).astype(jnp.bfloat16)
        x_in = inner[:, :channels]
        gate_in = inner[:, channels:]
        since_blk = lax.dynamic_slice_in_dim(since, first, block, 0)
        keep_blk = lax.dynamic_slice_in_dim(keep, first, block, 0)
        extended = jnp.concatenate([tail, x_in], axis=0)
        convolved = conv_bias[None, :] + conv_weight[kernel - 1][None, :] * x_in.astype(jnp.float32)
        for back in range(1, kernel):
            term = conv_weight[kernel - 1 - back][None, :] * extended[kernel - 1 - back:kernel - 1 - back + block].astype(jnp.float32)
            convolved = convolved + jnp.where((since_blk >= back)[:, None], term, 0.0)
        activated = jax.nn.silu(convolved).astype(jnp.bfloat16)
        low = jnp.dot(activated, proj_weight, preferred_element_type=jnp.float32)
        dt_low = low[:, :rank].astype(jnp.bfloat16)
        input_map = low[:, rank:rank + states]
        output_map = low[:, rank + states:]
        step_size = jax.nn.softplus(jnp.dot(dt_low, dt_weight, preferred_element_type=jnp.float32) + dt_bias[None, :])
        act_float = activated.astype(jnp.float32)
        state, scanned = lax.scan(one_row, state, (step_size, keep_blk, input_map, output_map, act_float))
        scanned = scanned + skip_gain[None, :] * act_float
        result = (scanned * jax.nn.silu(gate_in.astype(jnp.float32))).astype(jnp.bfloat16)
        return ((state, x_in[block - (kernel - 1):]), result)
    start_state = jnp.zeros((channels, states), jnp.float32)
    start_tail = jnp.zeros((kernel - 1, channels), jnp.bfloat16)
    _, outputs = lax.scan(one_block, (start_state, start_tail), jnp.arange(row_total // block, dtype=jnp.int32))
    return outputs.reshape(row_total, channels)
```

```python
import functools
import math

import jax
import jax.numpy as jnp
from jax import lax
from jax.experimental import pallas as pl
from jax.experimental.pallas import tpu as pltpu
from jax.sharding import PartitionSpec as P

EPSILON = 1e-05
LOG2E = math.log2(math.e)
FAR = 1e30
F32 = jnp.float32
BF16 = jnp.bfloat16

VMEM = pl.BlockSpec(memory_space=pltpu.VMEM)
SMEM = pl.BlockSpec(memory_space=pltpu.SMEM)

NN = (((1,), (0,)), ((), ()))
NT = (((1,), (1,)), ((), ()))
TN = (((0,), (0,)), ((), ()))


def dot(a, b, dims=NN):
    return lax.dot_general(a, b, dims, preferred_element_type=F32)


def iota(shape, dim):
    return lax.broadcasted_iota(jnp.int32, shape, dim)


def call(body, outs, specs, args, scratch=(), limit=24):
    return pl.pallas_call(
        body,
        out_shape=outs,
        in_specs=specs,
        out_specs=jax.tree.map(lambda _: VMEM, outs),
        scratch_shapes=list(scratch),
        compiler_params=pltpu.CompilerParams(vmem_limit_bytes=limit << 20),
    )(*args)


def pack_body(slots, target, me, tok_ref, starts_ref, out_ref):
    features, tokens = tok_ref.shape
    rows = out_ref.shape[0]
    lane = iota((1, tokens), 1)
    where_to = jnp.zeros((1, tokens), jnp.int32)
    for group in range(slots):
        where_to = jnp.where((lane >> 3) == group, target[group], where_to)
    dev = where_to // slots
    slot = where_to % slots
    inner = lane & 7
    main_key = dev * 16 + inner
    tail_key = jnp.where((slot == slots - 1) & (inner >= 5), (dev + 1) * 16 + inner + 3, -1)
    slot_key = jnp.where(inner == 0, dev * 16 + 11, -1)
    row = iota((rows, tokens), 0)
    pick = jnp.where((row == main_key) | (row == tail_key), 1.0, 0.0)
    mark = jnp.where(row == slot_key, (slot + 1).astype(F32), 0.0)
    both = jnp.concatenate([pick, mark], axis=1).astype(BF16)
    values = jnp.concatenate([tok_ref[...], jnp.ones((features, tokens), BF16)], axis=1)
    pieces = dot(both, values, NT)
    fresh = 1.0 - jnp.broadcast_to(starts_ref[...].astype(F32), (8, tokens))
    lane8 = iota((8, tokens), 1)
    next_one = pltpu.roll(fresh, tokens - 1, 1)
    next_two = pltpu.roll(fresh, tokens - 2, 1)
    open_tail = jnp.where(
        lane8 == tokens - 1, 1.0, jnp.where(lane8 == tokens - 2, next_one, next_one * next_two)
    )
    open_tail = jnp.where(lane8 >= tokens - 3, open_tail, 0.0)[:1]
    open_wide = jnp.concatenate([open_tail, jnp.zeros((1, features - tokens), F32)], axis=1)
    row_wide = iota((rows, features), 0)
    pieces = jnp.where(row_wide == (me[0] + 1) * 16 + 12, open_wide, pieces)
    out_ref[...] = pieces.astype(BF16)


def place_body(in_ref, gain_ref, out_ref):
    rows, features = in_ref.shape
    tokens = out_ref.shape[1]
    arrived = in_ref[...]
    head = arrived[:, :tokens].astype(F32).reshape(rows // 16, 16, tokens)
    label = jnp.broadcast_to(head[:, 11:12, :], head.shape).reshape(rows, tokens)
    open_tail = jnp.sum(head, axis=0)[12:13]
    row = (iota((rows, tokens), 0) & 15).astype(F32)
    lane = iota((rows, tokens), 1)
    want = (((lane >> 3) + 1) * 16 + (lane & 7)).astype(F32)
    main = jnp.where(label * 16.0 + row == want, 1.0, 0.0)
    tail_row = jnp.where(lane >= tokens - 3, lane - (tokens - 3) + 8, -1).astype(F32)
    tail = jnp.where(row == tail_row, 1.0, 0.0)
    pick = jnp.concatenate([main, tail], axis=1).astype(BF16)
    found = dot(arrived, pick, TN)
    gain = gain_ref[...]
    x_main = found[:, :tokens]
    x_tail = found[:, tokens:] * open_tail
    main_sq = jnp.sum(x_main * x_main, axis=0, keepdims=True)
    tail_sq = jnp.sum(x_tail * x_tail, axis=0, keepdims=True)
    out_ref[0:features, :] = (x_main * gain).astype(BF16)
    x_tail = x_tail * gain
    packed = jnp.zeros((16, tokens), F32)
    for part in range(features // 16):
        shift = (8 * part - (tokens - 8)) % tokens
        packed = packed + pltpu.roll(x_tail[16 * part : 16 * part + 16], shift, 1)
    out_ref[features : features + 16, :] = packed.astype(BF16)
    main_high = main_sq.astype(BF16).astype(F32)
    tail_high = tail_sq.astype(BF16).astype(F32)
    line = iota((16, tokens), 0)
    sums = jnp.where(
        line == 0,
        main_high,
        jnp.where(
            line == 1,
            main_sq - main_high,
            jnp.where(line == 2, tail_high, jnp.where(line == 3, tail_sq - tail_high, 0.0)),
        ),
    )
    out_ref[features + 16 : features + 32, :] = sums.astype(BF16)


def project_body(
    features, in_ref, weight_ref, taps_ref, bias_ref, proj_ref, starts_ref,
    low_ref, act_ref, gate_ref, wide,
):
    count = in_ref.shape[0]
    tokens = in_ref.shape[2]
    channels = act_ref.shape[0]
    taps = taps_ref.shape[1]
    width = count * features
    sums = jnp.zeros((16, tokens), F32)
    for peer in range(count):
        base = peer * features
        wide[base : base + features, 0:tokens] = in_ref[peer, 0:features, :]
        packed = in_ref[peer, features : features + 16, :].astype(F32)
        sums = sums + in_ref[peer, features + 16 : features + 32, :].astype(F32)
        for part in range(features // 16):
            shift = (tokens - 8 - 8 * part) % tokens
            moved = packed if shift == 0 else pltpu.roll(packed, shift, 1)
            wide[base + 16 * part : base + 16 * part + 16, tokens:] = moved.astype(BF16)
    scale_main = lax.rsqrt((sums[0:1] + sums[1:2]) / width + EPSILON)
    scale_tail = lax.rsqrt((sums[2:3] + sums[3:4]) / width + EPSILON)
    both = dot(weight_ref[0:channels, :], wide[...])
    gate = dot(weight_ref[channels:, :], wide[:, 0:tokens])
    x_in = (both[:, :tokens] * scale_main).astype(BF16).astype(F32)
    tail = (both[:, tokens:] * scale_tail).astype(BF16).astype(F32)
    gate = (gate * scale_main).astype(BF16).astype(F32)
    gate_ref[...] = gate * (1.0 / (1.0 + jnp.exp(-gate)))
    fresh = 1.0 - jnp.broadcast_to(starts_ref[...].astype(F32), (8, tokens))
    lane8 = iota((8, tokens), 1)
    lane = iota((channels, tokens), 1)
    convolved = bias_ref[...] + taps_ref[:, taps - 1 : taps] * x_in
    mask = fresh
    for back in range(1, taps):
        if back > 1:
            mask = mask * jnp.where(lane8 < back - 1, 1.0, pltpu.roll(fresh, back - 1, 1))
        behind = pltpu.roll(jnp.where(lane >= tokens - back, tail, x_in), back, 1)
        tap = taps_ref[:, taps - 1 - back : taps - back]
        convolved = convolved + jnp.where(mask[:1] > 0.5, tap * behind, 0.0)
    act = (convolved * (1.0 / (1.0 + jnp.exp(-convolved)))).astype(BF16)
    act_ref[...] = act
    low_ref[...] = dot(proj_ref[...], act).astype(BF16)


def scan_body(
    rank, in_ref, act_ref, dtw_ref, bias_ref, rate_ref, skip_ref, starts_ref,
    out_ref, elapsed_ref, map_ref, send_ref, decay_step, drive_step, hidden,
):
    tokens = in_ref.shape[2]
    states, channels = rate_ref.shape
    low = in_ref[0].astype(F32)
    for peer in range(1, in_ref.shape[0]):
        low = low + in_ref[peer].astype(F32)
    dt_low = low[:rank].astype(BF16)
    in_map = low[rank : rank + states]
    out_map = low[rank + states :]
    raw = dot(dt_low, dtw_ref[...], TN) + bias_ref[...]
    step = jnp.maximum(raw, 0.0) + jnp.log1p(jnp.exp(-jnp.abs(raw)))
    act = jnp.transpose(act_ref[...].astype(F32))
    out_ref[...] = skip_ref[...] * act
    drive_step[...] = step * act
    first = jnp.transpose(jnp.broadcast_to(starts_ref[...].astype(F32), (tokens, tokens)))
    first = first[:, :1]
    step = jnp.where(first > 0.5, FAR, step)
    decay_step[...] = step
    high = step.astype(BF16)
    rest = (step - high.astype(F32)).astype(BF16)
    lower = jnp.where(iota((tokens, tokens), 0) >= iota((tokens, tokens), 1), 1.0, 0.0).astype(BF16)
    elapsed = dot(lower, high) + dot(lower, rest)
    elapsed_ref[...] = elapsed
    spread = jnp.where((iota((states, tokens), 1) & (states - 1)) == iota((states, tokens), 0), 1.0, 0.0)
    maps = dot(out_map.astype(BF16), spread.astype(BF16), TN)
    own = (iota((tokens, tokens), 1) // states) == (iota((tokens, tokens), 0) & 7)
    maps = jnp.where(own, maps, 0.0).astype(BF16)
    map_ref[...] = maps
    rate = rate_ref[...] * (-LOG2E)
    state = jnp.zeros((states, channels), F32)
    for block in range(tokens // 8):
        for inner in range(8):
            t = block * 8 + inner
            decay = jnp.exp2(decay_step[t : t + 1, :] * rate)
            state = decay * state + drive_step[t : t + 1, :] * in_map[:, t : t + 1]
            hidden[inner * states : (inner + 1) * states, :] = state.astype(BF16)
        out_ref[block * 8 : block * 8 + 8, :] += dot(maps[block * 8 : block * 8 + 8], hidden[...])
    last = elapsed[tokens - 1 : tokens]
    last_high = last.astype(BF16).astype(F32)
    line = iota((16, channels), 0)
    ends = jnp.where(line == 0, last_high, jnp.where(line == 1, last - last_high, 0.0)).astype(BF16)
    final = state.astype(BF16)
    for peer in range(send_ref.shape[0]):
        send_ref[peer, 0:states, :] = final
        send_ref[peer, states : states + 16, :] = ends


def finish_body(me, in_ref, rate_ref, out_in_ref, elapsed_ref, map_ref, gate_ref, mixed_ref, carried):
    states, channels = rate_ref.shape
    tokens = elapsed_ref.shape[0]
    rate = rate_ref[...] * (-LOG2E)
    state = jnp.zeros((states, channels), F32)
    for peer in range(in_ref.shape[0]):
        ends = in_ref[peer, states : states + 16, :].astype(F32)
        length = ends[0:1] + ends[1:2]
        final = in_ref[peer, 0:states, :].astype(F32)
        state = jnp.where(peer < me[0], jnp.exp2(length * rate) * state + final, state)
    corrected = []
    for block in range(tokens // 8):
        for inner in range(8):
            t = block * 8 + inner
            value = jnp.exp2(elapsed_ref[t : t + 1, :] * rate) * state
            carried[inner * states : (inner + 1) * states, :] = value.astype(BF16)
        corrected.append(
            out_in_ref[block * 8 : block * 8 + 8, :]
            + dot(map_ref[block * 8 : block * 8 + 8, :], carried[...])
        )
    scanned = jnp.transpose(jnp.concatenate(corrected, axis=0))
    mixed_ref[...] = (scanned * gate_ref[...]).astype(BF16)


def local(
    tokens, norm_gain, in_weight, conv_weight, conv_bias, proj_weight, dt_weight, dt_bias,
    decay_rate, skip_gain, doc_starts, group_target,
):
    peers = lax.axis_size("dp")
    row_count, features = tokens.shape
    slots = group_target.shape[0]
    width = in_weight.shape[0]
    channels = in_weight.shape[2]
    rank = dt_weight.shape[0]
    states = decay_rate.shape[1]
    shape = jax.ShapeDtypeStruct
    me = lax.axis_index("dp").astype(jnp.int32).reshape(1)
    starts = doc_starts.reshape(1, row_count)
    my_gain = lax.dynamic_slice_in_dim(norm_gain, lax.axis_index("chan") * features, features)
    my_gain = jnp.broadcast_to(my_gain[:, None], (features, row_count))
    weight = jnp.transpose(in_weight, (1, 2, 0)).reshape(2 * channels, width)
    rate = decay_rate.T

    pieces = call(
        functools.partial(pack_body, slots),
        shape((peers * 16, features), BF16),
        [SMEM, SMEM, VMEM, VMEM],
        (group_target, me, tokens.T, starts),
    )
    arrived = lax.all_to_all(pieces.reshape(peers, 16, features), "dp", 0, 0, tiled=True)
    payload = call(
        place_body,
        shape((features + 32, row_count), BF16),
        [VMEM, VMEM],
        (arrived.reshape(peers * 16, features), my_gain),
    )
    gathered = lax.all_gather(payload, "chan", axis=0)
    low, act, gate = call(
        functools.partial(project_body, features),
        (
            shape((rank + 2 * states, row_count), BF16),
            shape((channels, row_count), BF16),
            shape((channels, row_count), F32),
        ),
        [VMEM] * 6,
        (gathered, weight, conv_weight.T, conv_bias[:, None], proj_weight.T, starts),
        [pltpu.VMEM((width, 2 * row_count), BF16)],
    )
    lows = lax.all_gather(low, "chan", axis=0)
    out, elapsed, maps, send = call(
        functools.partial(scan_body, rank),
        (
            shape((row_count, channels), F32),
            shape((row_count, channels), F32),
            shape((row_count, row_count), BF16),
            shape((peers, states + 16, channels), BF16),
        ),
        [VMEM] * 7,
        (lows, act, dt_weight, dt_bias[None, :], rate, skip_gain[None, :], starts),
        [
            pltpu.VMEM((row_count, channels), F32),
            pltpu.VMEM((row_count, channels), F32),
            pltpu.VMEM((8 * states, channels), BF16),
        ],
    )
    ends = lax.all_to_all(send, "dp", 0, 0, tiled=True)
    mixed = call(
        finish_body,
        shape((channels, row_count), BF16),
        [SMEM] + [VMEM] * 6,
        (me, ends, rate, out, elapsed, maps, gate),
        [pltpu.VMEM((8 * states, channels), BF16)],
    )
    return mixed.T


def solution(mesh):
    return jax.shard_map(
        local,
        mesh=mesh,
        in_specs=(
            P("dp", "chan"),
            P(),
            P(None, None, "chan"),
            P(None, "chan"),
            P("chan"),
            P("chan", None),
            P(None, "chan"),
            P("chan"),
            P("chan", None),
            P("chan"),
            P("dp"),
            P("dp"),
        ),
        out_specs=P("dp", "chan"),
        check_vma=False,
    )
```

```python
import functools
import math

import jax
import jax.numpy as jnp
from jax import lax
from jax.experimental import pallas as pl
from jax.experimental.pallas import tpu as pltpu
from jax.sharding import PartitionSpec as P

EPSILON = 1e-05
LOG2E = math.log2(math.e)
FAR = 1e30
F32 = jnp.float32
BF16 = jnp.bfloat16

VMEM = pl.BlockSpec(memory_space=pltpu.VMEM)
SMEM = pl.BlockSpec(memory_space=pltpu.SMEM)
HBM = pl.BlockSpec(memory_space=pltpu.HBM)

NN = (((1,), (0,)), ((), ()))
NT = (((1,), (1,)), ((), ()))
TN = (((0,), (0,)), ((), ()))


def dot(a, b, dims=NN):
    return lax.dot_general(a, b, dims, preferred_element_type=F32)


def in_hbm(value):
    return pltpu.with_memory_space_constraint(value, pltpu.HBM)


def iota(shape, dim):
    return lax.broadcasted_iota(jnp.int32, shape, dim)


def call(body, outs, specs, args, scratch=(), limit=24):
    return pl.pallas_call(
        body,
        out_shape=outs,
        in_specs=specs,
        out_specs=jax.tree.map(lambda _: VMEM, outs),
        scratch_shapes=list(scratch),
        compiler_params=pltpu.CompilerParams(vmem_limit_bytes=limit << 20),
    )(*args)


def pack_body(slots, me, target_hbm, tok_hbm, starts_hbm, out_ref, starts_ref, target, tok_ref, sems):
    copies = [
        pltpu.make_async_copy(target_hbm, target, sems.at[0]),
        pltpu.make_async_copy(tok_hbm, tok_ref, sems.at[1]),
        pltpu.make_async_copy(starts_hbm, starts_ref, sems.at[2]),
    ]
    for copy in copies:
        copy.start()
    for copy in copies:
        copy.wait()
    features, tokens = tok_ref.shape
    rows = out_ref.shape[0]
    lane = iota((1, tokens), 1)
    where_to = jnp.zeros((1, tokens), jnp.int32)
    for group in range(slots):
        where_to = jnp.where((lane >> 3) == group, target[group], where_to)
    dev = where_to // slots
    slot = where_to % slots
    inner = lane & 7
    main_key = dev * 16 + inner
    tail_key = jnp.where((slot == slots - 1) & (inner >= 5), (dev + 1) * 16 + inner + 3, -1)
    slot_key = jnp.where(inner == 0, dev * 16 + 11, -1)
    row = iota((rows, tokens), 0)
    pick = jnp.where((row == main_key) | (row == tail_key), 1.0, 0.0)
    mark = jnp.where(row == slot_key, (slot + 1).astype(F32), 0.0)
    both = jnp.concatenate([pick, mark], axis=1).astype(BF16)
    values = jnp.concatenate([tok_ref[...], jnp.ones((features, tokens), BF16)], axis=1)
    pieces = dot(both, values, NT)
    fresh = 1.0 - jnp.broadcast_to(starts_ref[...].astype(F32), (8, tokens))
    lane8 = iota((8, tokens), 1)
    next_one = pltpu.roll(fresh, tokens - 1, 1)
    next_two = pltpu.roll(fresh, tokens - 2, 1)
    open_tail = jnp.where(
        lane8 == tokens - 1, 1.0, jnp.where(lane8 == tokens - 2, next_one, next_one * next_two)
    )
    open_tail = jnp.where(lane8 >= tokens - 3, open_tail, 0.0)[:1]
    open_wide = jnp.concatenate([open_tail, jnp.zeros((1, features - tokens), F32)], axis=1)
    row_wide = iota((rows, features), 0)
    pieces = jnp.where(row_wide == (me[0] + 1) * 16 + 12, open_wide, pieces)
    out_ref[...] = pieces.astype(BF16)


def fetch_body(
    weight_hbm, proj_hbm, dtw_hbm, rate_hbm, taps_hbm, conv_bias_hbm, dt_bias_hbm, skip_hbm,
    weight_ref, proj_ref, dtw_ref, rate_ref, cols_ref, rows_ref,
    taps_in, conv_bias, dt_bias, skip, sems,
):
    taps, channels = taps_in.shape
    pairs = (
        (taps_hbm, taps_in),
        (conv_bias_hbm, conv_bias),
        (dt_bias_hbm, dt_bias),
        (skip_hbm, skip),
        (weight_hbm.at[0:channels], weight_ref),
        (proj_hbm, proj_ref),
        (dtw_hbm, dtw_ref),
        (rate_hbm, rate_ref),
    )
    copies = [
        pltpu.make_async_copy(source, target, sems.at[index])
        for index, (source, target) in enumerate(pairs)
    ]
    for copy in copies:
        copy.start()
    for copy in copies[:4]:
        copy.wait()
    bias = conv_bias[...].reshape(1, channels)
    blank = jnp.zeros((8 - taps - 1, channels), F32)
    cols_ref[...] = jnp.transpose(jnp.concatenate([taps_in[...], bias, blank], axis=0))
    rows_ref[0:1, :] = dt_bias[...].reshape(1, channels)
    rows_ref[1:2, :] = skip[...].reshape(1, channels)
    for copy in copies[4:]:
        copy.wait()


def place_body(in_ref, gain_ref, out_ref):
    rows, features = in_ref.shape
    tokens = out_ref.shape[1]
    arrived = in_ref[...]
    head = arrived[:, :tokens].astype(F32).reshape(rows // 16, 16, tokens)
    label = jnp.broadcast_to(head[:, 11:12, :], head.shape).reshape(rows, tokens)
    open_tail = jnp.sum(head, axis=0)[12:13]
    row = (iota((rows, tokens), 0) & 15).astype(F32)
    lane = iota((rows, tokens), 1)
    want = (((lane >> 3) + 1) * 16 + (lane & 7)).astype(F32)
    main = jnp.where(label * 16.0 + row == want, 1.0, 0.0)
    tail_row = jnp.where(lane >= tokens - 3, lane - (tokens - 3) + 8, -1).astype(F32)
    tail = jnp.where(row == tail_row, 1.0, 0.0)
    pick = jnp.concatenate([main, tail], axis=1).astype(BF16)
    found = dot(arrived, pick, TN)
    gain = gain_ref[...]
    x_main = found[:, :tokens]
    x_tail = found[:, tokens:] * open_tail
    main_sq = jnp.sum(x_main * x_main, axis=0, keepdims=True)
    tail_sq = jnp.sum(x_tail * x_tail, axis=0, keepdims=True)
    out_ref[0:features, :] = (x_main * gain).astype(BF16)
    x_tail = x_tail * gain
    packed = jnp.zeros((16, tokens), F32)
    for part in range(features // 16):
        shift = (8 * part - (tokens - 8)) % tokens
        packed = packed + pltpu.roll(x_tail[16 * part : 16 * part + 16], shift, 1)
    out_ref[features : features + 16, :] = packed.astype(BF16)
    main_high = main_sq.astype(BF16).astype(F32)
    tail_high = tail_sq.astype(BF16).astype(F32)
    line = iota((16, tokens), 0)
    sums = jnp.where(
        line == 0,
        main_high,
        jnp.where(
            line == 1,
            main_sq - main_high,
            jnp.where(line == 2, tail_high, jnp.where(line == 3, tail_sq - tail_high, 0.0)),
        ),
    )
    out_ref[features + 16 : features + 32, :] = sums.astype(BF16)


def project_body(
    features, taps, in_ref, weight_ref, weight_hbm, taps_ref, proj_ref, starts_ref,
    low_ref, act_ref, gate_ref, wide, gate_weight, sem,
):
    count = in_ref.shape[0]
    tokens = in_ref.shape[2]
    channels = act_ref.shape[0]
    fetch = pltpu.make_async_copy(weight_hbm.at[channels:], gate_weight, sem)
    fetch.start()
    width = count * features
    sums = jnp.zeros((16, tokens), F32)
    for peer in range(count):
        base = peer * features
        wide[base : base + features, 0:tokens] = in_ref[peer, 0:features, :]
        packed = in_ref[peer, features : features + 16, :].astype(F32)
        sums = sums + in_ref[peer, features + 16 : features + 32, :].astype(F32)
        for part in range(features // 16):
            shift = (tokens - 8 - 8 * part) % tokens
            moved = packed if shift == 0 else pltpu.roll(packed, shift, 1)
            wide[base + 16 * part : base + 16 * part + 16, tokens:] = moved.astype(BF16)
    scale_main = lax.rsqrt((sums[0:1] + sums[1:2]) / width + EPSILON)
    scale_tail = lax.rsqrt((sums[2:3] + sums[3:4]) / width + EPSILON)
    both = dot(weight_ref[...], wide[...])
    x_in = (both[:, :tokens] * scale_main).astype(BF16).astype(F32)
    tail = (both[:, tokens:] * scale_tail).astype(BF16).astype(F32)
    fresh = 1.0 - jnp.broadcast_to(starts_ref[...].astype(F32), (8, tokens))
    lane8 = iota((8, tokens), 1)
    lane = iota((channels, tokens), 1)
    convolved = taps_ref[:, taps : taps + 1] + taps_ref[:, taps - 1 : taps] * x_in
    mask = fresh
    for back in range(1, taps):
        if back > 1:
            mask = mask * jnp.where(lane8 < back - 1, 1.0, pltpu.roll(fresh, back - 1, 1))
        behind = pltpu.roll(jnp.where(lane >= tokens - back, tail, x_in), back, 1)
        tap = taps_ref[:, taps - 1 - back : taps - back]
        convolved = convolved + jnp.where(mask[:1] > 0.5, tap * behind, 0.0)
    act = (convolved * (1.0 / (1.0 + jnp.exp(-convolved)))).astype(BF16)
    act_ref[...] = act
    low_ref[...] = dot(proj_ref[...], act).astype(BF16)
    fetch.wait()
    gate = dot(gate_weight[...], wide[:, 0:tokens])
    gate = (gate * scale_main).astype(BF16).astype(F32)
    gate_ref[...] = gate * (1.0 / (1.0 + jnp.exp(-gate)))


def scan_body(
    rank, in_ref, act_ref, dtw_ref, rate_ref, rows_ref, starts_ref,
    out_ref, elapsed_ref, map_ref, send_ref, decay_step, drive_step, hidden,
):
    tokens = in_ref.shape[2]
    states, channels = rate_ref.shape
    low = in_ref[0].astype(F32)
    for peer in range(1, in_ref.shape[0]):
        low = low + in_ref[peer].astype(F32)
    dt_low = low[:rank].astype(BF16)
    in_map = low[rank : rank + states]
    out_map = low[rank + states :]
    raw = dot(dt_low, dtw_ref[...], TN) + rows_ref[0:1, :]
    step = jnp.maximum(raw, 0.0) + jnp.log1p(jnp.exp(-jnp.abs(raw)))
    act = jnp.transpose(act_ref[...].astype(F32))
    out_ref[...] = rows_ref[1:2, :] * act
    drive_step[...] = step * act
    first = jnp.transpose(jnp.broadcast_to(starts_ref[...].astype(F32), (tokens, tokens)))
    first = first[:, :1]
    step = jnp.where(first > 0.5, FAR, step)
    decay_step[...] = step
    high = step.astype(BF16)
    rest = (step - high.astype(F32)).astype(BF16)
    lower = jnp.where(iota((tokens, tokens), 0) >= iota((tokens, tokens), 1), 1.0, 0.0).astype(BF16)
    elapsed = dot(lower, high) + dot(lower, rest)
    elapsed_ref[...] = elapsed
    spread = jnp.where((iota((states, tokens), 1) & (states - 1)) == iota((states, tokens), 0), 1.0, 0.0)
    maps = dot(out_map.astype(BF16), spread.astype(BF16), TN)
    own = (iota((tokens, tokens), 1) // states) == (iota((tokens, tokens), 0) & 7)
    maps = jnp.where(own, maps, 0.0).astype(BF16)
    map_ref[...] = maps
    rate = rate_ref[...] * (-LOG2E)
    state = jnp.zeros((states, channels), F32)
    for block in range(tokens // 8):
        for inner in range(8):
            t = block * 8 + inner
            decay = jnp.exp2(decay_step[t : t + 1, :] * rate)
            state = decay * state + drive_step[t : t + 1, :] * in_map[:, t : t + 1]
            hidden[inner * states : (inner + 1) * states, :] = state.astype(BF16)
        out_ref[block * 8 : block * 8 + 8, :] += dot(maps[block * 8 : block * 8 + 8], hidden[...])
    last = elapsed[tokens - 1 : tokens]
    spare = send_ref.shape[2] - channels
    parts = channels // spare
    last_high = last.astype(BF16).astype(F32)
    line = iota((states, spare), 0)
    ends = jnp.zeros((states, spare), F32)
    for part in range(parts):
        high_part = last_high[:, part * spare : part * spare + spare]
        rest_part = last[:, part * spare : part * spare + spare] - high_part
        ends = jnp.where(line == part, high_part, ends)
        ends = jnp.where(line == part + parts, rest_part, ends)
    final = jnp.concatenate([state, ends], axis=1).astype(BF16)
    for peer in range(send_ref.shape[0]):
        send_ref[peer] = final


def finish_body(me, in_ref, rate_ref, out_in_ref, elapsed_ref, map_ref, gate_ref, mixed_ref, carried):
    states, channels = rate_ref.shape
    tokens = elapsed_ref.shape[0]
    rate = rate_ref[...] * (-LOG2E)
    state = jnp.zeros((states, channels), F32)
    parts = channels // (in_ref.shape[2] - channels)
    for peer in range(in_ref.shape[0]):
        message = in_ref[peer].astype(F32)
        final = message[:, :channels]
        ends = message[:parts, channels:] + message[parts : 2 * parts, channels:]
        length = jnp.concatenate([ends[part : part + 1] for part in range(parts)], axis=1)
        state = jnp.where(peer < me[0], jnp.exp2(length * rate) * state + final, state)
    corrected = []
    for block in range(tokens // 8):
        for inner in range(8):
            t = block * 8 + inner
            value = jnp.exp2(elapsed_ref[t : t + 1, :] * rate) * state
            carried[inner * states : (inner + 1) * states, :] = value.astype(BF16)
        corrected.append(
            out_in_ref[block * 8 : block * 8 + 8, :]
            + dot(map_ref[block * 8 : block * 8 + 8, :], carried[...])
        )
    scanned = jnp.transpose(jnp.concatenate(corrected, axis=0))
    mixed_ref[...] = (scanned * gate_ref[...]).astype(BF16)


def local(
    tokens, norm_gain, in_weight, conv_weight, conv_bias, proj_weight, dt_weight, dt_bias,
    decay_rate, skip_gain, doc_starts, group_target,
):
    peers = lax.axis_size("dp")
    row_count, features = tokens.shape
    slots = group_target.shape[0]
    width = in_weight.shape[0]
    channels = in_weight.shape[2]
    rank = dt_weight.shape[0]
    states = decay_rate.shape[1]
    shape = jax.ShapeDtypeStruct
    me = lax.axis_index("dp").astype(jnp.int32).reshape(1)
    starts = doc_starts.reshape(1, row_count)
    my_gain = lax.dynamic_slice_in_dim(norm_gain, lax.axis_index("chan") * features, features)
    my_gain = jnp.broadcast_to(my_gain[:, None], (features, row_count))
    weight = jnp.transpose(in_weight, (1, 2, 0)).reshape(2 * channels, width)
    pieces, starts = call(
        functools.partial(pack_body, slots),
        (shape((peers * 16, features), BF16), shape((1, row_count), jnp.int32)),
        [SMEM, HBM, HBM, HBM],
        (me, in_hbm(group_target), in_hbm(tokens.T), in_hbm(starts)),
        [
            pltpu.SMEM((slots,), jnp.int32),
            pltpu.VMEM((features, row_count), BF16),
            pltpu.SemaphoreType.DMA((3,)),
        ],
    )
    weight = in_hbm(weight)
    sources = (proj_weight.T, dt_weight, decay_rate.T, conv_weight, conv_bias, dt_bias, skip_gain)
    scan_weight, proj, dtw, rate, cols, rows = call(
        fetch_body,
        (
            shape((channels, width), BF16),
            shape((rank + 2 * states, channels), BF16),
            shape((rank, channels), BF16),
            shape((states, channels), F32),
            shape((channels, 8), F32),
            shape((8, channels), F32),
        ),
        [HBM] * 8,
        (weight, *(in_hbm(source) for source in sources)),
        [
            pltpu.VMEM(conv_weight.shape, F32),
            pltpu.VMEM((channels,), F32),
            pltpu.VMEM((channels,), F32),
            pltpu.VMEM((channels,), F32),
            pltpu.SemaphoreType.DMA((8,)),
        ],
    )
    arrived = lax.all_to_all(pieces.reshape(peers, 16, features), "dp", 0, 0, tiled=True)
    payload = call(
        place_body,
        shape((features + 32, row_count), BF16),
        [VMEM, VMEM],
        (arrived.reshape(peers * 16, features), my_gain),
    )
    gathered = lax.all_gather(payload, "chan", axis=0)
    low, act, gate = call(
        functools.partial(project_body, features, conv_weight.shape[0]),
        (
            shape((rank + 2 * states, row_count), BF16),
            shape((channels, row_count), BF16),
            shape((channels, row_count), F32),
        ),
        [VMEM, VMEM, HBM, VMEM, VMEM, VMEM],
        (gathered, scan_weight, weight, cols, proj, starts),
        [
            pltpu.VMEM((width, 2 * row_count), BF16),
            pltpu.VMEM((channels, width), BF16),
            pltpu.SemaphoreType.DMA,
        ],
    )
    lows = lax.all_gather(low, "chan", axis=0)
    out, elapsed, maps, send = call(
        functools.partial(scan_body, rank),
        (
            shape((row_count, channels), F32),
            shape((row_count, channels), F32),
            shape((row_count, row_count), BF16),
            shape((peers, states, -(-channels // 128) * 128), BF16),
        ),
        [VMEM] * 6,
        (lows, act, dtw, rate, rows, starts),
        [
            pltpu.VMEM((row_count, channels), F32),
            pltpu.VMEM((row_count, channels), F32),
            pltpu.VMEM((8 * states, channels), BF16),
        ],
    )
    ends = lax.all_to_all(send, "dp", 0, 0, tiled=True)
    mixed = call(
        finish_body,
        shape((channels, row_count), BF16),
        [SMEM] + [VMEM] * 6,
        (me, ends, rate, out, elapsed, maps, gate),
        [pltpu.VMEM((8 * states, channels), BF16)],
    )
    return mixed.T


def solution(mesh):
    return jax.shard_map(
        local,
        mesh=mesh,
        in_specs=(
            P("dp", "chan"),
            P(),
            P(None, None, "chan"),
            P(None, "chan"),
            P("chan"),
            P("chan", None),
            P(None, "chan"),
            P("chan"),
            P("chan", None),
            P("chan"),
            P("dp"),
            P("dp"),
        ),
        out_specs=P("dp", "chan"),
        check_vma=False,
    )
```

```python
import functools
import math

import jax
import jax.numpy as jnp
from jax import lax
from jax.experimental import pallas as pl
from jax.experimental.pallas import tpu as pltpu
from jax.sharding import PartitionSpec as P

EPSILON = 1e-05
LOG2E = math.log2(math.e)
FAR = 1e30
F32 = jnp.float32
BF16 = jnp.bfloat16

VMEM = pl.BlockSpec(memory_space=pltpu.VMEM)
SMEM = pl.BlockSpec(memory_space=pltpu.SMEM)
HBM = pl.BlockSpec(memory_space=pltpu.HBM)

NN = (((1,), (0,)), ((), ()))
NT = (((1,), (1,)), ((), ()))
TN = (((0,), (0,)), ((), ()))


def dot(a, b, dims=NN):
    return lax.dot_general(a, b, dims, preferred_element_type=F32)


def in_hbm(value):
    return pltpu.with_memory_space_constraint(value, pltpu.HBM)


def iota(shape, dim):
    return lax.broadcasted_iota(jnp.int32, shape, dim)


def call(body, outs, specs, args, scratch=(), limit=24):
    return pl.pallas_call(
        body,
        out_shape=outs,
        in_specs=specs,
        out_specs=jax.tree.map(lambda _: VMEM, outs),
        scratch_shapes=list(scratch),
        compiler_params=pltpu.CompilerParams(vmem_limit_bytes=limit << 20),
    )(*args)


def pack_body(slots, me, target_hbm, tok_hbm, starts_hbm, out_ref, starts_ref, target, tok_ref, sems):
    copies = [
        pltpu.make_async_copy(target_hbm, target, sems.at[0]),
        pltpu.make_async_copy(tok_hbm, tok_ref, sems.at[1]),
        pltpu.make_async_copy(starts_hbm, starts_ref, sems.at[2]),
    ]
    for copy in copies:
        copy.start()
    for copy in copies:
        copy.wait()
    features, tokens = tok_ref.shape
    rows = out_ref.shape[0]
    lane = iota((1, tokens), 1)
    where_to = jnp.zeros((1, tokens), jnp.int32)
    for group in range(slots):
        where_to = jnp.where((lane >> 3) == group, target[group], where_to)
    dev = where_to // slots
    slot = where_to % slots
    inner = lane & 7
    main_key = dev * 16 + inner
    tail_key = jnp.where((slot == slots - 1) & (inner >= 5), (dev + 1) * 16 + inner + 3, -1)
    slot_key = jnp.where(inner == 0, dev * 16 + 11, -1)
    row = iota((rows, tokens), 0)
    pick = jnp.where((row == main_key) | (row == tail_key), 1.0, 0.0)
    mark = jnp.where(row == slot_key, (slot + 1).astype(F32), 0.0)
    both = jnp.concatenate([pick, mark], axis=1).astype(BF16)
    values = jnp.concatenate([tok_ref[...], jnp.ones((features, tokens), BF16)], axis=1)
    pieces = dot(both, values, NT)
    fresh = 1.0 - jnp.broadcast_to(starts_ref[...].astype(F32), (8, tokens))
    lane8 = iota((8, tokens), 1)
    next_one = pltpu.roll(fresh, tokens - 1, 1)
    next_two = pltpu.roll(fresh, tokens - 2, 1)
    open_tail = jnp.where(
        lane8 == tokens - 1, 1.0, jnp.where(lane8 == tokens - 2, next_one, next_one * next_two)
    )
    open_tail = jnp.where(lane8 >= tokens - 3, open_tail, 0.0)[:1]
    open_wide = jnp.concatenate([open_tail, jnp.zeros((1, features - tokens), F32)], axis=1)
    row_wide = iota((rows, features), 0)
    pieces = jnp.where(row_wide == (me[0] + 1) * 16 + 12, open_wide, pieces)
    out_ref[...] = pieces.astype(BF16)


def fetch_body(
    weight_hbm, proj_hbm, dtw_hbm, rate_hbm, taps_hbm, conv_bias_hbm, dt_bias_hbm, skip_hbm,
    weight_ref, proj_ref, dtw_ref, rate_ref, cols_ref, rows_ref,
    taps_in, conv_bias, dt_bias, skip, sems,
):
    taps, channels = taps_in.shape
    pairs = (
        (taps_hbm, taps_in),
        (conv_bias_hbm, conv_bias),
        (dt_bias_hbm, dt_bias),
        (skip_hbm, skip),
        (weight_hbm.at[0:channels], weight_ref),
        (proj_hbm, proj_ref),
        (dtw_hbm, dtw_ref),
        (rate_hbm, rate_ref),
    )
    copies = [
        pltpu.make_async_copy(source, target, sems.at[index])
        for index, (source, target) in enumerate(pairs)
    ]
    for copy in copies:
        copy.start()
    for copy in copies[:4]:
        copy.wait()
    bias = conv_bias[...].reshape(1, channels)
    blank = jnp.zeros((8 - taps - 1, channels), F32)
    cols_ref[...] = jnp.transpose(jnp.concatenate([taps_in[...], bias, blank], axis=0))
    rows_ref[0:1, :] = dt_bias[...].reshape(1, channels)
    rows_ref[1:2, :] = skip[...].reshape(1, channels)
    for copy in copies[4:]:
        copy.wait()


def place_body(in_ref, gain_ref, out_ref):
    rows, features = in_ref.shape
    tokens = out_ref.shape[1]
    arrived = in_ref[...]
    head = arrived[:, :tokens].astype(F32).reshape(rows // 16, 16, tokens)
    label = jnp.broadcast_to(head[:, 11:12, :], head.shape).reshape(rows, tokens)
    open_tail = jnp.sum(head, axis=0)[12:13]
    row = (iota((rows, tokens), 0) & 15).astype(F32)
    lane = iota((rows, tokens), 1)
    want = (((lane >> 3) + 1) * 16 + (lane & 7)).astype(F32)
    main = jnp.where(label * 16.0 + row == want, 1.0, 0.0)
    tail_row = jnp.where(lane >= tokens - 3, lane - (tokens - 3) + 8, -1).astype(F32)
    tail = jnp.where(row == tail_row, 1.0, 0.0)
    pick = jnp.concatenate([main, tail], axis=1).astype(BF16)
    found = dot(arrived, pick, TN)
    gain = gain_ref[...]
    x_main = found[:, :tokens]
    x_tail = found[:, tokens:] * open_tail
    main_sq = jnp.sum(x_main * x_main, axis=0, keepdims=True)
    tail_sq = jnp.sum(x_tail * x_tail, axis=0, keepdims=True)
    out_ref[0:features, :] = (x_main * gain).astype(BF16)
    x_tail = x_tail * gain
    packed = jnp.zeros((16, tokens), F32)
    for part in range(features // 16):
        shift = (8 * part - (tokens - 8)) % tokens
        packed = packed + pltpu.roll(x_tail[16 * part : 16 * part + 16], shift, 1)
    out_ref[features : features + 16, :] = packed.astype(BF16)
    main_high = main_sq.astype(BF16).astype(F32)
    tail_high = tail_sq.astype(BF16).astype(F32)
    line = iota((16, tokens), 0)
    sums = jnp.where(
        line == 0,
        main_high,
        jnp.where(
            line == 1,
            main_sq - main_high,
            jnp.where(line == 2, tail_high, jnp.where(line == 3, tail_sq - tail_high, 0.0)),
        ),
    )
    out_ref[features + 16 : features + 32, :] = sums.astype(BF16)


def project_body(
    features, taps, in_ref, weight_ref, taps_ref, proj_ref, starts_ref, low_ref, act_ref, wide,
):
    count = in_ref.shape[0]
    tokens = in_ref.shape[2]
    channels = act_ref.shape[0]
    width = count * features
    sums = jnp.zeros((16, tokens), F32)
    for peer in range(count):
        base = peer * features
        wide[base : base + features, 0:tokens] = in_ref[peer, 0:features, :]
        packed = in_ref[peer, features : features + 16, :].astype(F32)
        sums = sums + in_ref[peer, features + 16 : features + 32, :].astype(F32)
        for part in range(features // 16):
            shift = (tokens - 8 - 8 * part) % tokens
            moved = packed if shift == 0 else pltpu.roll(packed, shift, 1)
            wide[base + 16 * part : base + 16 * part + 16, tokens:] = moved.astype(BF16)
    scale_main = lax.rsqrt((sums[0:1] + sums[1:2]) / width + EPSILON)
    scale_tail = lax.rsqrt((sums[2:3] + sums[3:4]) / width + EPSILON)
    both = dot(weight_ref[...], wide[...])
    x_in = (both[:, :tokens] * scale_main).astype(BF16).astype(F32)
    tail = (both[:, tokens:] * scale_tail).astype(BF16).astype(F32)
    fresh = 1.0 - jnp.broadcast_to(starts_ref[...].astype(F32), (8, tokens))
    lane8 = iota((8, tokens), 1)
    lane = iota((channels, tokens), 1)
    convolved = taps_ref[:, taps : taps + 1] + taps_ref[:, taps - 1 : taps] * x_in
    mask = fresh
    for back in range(1, taps):
        if back > 1:
            mask = mask * jnp.where(lane8 < back - 1, 1.0, pltpu.roll(fresh, back - 1, 1))
        behind = pltpu.roll(jnp.where(lane >= tokens - back, tail, x_in), back, 1)
        tap = taps_ref[:, taps - 1 - back : taps - back]
        convolved = convolved + jnp.where(mask[:1] > 0.5, tap * behind, 0.0)
    act = (convolved * (1.0 / (1.0 + jnp.exp(-convolved)))).astype(BF16)
    act_ref[...] = act
    low_ref[...] = dot(proj_ref[...], act).astype(BF16)


def state_body(
    rank, in_ref, act_ref, dtw_ref, rate_ref, rows_ref, starts_ref,
    send_ref, decay_step, drive_step, maps_ref,
):
    tokens = in_ref.shape[2]
    states, channels = rate_ref.shape
    low = in_ref[0].astype(F32)
    for peer in range(1, in_ref.shape[0]):
        low = low + in_ref[peer].astype(F32)
    dt_low = low[:rank].astype(BF16)
    in_map = low[rank : rank + states]
    maps_ref[...] = low[rank:]
    raw = dot(dt_low, dtw_ref[...], TN) + rows_ref[0:1, :]
    step = jnp.maximum(raw, 0.0) + jnp.log1p(jnp.exp(-jnp.abs(raw)))
    drive_step[...] = step * jnp.transpose(act_ref[...].astype(F32))
    first = jnp.transpose(jnp.broadcast_to(starts_ref[...].astype(F32), (tokens, tokens)))
    step = jnp.where(first[:, :1] > 0.5, FAR, step)
    decay_step[...] = step
    last = jnp.sum(step, axis=0, keepdims=True)
    rate = rate_ref[...] * (-LOG2E)
    state = jnp.zeros((states, channels), F32)
    for t in range(tokens):
        decay = jnp.exp2(decay_step[t : t + 1, :] * rate)
        state = decay * state + drive_step[t : t + 1, :] * in_map[:, t : t + 1]
    spare = send_ref.shape[2] - channels
    parts = channels // spare
    last_high = last.astype(BF16).astype(F32)
    line = iota((states, spare), 0)
    ends = jnp.zeros((states, spare), F32)
    for part in range(parts):
        high_part = last_high[:, part * spare : part * spare + spare]
        rest_part = last[:, part * spare : part * spare + spare] - high_part
        ends = jnp.where(line == part, high_part, ends)
        ends = jnp.where(line == part + parts, rest_part, ends)
    final = jnp.concatenate([state, ends], axis=1).astype(BF16)
    for peer in range(send_ref.shape[0]):
        send_ref[peer] = final


def side_body(
    features, in_ref, weight_hbm, act_ref, rate_ref, rows_ref, decay_step, drive_step, maps_ref,
    out_ref, elapsed_ref, map_ref, gate_ref, wide, gate_weight, hidden, sem,
):
    count = in_ref.shape[0]
    tokens = in_ref.shape[2]
    states, channels = rate_ref.shape
    fetch = pltpu.make_async_copy(weight_hbm.at[channels:], gate_weight, sem)
    fetch.start()
    sums = jnp.zeros((16, tokens), F32)
    for peer in range(count):
        wide[peer * features : (peer + 1) * features, :] = in_ref[peer, 0:features, :]
        sums = sums + in_ref[peer, features + 16 : features + 32, :].astype(F32)
    scale = lax.rsqrt((sums[0:1] + sums[1:2]) / (count * features) + EPSILON)
    in_map = maps_ref[0:states, :]
    out_map = maps_ref[states:, :]
    step = decay_step[...]
    high = step.astype(BF16)
    rest = (step - high.astype(F32)).astype(BF16)
    lower = jnp.where(iota((tokens, tokens), 0) >= iota((tokens, tokens), 1), 1.0, 0.0).astype(BF16)
    elapsed_ref[...] = dot(lower, high) + dot(lower, rest)
    spread = jnp.where((iota((states, tokens), 1) & (states - 1)) == iota((states, tokens), 0), 1.0, 0.0)
    maps = dot(out_map.astype(BF16), spread.astype(BF16), TN)
    own = (iota((tokens, tokens), 1) // states) == (iota((tokens, tokens), 0) & 7)
    maps = jnp.where(own, maps, 0.0).astype(BF16)
    map_ref[...] = maps
    out_ref[...] = rows_ref[1:2, :] * jnp.transpose(act_ref[...].astype(F32))
    rate = rate_ref[...] * (-LOG2E)
    state = jnp.zeros((states, channels), F32)
    for block in range(tokens // 8):
        for inner in range(8):
            t = block * 8 + inner
            decay = jnp.exp2(decay_step[t : t + 1, :] * rate)
            state = decay * state + drive_step[t : t + 1, :] * in_map[:, t : t + 1]
            hidden[inner * states : (inner + 1) * states, :] = state.astype(BF16)
        out_ref[block * 8 : block * 8 + 8, :] += dot(maps[block * 8 : block * 8 + 8], hidden[...])
    fetch.wait()
    gate = dot(gate_weight[...], wide[...])
    gate = (gate * scale).astype(BF16).astype(F32)
    gate_ref[...] = gate * (1.0 / (1.0 + jnp.exp(-gate)))


def finish_body(me, in_ref, rate_ref, out_in_ref, elapsed_ref, map_ref, gate_ref, mixed_ref, carried):
    states, channels = rate_ref.shape
    tokens = elapsed_ref.shape[0]
    rate = rate_ref[...] * (-LOG2E)
    state = jnp.zeros((states, channels), F32)
    parts = channels // (in_ref.shape[2] - channels)
    for peer in range(in_ref.shape[0]):
        message = in_ref[peer].astype(F32)
        final = message[:, :channels]
        ends = message[:parts, channels:] + message[parts : 2 * parts, channels:]
        length = jnp.concatenate([ends[part : part + 1] for part in range(parts)], axis=1)
        state = jnp.where(peer < me[0], jnp.exp2(length * rate) * state + final, state)
    corrected = []
    for block in range(tokens // 8):
        for inner in range(8):
            t = block * 8 + inner
            value = jnp.exp2(elapsed_ref[t : t + 1, :] * rate) * state
            carried[inner * states : (inner + 1) * states, :] = value.astype(BF16)
        corrected.append(
            out_in_ref[block * 8 : block * 8 + 8, :]
            + dot(map_ref[block * 8 : block * 8 + 8, :], carried[...])
        )
    scanned = jnp.transpose(jnp.concatenate(corrected, axis=0))
    mixed_ref[...] = (scanned * gate_ref[...]).astype(BF16)


def local(
    tokens, norm_gain, in_weight, conv_weight, conv_bias, proj_weight, dt_weight, dt_bias,
    decay_rate, skip_gain, doc_starts, group_target,
):
    peers = lax.axis_size("dp")
    row_count, features = tokens.shape
    slots = group_target.shape[0]
    width = in_weight.shape[0]
    channels = in_weight.shape[2]
    rank = dt_weight.shape[0]
    states = decay_rate.shape[1]
    shape = jax.ShapeDtypeStruct
    me = lax.axis_index("dp").astype(jnp.int32).reshape(1)
    starts = doc_starts.reshape(1, row_count)
    my_gain = lax.dynamic_slice_in_dim(norm_gain, lax.axis_index("chan") * features, features)
    my_gain = jnp.broadcast_to(my_gain[:, None], (features, row_count))
    weight = jnp.transpose(in_weight, (1, 2, 0)).reshape(2 * channels, width)
    pieces, starts = call(
        functools.partial(pack_body, slots),
        (shape((peers * 16, features), BF16), shape((1, row_count), jnp.int32)),
        [SMEM, HBM, HBM, HBM],
        (me, in_hbm(group_target), in_hbm(tokens.T), in_hbm(starts)),
        [
            pltpu.SMEM((slots,), jnp.int32),
            pltpu.VMEM((features, row_count), BF16),
            pltpu.SemaphoreType.DMA((3,)),
        ],
    )
    weight = in_hbm(weight)
    sources = (proj_weight.T, dt_weight, decay_rate.T, conv_weight, conv_bias, dt_bias, skip_gain)
    scan_weight, proj, dtw, rate, cols, rows = call(
        fetch_body,
        (
            shape((channels, width), BF16),
            shape((rank + 2 * states, channels), BF16),
            shape((rank, channels), BF16),
            shape((states, channels), F32),
            shape((channels, 8), F32),
            shape((8, channels), F32),
        ),
        [HBM] * 8,
        (weight, *(in_hbm(source) for source in sources)),
        [
            pltpu.VMEM(conv_weight.shape, F32),
            pltpu.VMEM((channels,), F32),
            pltpu.VMEM((channels,), F32),
            pltpu.VMEM((channels,), F32),
            pltpu.SemaphoreType.DMA((8,)),
        ],
    )
    arrived = lax.all_to_all(pieces.reshape(peers, 16, features), "dp", 0, 0, tiled=True)
    payload = call(
        place_body,
        shape((features + 32, row_count), BF16),
        [VMEM, VMEM],
        (arrived.reshape(peers * 16, features), my_gain),
    )
    gathered = lax.all_gather(payload, "chan", axis=0)
    low, act = call(
        functools.partial(project_body, features, conv_weight.shape[0]),
        (shape((rank + 2 * states, row_count), BF16), shape((channels, row_count), BF16)),
        [VMEM] * 5,
        (gathered, scan_weight, cols, proj, starts),
        [pltpu.VMEM((width, 2 * row_count), BF16)],
    )
    lows = lax.all_gather(low, "chan", axis=0)
    by_token = shape((row_count, channels), F32)
    send, decay_step, drive_step, maps = call(
        functools.partial(state_body, rank),
        (
            shape((peers, states, -(-channels // 128) * 128), BF16),
            by_token,
            by_token,
            shape((2 * states, row_count), F32),
        ),
        [VMEM] * 6,
        (lows, act, dtw, rate, rows, starts),
    )
    out, elapsed, own_maps, gate = call(
        functools.partial(side_body, features),
        (by_token, by_token, shape((row_count, row_count), BF16), shape((channels, row_count), F32)),
        [VMEM, HBM] + [VMEM] * 6,
        (gathered, weight, act, rate, rows, decay_step, drive_step, maps),
        [
            pltpu.VMEM((width, row_count), BF16),
            pltpu.VMEM((channels, width), BF16),
            pltpu.VMEM((8 * states, channels), BF16),
            pltpu.SemaphoreType.DMA,
        ],
    )
    ends = lax.all_to_all(send, "dp", 0, 0, tiled=True)
    mixed = call(
        finish_body,
        shape((channels, row_count), BF16),
        [SMEM] + [VMEM] * 6,
        (me, ends, rate, out, elapsed, own_maps, gate),
        [pltpu.VMEM((8 * states, channels), BF16)],
    )
    return mixed.T


def solution(mesh):
    return jax.shard_map(
        local,
        mesh=mesh,
        in_specs=(
            P("dp", "chan"),
            P(),
            P(None, None, "chan"),
            P(None, "chan"),
            P("chan"),
            P("chan", None),
            P(None, "chan"),
            P("chan"),
            P("chan", None),
            P("chan"),
            P("dp"),
            P("dp"),
        ),
        out_specs=P("dp", "chan"),
        check_vma=False,
    )
```

```python
import functools
import math

import jax
import jax.numpy as jnp
from jax import lax
from jax.experimental import pallas as pl
from jax.experimental.pallas import tpu as pltpu
from jax.sharding import PartitionSpec as P

EPSILON = 1e-05
LOG2E = math.log2(math.e)
FAR = 1e30
F32 = jnp.float32
BF16 = jnp.bfloat16

VMEM = pl.BlockSpec(memory_space=pltpu.VMEM)
SMEM = pl.BlockSpec(memory_space=pltpu.SMEM)
HBM = pl.BlockSpec(memory_space=pltpu.HBM)

NN = (((1,), (0,)), ((), ()))
NT = (((1,), (1,)), ((), ()))
TN = (((0,), (0,)), ((), ()))


def dot(a, b, dims=NN):
    return lax.dot_general(a, b, dims, preferred_element_type=F32)


def in_hbm(value):
    return pltpu.with_memory_space_constraint(value, pltpu.HBM)


def iota(shape, dim):
    return lax.broadcasted_iota(jnp.int32, shape, dim)


def call(body, outs, specs, args, scratch=(), limit=24):
    return pl.pallas_call(
        body,
        out_shape=outs,
        in_specs=specs,
        out_specs=jax.tree.map(lambda _: VMEM, outs),
        scratch_shapes=list(scratch),
        compiler_params=pltpu.CompilerParams(vmem_limit_bytes=limit << 20),
    )(*args)


def pack_body(slots, me, target_hbm, tok_hbm, starts_hbm, out_ref, starts_ref, target, tok_ref, pieces, sems):
    copies = [
        pltpu.make_async_copy(target_hbm, target, sems.at[0]),
        pltpu.make_async_copy(starts_hbm, starts_ref, sems.at[1]),
        pltpu.make_async_copy(tok_hbm, tok_ref, sems.at[2]),
    ]
    for copy in copies:
        copy.start()
    features, tokens = tok_ref.shape
    peers = pieces.shape[0]
    parts = features // 16
    pieces[...] = jnp.zeros(pieces.shape, F32)
    lane = iota((16, tokens), 1)
    source = iota((tokens, tokens), 0)
    place = iota((tokens, tokens), 1)
    late = (source < features // 2) & ((source & 7) >= 5)
    to_tail = jnp.where(
        late & (place == features // 2 + 3 * (source >> 3) + (source & 7) - 5), 1.0, 0.0
    ).astype(BF16)
    copies[2].wait()
    slabs = [tok_ref[16 * part : 16 * part + 16, :].astype(F32) for part in range(parts)]
    groups = []
    for group in range(slots):
        piece = jnp.zeros((16, tokens), F32)
        for part in range(parts):
            shift = (8 * (part - group)) % tokens
            moved = slabs[part] if shift == 0 else pltpu.roll(slabs[part], shift, 1)
            piece = jnp.where((lane >> 3) == part, moved, piece)
        groups.append(piece)
    tails = dot(jnp.concatenate(groups, axis=0).astype(BF16), to_tail)
    copies[0].wait()
    copies[1].wait()
    fresh = 1.0 - jnp.broadcast_to(starts_ref[...].astype(F32), (16, tokens))
    one = pltpu.roll(fresh, (114 - (tokens - 1)) % tokens, 1)
    two = pltpu.roll(fresh, (113 - (tokens - 1)) % tokens, 1)
    flags = jnp.where(
        lane == 115, 1.0, jnp.where(lane == 114, one, jnp.where(lane == 113, one * two, 0.0))
    )
    after = me[0] + 1
    pieces[jnp.minimum(after, peers - 1)] += jnp.where(after < peers, flags, 0.0)
    for group in range(slots):
        dev = target[group] // slots
        slot = target[group] % slots
        label = jnp.where(lane == 112, (slot + 1).astype(F32), 0.0)
        pieces[dev] += groups[group] + label
        follows = (slot == slots - 1) & (dev + 1 < peers)
        tail = jnp.where(follows, tails[16 * group : 16 * group + 16], 0.0)
        pieces[jnp.minimum(dev + 1, peers - 1)] += tail
    out_ref[...] = pieces[...].astype(BF16)


def fetch_body(
    weight_hbm, proj_hbm, dtw_hbm, rate_hbm, taps_hbm, conv_bias_hbm, dt_bias_hbm, skip_hbm,
    weight_ref, proj_ref, dtw_ref, rate_ref, cols_ref, rows_ref,
    taps_in, conv_bias, dt_bias, skip, sems,
):
    taps, channels = taps_in.shape
    pairs = (
        (taps_hbm, taps_in),
        (conv_bias_hbm, conv_bias),
        (dt_bias_hbm, dt_bias),
        (skip_hbm, skip),
        (weight_hbm.at[0:channels], weight_ref),
        (proj_hbm, proj_ref),
        (dtw_hbm, dtw_ref),
        (rate_hbm, rate_ref),
    )
    copies = [
        pltpu.make_async_copy(source, target, sems.at[index])
        for index, (source, target) in enumerate(pairs)
    ]
    for copy in copies:
        copy.start()
    for copy in copies[:4]:
        copy.wait()
    bias = conv_bias[...].reshape(1, channels)
    blank = jnp.zeros((8 - taps - 1, channels), F32)
    cols_ref[...] = jnp.transpose(jnp.concatenate([taps_in[...], bias, blank], axis=0))
    rows_ref[0:1, :] = dt_bias[...].reshape(1, channels)
    rows_ref[1:2, :] = skip[...].reshape(1, channels)
    for copy in copies[4:]:
        copy.wait()


def place_body(in_ref, gain_ref, out_ref):
    peers, _, tokens = in_ref.shape
    features = gain_ref.shape[0]
    rows = 16 * peers
    slots = tokens // 8
    parts = features // 16
    arrived = in_ref[...].reshape(rows, tokens)
    wide = arrived.astype(F32)
    label = jnp.broadcast_to(wide[:, 112:113], (rows, 16 * slots))
    key = (iota((rows, 16 * slots), 1) + 16 - (iota((rows, 16 * slots), 0) & 15)).astype(F32)
    pick = jnp.where(label * 16.0 == key, 1.0, 0.0).astype(BF16)
    ordered = dot(pick, arrived, TN)
    total = jnp.sum(wide.reshape(peers, 16, tokens), axis=0)
    lane = iota((16, tokens), 1)
    open_tail = jnp.where(lane >= tokens - 3, pltpu.roll(total, tokens - 3 - 113, 1), 0.0)
    mains, tails = [], []
    for part in range(parts):
        slab = jnp.zeros((16, tokens), F32)
        for slot in range(slots):
            shift = (8 * (slot - part)) % tokens
            piece = ordered[16 * slot : 16 * slot + 16]
            moved = piece if shift == 0 else pltpu.roll(piece, shift, 1)
            slab = jnp.where((lane >> 3) == slot, moved, slab)
        mains.append(slab)
        shift = (tokens - 3 - features // 2 - 3 * part) % tokens
        tails.append((total if shift == 0 else pltpu.roll(total, shift, 1)) * open_tail)
    x_main = jnp.concatenate(mains, axis=0)
    x_tail = jnp.concatenate(tails, axis=0)
    gain = gain_ref[...]
    main_sq = jnp.sum(x_main * x_main, axis=0, keepdims=True)
    tail_sq = jnp.sum(x_tail * x_tail, axis=0, keepdims=True)
    out_ref[0:features, :] = (x_main * gain).astype(BF16)
    x_tail = x_tail * gain
    packed = jnp.zeros((16, tokens), F32)
    for part in range(features // 16):
        shift = (8 * part - (tokens - 8)) % tokens
        packed = packed + pltpu.roll(x_tail[16 * part : 16 * part + 16], shift, 1)
    out_ref[features : features + 16, :] = packed.astype(BF16)
    main_high = main_sq.astype(BF16).astype(F32)
    tail_high = tail_sq.astype(BF16).astype(F32)
    line = iota((16, tokens), 0)
    sums = jnp.where(
        line == 0,
        main_high,
        jnp.where(
            line == 1,
            main_sq - main_high,
            jnp.where(line == 2, tail_high, jnp.where(line == 3, tail_sq - tail_high, 0.0)),
        ),
    )
    out_ref[features + 16 : features + 32, :] = sums.astype(BF16)


def project_body(
    features, taps, in_ref, weight_ref, taps_ref, proj_ref, starts_ref, low_ref, act_ref, wide,
):
    count = in_ref.shape[0]
    tokens = in_ref.shape[2]
    channels = act_ref.shape[0]
    width = count * features
    sums = jnp.zeros((16, tokens), F32)
    for peer in range(count):
        base = peer * features
        wide[base : base + features, 0:tokens] = in_ref[peer, 0:features, :]
        packed = in_ref[peer, features : features + 16, :].astype(F32)
        sums = sums + in_ref[peer, features + 16 : features + 32, :].astype(F32)
        for part in range(features // 16):
            shift = (tokens - 8 - 8 * part) % tokens
            moved = packed if shift == 0 else pltpu.roll(packed, shift, 1)
            wide[base + 16 * part : base + 16 * part + 16, tokens:] = moved.astype(BF16)
    scale_main = lax.rsqrt((sums[0:1] + sums[1:2]) / width + EPSILON)
    scale_tail = lax.rsqrt((sums[2:3] + sums[3:4]) / width + EPSILON)
    both = dot(weight_ref[...], wide[...])
    x_in = (both[:, :tokens] * scale_main).astype(BF16).astype(F32)
    tail = (both[:, tokens:] * scale_tail).astype(BF16).astype(F32)
    fresh = 1.0 - jnp.broadcast_to(starts_ref[...].astype(F32), (8, tokens))
    lane8 = iota((8, tokens), 1)
    lane = iota((channels, tokens), 1)
    convolved = taps_ref[:, taps : taps + 1] + taps_ref[:, taps - 1 : taps] * x_in
    mask = fresh
    for back in range(1, taps):
        if back > 1:
            mask = mask * jnp.where(lane8 < back - 1, 1.0, pltpu.roll(fresh, back - 1, 1))
        behind = pltpu.roll(jnp.where(lane >= tokens - back, tail, x_in), back, 1)
        tap = taps_ref[:, taps - 1 - back : taps - back]
        convolved = convolved + jnp.where(mask[:1] > 0.5, tap * behind, 0.0)
    act = (convolved * (1.0 / (1.0 + jnp.exp(-convolved)))).astype(BF16)
    act_ref[...] = act
    low_ref[...] = dot(proj_ref[...], act).astype(BF16)


def state_body(
    rank, in_ref, act_ref, dtw_ref, rate_ref, rows_ref, starts_ref,
    send_ref, decay_step, drive_step, maps_ref,
):
    tokens = in_ref.shape[2]
    states, channels = rate_ref.shape
    low = in_ref[0].astype(F32)
    for peer in range(1, in_ref.shape[0]):
        low = low + in_ref[peer].astype(F32)
    dt_low = low[:rank].astype(BF16)
    in_map = low[rank : rank + states]
    maps_ref[...] = low[rank:]
    raw = dot(dt_low, dtw_ref[...], TN) + rows_ref[0:1, :]
    step = jnp.maximum(raw, 0.0) + jnp.log1p(jnp.exp(-jnp.abs(raw)))
    drive_step[...] = step * jnp.transpose(act_ref[...].astype(F32))
    first = jnp.transpose(jnp.broadcast_to(starts_ref[...].astype(F32), (tokens, tokens)))
    step = jnp.where(first[:, :1] > 0.5, FAR, step)
    decay_step[...] = step
    last = jnp.sum(step, axis=0, keepdims=True)
    rate = rate_ref[...] * (-LOG2E)
    state = jnp.zeros((states, channels), F32)
    for t in range(tokens):
        decay = jnp.exp2(decay_step[t : t + 1, :] * rate)
        state = decay * state + drive_step[t : t + 1, :] * in_map[:, t : t + 1]
    spare = send_ref.shape[2] - channels
    parts = channels // spare
    last_high = last.astype(BF16).astype(F32)
    line = iota((states, spare), 0)
    ends = jnp.zeros((states, spare), F32)
    for part in range(parts):
        high_part = last_high[:, part * spare : part * spare + spare]
        rest_part = last[:, part * spare : part * spare + spare] - high_part
        ends = jnp.where(line == part, high_part, ends)
        ends = jnp.where(line == part + parts, rest_part, ends)
    final = jnp.concatenate([state, ends], axis=1).astype(BF16)
    for peer in range(send_ref.shape[0]):
        send_ref[peer] = final


def side_body(
    features, in_ref, weight_hbm, act_ref, rate_ref, rows_ref, decay_step, drive_step, maps_ref,
    out_ref, share_ref, wide, gate_weight, hidden, gate_token, sem,
):
    count = in_ref.shape[0]
    tokens = in_ref.shape[2]
    states, channels = rate_ref.shape
    fetch = pltpu.make_async_copy(weight_hbm.at[channels:], gate_weight, sem)
    fetch.start()
    sums = jnp.zeros((16, tokens), F32)
    for peer in range(count):
        wide[peer * features : (peer + 1) * features, :] = in_ref[peer, 0:features, :]
        sums = sums + in_ref[peer, features + 16 : features + 32, :].astype(F32)
    scale = lax.rsqrt((sums[0:1] + sums[1:2]) / (count * features) + EPSILON)
    in_map = maps_ref[0:states, :]
    out_map = maps_ref[states:, :]
    step = decay_step[...]
    high = step.astype(BF16)
    rest = (step - high.astype(F32)).astype(BF16)
    lower = jnp.where(iota((tokens, tokens), 0) >= iota((tokens, tokens), 1), 1.0, 0.0).astype(BF16)
    elapsed = dot(lower, high) + dot(lower, rest)
    spread = jnp.where((iota((states, tokens), 1) & (states - 1)) == iota((states, tokens), 0), 1.0, 0.0)
    maps = dot(out_map.astype(BF16), spread.astype(BF16), TN)
    own = (iota((tokens, tokens), 1) // states) == (iota((tokens, tokens), 0) & 7)
    maps = jnp.where(own, maps, 0.0).astype(BF16)
    out_ref[...] = rows_ref[1:2, :] * jnp.transpose(act_ref[...].astype(F32))
    fetch.wait()
    gate = dot(gate_weight[...], wide[...])
    gate = (gate * scale).astype(BF16).astype(F32)
    gate_token[...] = jnp.transpose(gate * (1.0 / (1.0 + jnp.exp(-gate))))
    rate = rate_ref[...] * (-LOG2E)
    by_token = jnp.transpose(out_map)
    for index in range(states):
        remains = jnp.exp2(elapsed * rate[index : index + 1, :]) * gate_token[...]
        share_ref[index] = (by_token[:, index : index + 1] * remains).astype(BF16)
    state = jnp.zeros((states, channels), F32)
    for block in range(tokens // 8):
        for inner in range(8):
            t = block * 8 + inner
            decay = jnp.exp2(decay_step[t : t + 1, :] * rate)
            state = decay * state + drive_step[t : t + 1, :] * in_map[:, t : t + 1]
            hidden[inner * states : (inner + 1) * states, :] = state.astype(BF16)
        out_ref[block * 8 : block * 8 + 8, :] += dot(maps[block * 8 : block * 8 + 8], hidden[...])
    out_ref[...] *= gate_token[...]


def finish_body(me, in_ref, rate_ref, out_in_ref, share_ref, mixed_ref):
    states, channels = rate_ref.shape
    rate = rate_ref[...] * (-LOG2E)
    state = jnp.zeros((states, channels), F32)
    parts = channels // (in_ref.shape[2] - channels)
    for peer in range(in_ref.shape[0]):
        message = in_ref[peer].astype(F32)
        ends = message[:parts, channels:] + message[parts : 2 * parts, channels:]
        length = jnp.concatenate([ends[part : part + 1] for part in range(parts)], axis=1)
        before = peer < me[0]
        through = jnp.where(before, jnp.exp2(length * rate), 1.0)
        final = jnp.where(before, message[:, :channels], 0.0)
        state = through * state + final
    scanned = out_in_ref[...]
    for index in range(states):
        scanned = scanned + share_ref[index].astype(F32) * state[index : index + 1, :]
    mixed_ref[...] = jnp.transpose(scanned).astype(BF16)


def local(
    tokens, norm_gain, in_weight, conv_weight, conv_bias, proj_weight, dt_weight, dt_bias,
    decay_rate, skip_gain, doc_starts, group_target,
):
    peers = lax.axis_size("dp")
    row_count, features = tokens.shape
    slots = group_target.shape[0]
    width = in_weight.shape[0]
    channels = in_weight.shape[2]
    rank = dt_weight.shape[0]
    states = decay_rate.shape[1]
    shape = jax.ShapeDtypeStruct
    me = lax.axis_index("dp").astype(jnp.int32).reshape(1)
    starts = doc_starts.reshape(1, row_count)
    my_gain = lax.dynamic_slice_in_dim(norm_gain, lax.axis_index("chan") * features, features)
    my_gain = jnp.broadcast_to(my_gain[:, None], (features, row_count))
    weight = jnp.transpose(in_weight, (1, 2, 0)).reshape(2 * channels, width)
    pieces, starts = call(
        functools.partial(pack_body, slots),
        (shape((peers, 16, row_count), BF16), shape((1, row_count), jnp.int32)),
        [SMEM, HBM, HBM, HBM],
        (me, in_hbm(group_target), in_hbm(tokens.T), in_hbm(starts)),
        [
            pltpu.SMEM((slots,), jnp.int32),
            pltpu.VMEM((features, row_count), BF16),
            pltpu.VMEM((peers, 16, row_count), F32),
            pltpu.SemaphoreType.DMA((3,)),
        ],
    )
    weight = in_hbm(weight)
    sources = (proj_weight.T, dt_weight, decay_rate.T, conv_weight, conv_bias, dt_bias, skip_gain)
    scan_weight, proj, dtw, rate, cols, rows = call(
        fetch_body,
        (
            shape((channels, width), BF16),
            shape((rank + 2 * states, channels), BF16),
            shape((rank, channels), BF16),
            shape((states, channels), F32),
            shape((channels, 8), F32),
            shape((8, channels), F32),
        ),
        [HBM] * 8,
        (weight, *(in_hbm(source) for source in sources)),
        [
            pltpu.VMEM(conv_weight.shape, F32),
            pltpu.VMEM((channels,), F32),
            pltpu.VMEM((channels,), F32),
            pltpu.VMEM((channels,), F32),
            pltpu.SemaphoreType.DMA((8,)),
        ],
    )
    arrived = lax.all_to_all(pieces, "dp", 0, 0, tiled=True)
    payload = call(
        place_body,
        shape((features + 32, row_count), BF16),
        [VMEM, VMEM],
        (arrived, my_gain),
    )
    gathered = lax.all_gather(payload, "chan", axis=0)
    low, act = call(
        functools.partial(project_body, features, conv_weight.shape[0]),
        (shape((rank + 2 * states, row_count), BF16), shape((channels, row_count), BF16)),
        [VMEM] * 5,
        (gathered, scan_weight, cols, proj, starts),
        [pltpu.VMEM((width, 2 * row_count), BF16)],
    )
    lows = lax.all_gather(low, "chan", axis=0)
    by_token = shape((row_count, channels), F32)
    send, decay_step, drive_step, maps = call(
        functools.partial(state_body, rank),
        (
            shape((peers, states, -(-channels // 128) * 128), BF16),
            by_token,
            by_token,
            shape((2 * states, row_count), F32),
        ),
        [VMEM] * 6,
        (lows, act, dtw, rate, rows, starts),
    )
    out, share = call(
        functools.partial(side_body, features),
        (by_token, shape((states, row_count, channels), BF16)),
        [VMEM, HBM] + [VMEM] * 6,
        (gathered, weight, act, rate, rows, decay_step, drive_step, maps),
        [
            pltpu.VMEM((width, row_count), BF16),
            pltpu.VMEM((channels, width), BF16),
            pltpu.VMEM((8 * states, channels), BF16),
            pltpu.VMEM((row_count, channels), F32),
            pltpu.SemaphoreType.DMA,
        ],
    )
    ends = lax.all_to_all(send, "dp", 0, 0, tiled=True)
    mixed = call(
        finish_body,
        shape((channels, row_count), BF16),
        [SMEM] + [VMEM] * 4,
        (me, ends, rate, out, share),
    )
    return mixed.T


def solution(mesh):
    return jax.shard_map(
        local,
        mesh=mesh,
        in_specs=(
            P("dp", "chan"),
            P(),
            P(None, None, "chan"),
            P(None, "chan"),
            P("chan"),
            P("chan", None),
            P(None, "chan"),
            P("chan"),
            P("chan", None),
            P("chan"),
            P("dp"),
            P("dp"),
        ),
        out_specs=P("dp", "chan"),
        check_vma=False,
    )
```

```python
import functools
import math

import jax
import jax.numpy as jnp
from jax import lax
from jax.experimental import pallas as pl
from jax.experimental.pallas import tpu as pltpu
from jax.sharding import PartitionSpec as P

EPSILON = 1e-05
LOG2E = math.log2(math.e)
FAR = 1e30
F32 = jnp.float32
BF16 = jnp.bfloat16

VMEM = pl.BlockSpec(memory_space=pltpu.VMEM)
SMEM = pl.BlockSpec(memory_space=pltpu.SMEM)
HBM = pl.BlockSpec(memory_space=pltpu.HBM)

NN = (((1,), (0,)), ((), ()))
NT = (((1,), (1,)), ((), ()))
TN = (((0,), (0,)), ((), ()))


def dot(a, b, dims=NN):
    return lax.dot_general(a, b, dims, preferred_element_type=F32)


def in_hbm(value):
    return pltpu.with_memory_space_constraint(value, pltpu.HBM)


def iota(shape, dim):
    return lax.broadcasted_iota(jnp.int32, shape, dim)


def call(body, outs, specs, args, scratch=(), limit=24):
    return pl.pallas_call(
        body,
        out_shape=outs,
        in_specs=specs,
        out_specs=jax.tree.map(lambda _: VMEM, outs),
        scratch_shapes=list(scratch),
        compiler_params=pltpu.CompilerParams(vmem_limit_bytes=limit << 20),
    )(*args)


def pack_body(slots, me, target_hbm, tok_hbm, starts_hbm, out_ref, starts_ref, target, tok_ref, pieces, sems):
    copies = [
        pltpu.make_async_copy(target_hbm, target, sems.at[0]),
        pltpu.make_async_copy(starts_hbm, starts_ref, sems.at[1]),
        pltpu.make_async_copy(tok_hbm, tok_ref, sems.at[2]),
    ]
    for copy in copies:
        copy.start()
    features, tokens = tok_ref.shape
    peers = pieces.shape[0]
    parts = features // 16
    pieces[...] = jnp.zeros(pieces.shape, F32)
    lane = iota((16, tokens), 1)
    source = iota((tokens, tokens), 0)
    place = iota((tokens, tokens), 1)
    late = (source < features // 2) & ((source & 7) >= 5)
    to_tail = jnp.where(
        late & (place == features // 2 + 3 * (source >> 3) + (source & 7) - 5), 1.0, 0.0
    ).astype(BF16)
    copies[2].wait()
    slabs = [tok_ref[16 * part : 16 * part + 16, :].astype(F32) for part in range(parts)]
    groups = []
    for group in range(slots):
        piece = jnp.zeros((16, tokens), F32)
        for part in range(parts):
            shift = (8 * (part - group)) % tokens
            moved = slabs[part] if shift == 0 else pltpu.roll(slabs[part], shift, 1)
            piece = jnp.where((lane >> 3) == part, moved, piece)
        groups.append(piece)
    tails = dot(jnp.concatenate(groups, axis=0).astype(BF16), to_tail)
    copies[0].wait()
    copies[1].wait()
    fresh = 1.0 - jnp.broadcast_to(starts_ref[...].astype(F32), (16, tokens))
    one = pltpu.roll(fresh, (114 - (tokens - 1)) % tokens, 1)
    two = pltpu.roll(fresh, (113 - (tokens - 1)) % tokens, 1)
    flags = jnp.where(
        lane == 115, 1.0, jnp.where(lane == 114, one, jnp.where(lane == 113, one * two, 0.0))
    )
    after = me[0] + 1
    pieces[jnp.minimum(after, peers - 1)] += jnp.where(after < peers, flags, 0.0)
    for group in range(slots):
        dev = target[group] // slots
        slot = target[group] % slots
        label = jnp.where(lane == 112, (slot + 1).astype(F32), 0.0)
        pieces[dev] += groups[group] + label
        follows = (slot == slots - 1) & (dev + 1 < peers)
        tail = jnp.where(follows, tails[16 * group : 16 * group + 16], 0.0)
        pieces[jnp.minimum(dev + 1, peers - 1)] += tail
    out_ref[...] = pieces[...].astype(BF16)


def fetch_body(
    weight_hbm, proj_hbm, dtw_hbm, rate_hbm, taps_hbm, conv_bias_hbm, dt_bias_hbm, skip_hbm,
    weight_ref, proj_ref, dtw_ref, rate_ref, cols_ref, rows_ref,
    taps_in, conv_bias, dt_bias, skip, sems,
):
    taps, channels = taps_in.shape
    pairs = (
        (taps_hbm, taps_in),
        (conv_bias_hbm, conv_bias),
        (dt_bias_hbm, dt_bias),
        (skip_hbm, skip),
        (weight_hbm.at[0:channels], weight_ref),
        (proj_hbm, proj_ref),
        (dtw_hbm, dtw_ref),
        (rate_hbm, rate_ref),
    )
    copies = [
        pltpu.make_async_copy(source, target, sems.at[index])
        for index, (source, target) in enumerate(pairs)
    ]
    for copy in copies:
        copy.start()
    for copy in copies[:4]:
        copy.wait()
    bias = conv_bias[...].reshape(1, channels)
    blank = jnp.zeros((8 - taps - 1, channels), F32)
    cols_ref[...] = jnp.transpose(jnp.concatenate([taps_in[...], bias, blank], axis=0))
    rows_ref[0:1, :] = dt_bias[...].reshape(1, channels)
    rows_ref[1:2, :] = skip[...].reshape(1, channels)
    for copy in copies[4:]:
        copy.wait()


def place_body(in_ref, gain_ref, out_ref):
    peers, _, tokens = in_ref.shape
    features = gain_ref.shape[0]
    rows = 16 * peers
    slots = tokens // 8
    parts = features // 16
    arrived = in_ref[...].reshape(rows, tokens)
    wide = arrived.astype(F32)
    label = jnp.broadcast_to(wide[:, 112:113], (rows, 16 * slots))
    key = (iota((rows, 16 * slots), 1) + 16 - (iota((rows, 16 * slots), 0) & 15)).astype(F32)
    pick = jnp.where(label * 16.0 == key, 1.0, 0.0).astype(BF16)
    ordered = dot(pick, arrived, TN)
    total = jnp.sum(wide.reshape(peers, 16, tokens), axis=0)
    lane = iota((16, tokens), 1)
    open_tail = jnp.where(lane >= tokens - 3, pltpu.roll(total, tokens - 3 - 113, 1), 0.0)
    mains, tails = [], []
    for part in range(parts):
        slab = jnp.zeros((16, tokens), F32)
        for slot in range(slots):
            shift = (8 * (slot - part)) % tokens
            piece = ordered[16 * slot : 16 * slot + 16]
            moved = piece if shift == 0 else pltpu.roll(piece, shift, 1)
            slab = jnp.where((lane >> 3) == slot, moved, slab)
        mains.append(slab)
        shift = (tokens - 3 - features // 2 - 3 * part) % tokens
        tails.append((total if shift == 0 else pltpu.roll(total, shift, 1)) * open_tail)
    x_main = jnp.concatenate(mains, axis=0)
    x_tail = jnp.concatenate(tails, axis=0)
    gain = gain_ref[...]
    main_sq = jnp.sum(x_main * x_main, axis=0, keepdims=True)
    tail_sq = jnp.sum(x_tail * x_tail, axis=0, keepdims=True)
    out_ref[0:features, :] = (x_main * gain).astype(BF16)
    x_tail = x_tail * gain
    packed = jnp.zeros((16, tokens), F32)
    for part in range(features // 16):
        shift = (8 * part - (tokens - 8)) % tokens
        packed = packed + pltpu.roll(x_tail[16 * part : 16 * part + 16], shift, 1)
    out_ref[features : features + 16, :] = packed.astype(BF16)
    main_high = main_sq.astype(BF16).astype(F32)
    tail_high = tail_sq.astype(BF16).astype(F32)
    line = iota((16, tokens), 0)
    sums = jnp.where(
        line == 0,
        main_high,
        jnp.where(
            line == 1,
            main_sq - main_high,
            jnp.where(line == 2, tail_high, jnp.where(line == 3, tail_sq - tail_high, 0.0)),
        ),
    )
    out_ref[features + 16 : features + 32, :] = sums.astype(BF16)


def project_body(
    features, taps, in_ref, weight_ref, taps_ref, proj_ref, starts_ref, low_ref, act_ref, wide,
):
    count = in_ref.shape[0]
    tokens = in_ref.shape[2]
    channels = act_ref.shape[0]
    width = count * features
    sums = jnp.zeros((16, tokens), F32)
    for peer in range(count):
        base = peer * features
        wide[base : base + features, 0:tokens] = in_ref[peer, 0:features, :]
        packed = in_ref[peer, features : features + 16, :].astype(F32)
        sums = sums + in_ref[peer, features + 16 : features + 32, :].astype(F32)
        for part in range(features // 16):
            shift = (tokens - 8 - 8 * part) % tokens
            moved = packed if shift == 0 else pltpu.roll(packed, shift, 1)
            wide[base + 16 * part : base + 16 * part + 16, tokens:] = moved.astype(BF16)
    scale_main = lax.rsqrt((sums[0:1] + sums[1:2]) / width + EPSILON)
    scale_tail = lax.rsqrt((sums[2:3] + sums[3:4]) / width + EPSILON)
    both = dot(weight_ref[...], wide[...])
    x_in = (both[:, :tokens] * scale_main).astype(BF16).astype(F32)
    tail = (both[:, tokens:] * scale_tail).astype(BF16).astype(F32)
    fresh = 1.0 - jnp.broadcast_to(starts_ref[...].astype(F32), (8, tokens))
    lane8 = iota((8, tokens), 1)
    lane = iota((channels, tokens), 1)
    convolved = taps_ref[:, taps : taps + 1] + taps_ref[:, taps - 1 : taps] * x_in
    mask = fresh
    for back in range(1, taps):
        if back > 1:
            mask = mask * jnp.where(lane8 < back - 1, 1.0, pltpu.roll(fresh, back - 1, 1))
        behind = pltpu.roll(jnp.where(lane >= tokens - back, tail, x_in), back, 1)
        tap = taps_ref[:, taps - 1 - back : taps - back]
        convolved = convolved + jnp.where(mask[:1] > 0.5, tap * behind, 0.0)
    act = (convolved * (1.0 / (1.0 + jnp.exp(-convolved)))).astype(BF16)
    act_ref[...] = act
    low_ref[...] = dot(proj_ref[...], act).astype(BF16)


def join(state, length, lanes):
    states, channels = state.shape
    spare = lanes - channels
    pieces = channels // spare
    length_high = length.astype(BF16).astype(F32)
    line = iota((states, spare), 0)
    ends = jnp.zeros((states, spare), F32)
    for piece in range(pieces):
        high = length_high[:, piece * spare : piece * spare + spare]
        rest = length[:, piece * spare : piece * spare + spare] - high
        ends = jnp.where(line == piece, high, ends)
        ends = jnp.where(line == piece + pieces, rest, ends)
    return jnp.concatenate([state, ends], axis=1).astype(BF16)


def part(message, channels):
    message = message.astype(F32)
    pieces = channels // (message.shape[1] - channels)
    ends = message[:pieces, channels:] + message[pieces : 2 * pieces, channels:]
    length = jnp.concatenate([ends[piece : piece + 1] for piece in range(pieces)], axis=1)
    return message[:, :channels], length


def state_body(
    rank, in_ref, act_ref, dtw_ref, rate_ref, rows_ref, starts_ref,
    send_ref, decay_step, drive_step, maps_ref,
):
    tokens = in_ref.shape[2]
    states, channels = rate_ref.shape
    low = in_ref[0].astype(F32)
    for peer in range(1, in_ref.shape[0]):
        low = low + in_ref[peer].astype(F32)
    dt_low = low[:rank].astype(BF16)
    in_map = low[rank : rank + states]
    maps_ref[...] = low[rank:]
    raw = dot(dt_low, dtw_ref[...], TN) + rows_ref[0:1, :]
    step = jnp.maximum(raw, 0.0) + jnp.log1p(jnp.exp(-jnp.abs(raw)))
    drive_step[...] = step * jnp.transpose(act_ref[...].astype(F32))
    first = jnp.transpose(jnp.broadcast_to(starts_ref[...].astype(F32), (tokens, tokens)))
    step = jnp.where(first[:, :1] > 0.5, FAR, step)
    decay_step[...] = step
    last = jnp.sum(step, axis=0, keepdims=True)
    rate = rate_ref[...] * (-LOG2E)
    state = jnp.zeros((states, channels), F32)
    for t in range(tokens):
        decay = jnp.exp2(decay_step[t : t + 1, :] * rate)
        state = decay * state + drive_step[t : t + 1, :] * in_map[:, t : t + 1]
    message = join(state, last, send_ref.shape[2])
    for peer in range(send_ref.shape[0]):
        send_ref[peer] = message


def row_body(me, in_ref, rate_ref, send_ref, before_ref, length_ref):
    states, channels = rate_ref.shape
    rate = rate_ref[...] * (-LOG2E)
    whole = jnp.zeros((states, channels), F32)
    before = whole
    whole_length = jnp.zeros((1, channels), F32)
    before_length = whole_length
    for peer in range(in_ref.shape[0]):
        final, length = part(in_ref[peer], channels)
        earlier = peer < me[0]
        through = jnp.exp2(length * rate)
        whole = through * whole + final
        before = jnp.where(earlier, whole, before)
        whole_length = whole_length + length
        before_length = jnp.where(earlier, whole_length, before_length)
    message = join(whole, whole_length, send_ref.shape[2])
    for peer in range(send_ref.shape[0]):
        send_ref[peer] = message
    before_ref[...] = before
    length_ref[...] = jnp.broadcast_to(before_length, length_ref.shape)


def side_body(
    features, in_ref, weight_hbm, act_ref, rate_ref, rows_ref, decay_step, drive_step, maps_ref, row_ref,
    out_ref, share_ref, wide, gate_weight, hidden, gate_token, sem,
):
    count = in_ref.shape[0]
    tokens = in_ref.shape[2]
    states, channels = rate_ref.shape
    fetch = pltpu.make_async_copy(weight_hbm.at[channels:], gate_weight, sem)
    fetch.start()
    sums = jnp.zeros((16, tokens), F32)
    for peer in range(count):
        wide[peer * features : (peer + 1) * features, :] = in_ref[peer, 0:features, :]
        sums = sums + in_ref[peer, features + 16 : features + 32, :].astype(F32)
    scale = lax.rsqrt((sums[0:1] + sums[1:2]) / (count * features) + EPSILON)
    in_map = maps_ref[0:states, :]
    out_map = maps_ref[states:, :]
    step = decay_step[...]
    high = step.astype(BF16)
    rest = (step - high.astype(F32)).astype(BF16)
    lower = jnp.where(iota((tokens, tokens), 0) >= iota((tokens, tokens), 1), 1.0, 0.0).astype(BF16)
    elapsed = dot(lower, high) + dot(lower, rest)
    spread = jnp.where((iota((states, tokens), 1) & (states - 1)) == iota((states, tokens), 0), 1.0, 0.0)
    maps = dot(out_map.astype(BF16), spread.astype(BF16), TN)
    own = (iota((tokens, tokens), 1) // states) == (iota((tokens, tokens), 0) & 7)
    maps = jnp.where(own, maps, 0.0).astype(BF16)
    out_ref[...] = rows_ref[1:2, :] * jnp.transpose(act_ref[...].astype(F32))
    fetch.wait()
    gate = dot(gate_weight[...], wide[...])
    gate = (gate * scale).astype(BF16).astype(F32)
    gate_token[...] = jnp.transpose(gate * (1.0 / (1.0 + jnp.exp(-gate))))
    rate = rate_ref[...] * (-LOG2E)
    by_token = jnp.transpose(out_map)
    for index in range(states):
        remains = jnp.exp2(elapsed * rate[index : index + 1, :]) * gate_token[...]
        share_ref[index] = (by_token[:, index : index + 1] * remains).astype(BF16)
    state = jnp.zeros((states, channels), F32)
    for block in range(tokens // 8):
        for inner in range(8):
            t = block * 8 + inner
            decay = jnp.exp2(decay_step[t : t + 1, :] * rate)
            state = decay * state + drive_step[t : t + 1, :] * in_map[:, t : t + 1]
            hidden[inner * states : (inner + 1) * states, :] = state.astype(BF16)
        out_ref[block * 8 : block * 8 + 8, :] += dot(maps[block * 8 : block * 8 + 8], hidden[...])
    out_ref[...] *= gate_token[...]


def finish_body(me, in_ref, rate_ref, before_ref, length_ref, out_in_ref, share_ref, mixed_ref):
    states, channels = rate_ref.shape
    rate = rate_ref[...] * (-LOG2E)
    state = jnp.zeros((states, channels), F32)
    for peer in range(in_ref.shape[0]):
        final, length = part(in_ref[peer], channels)
        earlier = peer < me[0]
        through = jnp.where(earlier, jnp.exp2(length * rate), 1.0)
        state = through * state + jnp.where(earlier, final, 0.0)
    state = jnp.exp2(length_ref[0:1, :] * rate) * state + before_ref[...]
    scanned = out_in_ref[...]
    for index in range(states):
        scanned = scanned + share_ref[index].astype(F32) * state[index : index + 1, :]
    mixed_ref[...] = jnp.transpose(scanned).astype(BF16)


def local(
    tokens, norm_gain, in_weight, conv_weight, conv_bias, proj_weight, dt_weight, dt_bias,
    decay_rate, skip_gain, doc_starts, group_target,
):
    rows_of, in_row = lax.axis_size("z"), lax.axis_size("x")
    peers = rows_of * in_row
    row_count, features = tokens.shape
    slots = group_target.shape[0]
    width = in_weight.shape[0]
    channels = in_weight.shape[2]
    rank = dt_weight.shape[0]
    states = decay_rate.shape[1]
    shape = jax.ShapeDtypeStruct
    me = lax.axis_index(("z", "x")).astype(jnp.int32).reshape(1)
    starts = doc_starts.reshape(1, row_count)
    my_gain = lax.dynamic_slice_in_dim(norm_gain, lax.axis_index("chan") * features, features)
    my_gain = jnp.broadcast_to(my_gain[:, None], (features, row_count))
    weight = jnp.transpose(in_weight, (1, 2, 0)).reshape(2 * channels, width)
    pieces, starts = call(
        functools.partial(pack_body, slots),
        (shape((peers, 16, row_count), BF16), shape((1, row_count), jnp.int32)),
        [SMEM, HBM, HBM, HBM],
        (me, in_hbm(group_target), in_hbm(tokens.T), in_hbm(starts)),
        [
            pltpu.SMEM((slots,), jnp.int32),
            pltpu.VMEM((features, row_count), BF16),
            pltpu.VMEM((peers, 16, row_count), F32),
            pltpu.SemaphoreType.DMA((3,)),
        ],
    )
    weight = in_hbm(weight)
    sources = (proj_weight.T, dt_weight, decay_rate.T, conv_weight, conv_bias, dt_bias, skip_gain)
    scan_weight, proj, dtw, rate, cols, rows = call(
        fetch_body,
        (
            shape((channels, width), BF16),
            shape((rank + 2 * states, channels), BF16),
            shape((rank, channels), BF16),
            shape((states, channels), F32),
            shape((channels, 8), F32),
            shape((8, channels), F32),
        ),
        [HBM] * 8,
        (weight, *(in_hbm(source) for source in sources)),
        [
            pltpu.VMEM(conv_weight.shape, F32),
            pltpu.VMEM((channels,), F32),
            pltpu.VMEM((channels,), F32),
            pltpu.VMEM((channels,), F32),
            pltpu.SemaphoreType.DMA((8,)),
        ],
    )
    arrived = lax.all_to_all(pieces, ("z", "x"), 0, 0, tiled=True)
    payload = call(
        place_body,
        shape((features + 32, row_count), BF16),
        [VMEM, VMEM],
        (arrived, my_gain),
    )
    gathered = lax.all_gather(payload, "chan", axis=0)
    low, act = call(
        functools.partial(project_body, features, conv_weight.shape[0]),
        (shape((rank + 2 * states, row_count), BF16), shape((channels, row_count), BF16)),
        [VMEM] * 5,
        (gathered, scan_weight, cols, proj, starts),
        [pltpu.VMEM((width, 2 * row_count), BF16)],
    )
    lows = lax.all_gather(low, "chan", axis=0)
    lanes = -(-channels // 128) * 128
    by_token = shape((row_count, channels), F32)
    send, decay_step, drive_step, maps = call(
        functools.partial(state_body, rank),
        (
            shape((in_row, states, lanes), BF16),
            by_token,
            by_token,
            shape((2 * states, row_count), F32),
        ),
        [VMEM] * 6,
        (lows, act, dtw, rate, rows, starts),
    )
    in_row_ends = lax.all_to_all(send, "x", 0, 0, tiled=True)
    send, before, before_length = call(
        row_body,
        (
            shape((rows_of, states, lanes), BF16),
            shape((states, channels), F32),
            shape((8, channels), F32),
        ),
        [SMEM, VMEM, VMEM],
        (lax.axis_index("x").astype(jnp.int32).reshape(1), in_row_ends, rate),
    )
    out, share = call(
        functools.partial(side_body, features),
        (by_token, shape((states, row_count, channels), BF16)),
        [VMEM, HBM] + [VMEM] * 7,
        (gathered, weight, act, rate, rows, decay_step, drive_step, maps, before_length),
        [
            pltpu.VMEM((width, row_count), BF16),
            pltpu.VMEM((channels, width), BF16),
            pltpu.VMEM((8 * states, channels), BF16),
            pltpu.VMEM((row_count, channels), F32),
            pltpu.SemaphoreType.DMA,
        ],
    )
    ends = lax.all_to_all(send, "z", 0, 0, tiled=True)
    my_row = lax.axis_index("z").astype(jnp.int32).reshape(1)
    mixed = call(
        finish_body,
        shape((channels, row_count), BF16),
        [SMEM] + [VMEM] * 6,
        (my_row, ends, rate, before, before_length, out, share),
    )
    return mixed.T


def solution(mesh):
    peers, chans = mesh.devices.shape
    in_row = 4 if peers % 4 == 0 else 1
    grid = mesh.devices.reshape(peers // in_row, in_row, chans)
    mesh = jax.sharding.Mesh(grid, ("z", "x", "chan"))
    return jax.shard_map(
        local,
        mesh=mesh,
        in_specs=(
            P(("z", "x"), "chan"),
            P(),
            P(None, None, "chan"),
            P(None, "chan"),
            P("chan"),
            P("chan", None),
            P(None, "chan"),
            P("chan"),
            P("chan", None),
            P("chan"),
            P(("z", "x")),
            P(("z", "x")),
        ),
        out_specs=P(("z", "x"), "chan"),
        check_vma=False,
    )
```

```python
import functools
import math

import jax
import jax.numpy as jnp
from jax import lax
from jax.experimental import pallas as pl
from jax.experimental.pallas import tpu as pltpu
from jax.sharding import PartitionSpec as P

EPSILON = 1e-05
LOG2E = math.log2(math.e)
FAR = 1e30
F32 = jnp.float32
BF16 = jnp.bfloat16

VMEM = pl.BlockSpec(memory_space=pltpu.VMEM)
SMEM = pl.BlockSpec(memory_space=pltpu.SMEM)
HBM = pl.BlockSpec(memory_space=pltpu.HBM)

NN = (((1,), (0,)), ((), ()))
NT = (((1,), (1,)), ((), ()))
TN = (((0,), (0,)), ((), ()))


def dot(a, b, dims=NN):
    return lax.dot_general(a, b, dims, preferred_element_type=F32)


def in_hbm(value):
    return pltpu.with_memory_space_constraint(value, pltpu.HBM)


def iota(shape, dim):
    return lax.broadcasted_iota(jnp.int32, shape, dim)


def call(body, outs, specs, args, scratch=(), limit=24):
    return pl.pallas_call(
        body,
        out_shape=outs,
        in_specs=specs,
        out_specs=jax.tree.map(lambda _: VMEM, outs),
        scratch_shapes=list(scratch),
        compiler_params=pltpu.CompilerParams(vmem_limit_bytes=limit << 20),
    )(*args)


def swap_blocks(slabs):
    lanes = 128
    block = iota((16, lanes), 1) >> 3
    slabs = list(slabs) + [None] * (16 - len(slabs))
    for step in (8, 4, 2, 1):
        keep = (block & step) == 0
        for low in range(16):
            if low & step:
                continue
            a, b = slabs[low], slabs[low | step]
            if a is None and b is None:
                continue
            zero = jnp.zeros((16, lanes), F32)
            up = zero if b is None else pltpu.roll(b, 8 * step, 1)
            down = zero if a is None else pltpu.roll(a, lanes - 8 * step, 1)
            slabs[low] = jnp.where(keep, zero if a is None else a, up)
            slabs[low | step] = jnp.where(keep, down, zero if b is None else b)
    return slabs


def pack_body(slots, me, target_hbm, tok_hbm, starts_hbm, out_ref, starts_ref, target, tok_ref, pieces, sems):
    copies = [
        pltpu.make_async_copy(target_hbm, target, sems.at[0]),
        pltpu.make_async_copy(starts_hbm, starts_ref, sems.at[1]),
        pltpu.make_async_copy(tok_hbm, tok_ref, sems.at[2]),
    ]
    for copy in copies:
        copy.start()
    features, tokens = tok_ref.shape
    peers = out_ref.shape[0]
    parts = features // 16
    pieces[...] = jnp.zeros(pieces.shape, F32)
    lane = iota((16, tokens), 1)
    source = iota((tokens, tokens), 0)
    place = iota((tokens, tokens), 1)
    late = (source < features // 2) & ((source & 7) >= 5)
    to_tail = jnp.where(
        late & (place == features // 2 + 3 * (source >> 3) + (source & 7) - 5), 1.0, 0.0
    ).astype(BF16)
    copies[2].wait()
    groups = swap_blocks(
        [tok_ref[16 * piece : 16 * piece + 16, :].astype(F32) for piece in range(parts)]
    )
    tails = dot(jnp.concatenate(groups, axis=0).astype(BF16), to_tail)
    copies[0].wait()
    copies[1].wait()
    fresh = 1.0 - jnp.broadcast_to(starts_ref[...].astype(F32), (16, tokens))
    one = pltpu.roll(fresh, (114 - (tokens - 1)) % tokens, 1)
    two = pltpu.roll(fresh, (113 - (tokens - 1)) % tokens, 1)
    flags = jnp.where(
        lane == 115, 1.0, jnp.where(lane == 114, one, jnp.where(lane == 113, one * two, 0.0))
    )
    for group in range(slots):
        where_to = target[group]
        dev = lax.shift_right_logical(where_to, slots.bit_length() - 1)
        slot = where_to & (slots - 1)
        pieces[dev] = jnp.where(lane == 112, (slot + 1).astype(F32), groups[group])
        follows = (slot == slots - 1) & (dev + 1 < peers)
        pieces[jnp.where(follows, peers + dev + 1, 2 * peers)] = tails[16 * group : 16 * group + 16]
    after = me[0] + 1
    for peer in range(peers):
        whole = pieces[peer] + pieces[peers + peer] + jnp.where(after == peer, flags, 0.0)
        out_ref[peer] = whole.astype(BF16)


def fetch_body(
    weight_hbm, proj_hbm, dtw_hbm, rate_hbm, taps_hbm, conv_bias_hbm, dt_bias_hbm, skip_hbm, starts_ref,
    weight_ref, proj_ref, dtw_ref, rate_ref, cols_ref, rows_ref, first_ref,
    taps_in, conv_bias, dt_bias, skip, sems,
):
    taps, channels = taps_in.shape
    pairs = (
        (taps_hbm, taps_in),
        (conv_bias_hbm, conv_bias),
        (dt_bias_hbm, dt_bias),
        (skip_hbm, skip),
        (weight_hbm.at[0:channels], weight_ref),
        (proj_hbm, proj_ref),
        (dtw_hbm, dtw_ref),
        (rate_hbm, rate_ref),
    )
    copies = [
        pltpu.make_async_copy(source, target, sems.at[index])
        for index, (source, target) in enumerate(pairs)
    ]
    for copy in copies:
        copy.start()
    for copy in copies[:4]:
        copy.wait()
    bias = conv_bias[...].reshape(1, channels)
    blank = jnp.zeros((8 - taps - 1, channels), F32)
    cols_ref[...] = jnp.transpose(jnp.concatenate([taps_in[...], bias, blank], axis=0))
    tokens = starts_ref.shape[1]
    first = jnp.transpose(jnp.broadcast_to(starts_ref[...].astype(F32), (tokens, tokens)))
    first_ref[...] = jnp.broadcast_to(first[:, :1], first_ref.shape)
    rows_ref[0:1, :] = dt_bias[...].reshape(1, channels)
    rows_ref[1:2, :] = skip[...].reshape(1, channels)
    for copy in copies[4:]:
        copy.wait()


def place_body(in_ref, gain_ref, out_ref):
    peers, _, tokens = in_ref.shape
    features = gain_ref.shape[0]
    rows = 16 * peers
    slots = tokens // 8
    parts = features // 16
    arrived = in_ref[...].reshape(rows, tokens)
    spot = jnp.where(iota((16, tokens), 1) == 112, 1.0, 0.0).astype(BF16)
    label = dot(spot, arrived, NT)[:1]
    key = label * 16.0 + (iota((1, rows), 1) & 15).astype(F32)
    want = (iota((16 * slots, rows), 0) + 16).astype(F32)
    pick = jnp.where(key == want, 1.0, 0.0).astype(BF16)
    ordered = dot(pick, arrived)
    total = jnp.sum(in_ref[...].astype(F32), axis=0)
    lane = iota((16, tokens), 1)
    open_tail = jnp.where(lane >= tokens - 3, pltpu.roll(total, tokens - 3 - 113, 1), 0.0)
    mains = swap_blocks([ordered[16 * slot : 16 * slot + 16] for slot in range(slots)])[:parts]
    tails = []
    for piece in range(parts):
        shift = (tokens - 3 - features // 2 - 3 * piece) % tokens
        tails.append((total if shift == 0 else pltpu.roll(total, shift, 1)) * open_tail)
    x_main = jnp.concatenate(mains, axis=0)
    x_tail = jnp.concatenate(tails, axis=0)
    gain = gain_ref[...]
    main_sq = jnp.sum(x_main * x_main, axis=0, keepdims=True)
    tail_sq = jnp.sum(x_tail * x_tail, axis=0, keepdims=True)
    out_ref[0:features, :] = (x_main * gain).astype(BF16)
    x_tail = x_tail * gain
    packed = jnp.zeros((16, tokens), F32)
    for part in range(features // 16):
        shift = (8 * part - (tokens - 8)) % tokens
        packed = packed + pltpu.roll(x_tail[16 * part : 16 * part + 16], shift, 1)
    out_ref[features : features + 16, :] = packed.astype(BF16)
    main_high = main_sq.astype(BF16).astype(F32)
    tail_high = tail_sq.astype(BF16).astype(F32)
    line = iota((16, tokens), 0)
    sums = jnp.where(
        line == 0,
        main_high,
        jnp.where(
            line == 1,
            main_sq - main_high,
            jnp.where(line == 2, tail_high, jnp.where(line == 3, tail_sq - tail_high, 0.0)),
        ),
    )
    out_ref[features + 16 : features + 32, :] = sums.astype(BF16)


def project_body(
    features, taps, in_ref, weight_ref, taps_ref, proj_ref, starts_ref, low_ref, act_ref, wide,
):
    count = in_ref.shape[0]
    tokens = in_ref.shape[2]
    channels = act_ref.shape[0]
    width = count * features
    sums = jnp.zeros((16, tokens), F32)
    for peer in range(count):
        base = peer * features
        wide[base : base + features, 0:tokens] = in_ref[peer, 0:features, :]
        packed = in_ref[peer, features : features + 16, :].astype(F32)
        sums = sums + in_ref[peer, features + 16 : features + 32, :].astype(F32)
        for part in range(features // 16):
            shift = (tokens - 8 - 8 * part) % tokens
            moved = packed if shift == 0 else pltpu.roll(packed, shift, 1)
            wide[base + 16 * part : base + 16 * part + 16, tokens:] = moved.astype(BF16)
    scale_main = lax.rsqrt((sums[0:1] + sums[1:2]) / width + EPSILON)
    scale_tail = lax.rsqrt((sums[2:3] + sums[3:4]) / width + EPSILON)
    both = dot(weight_ref[...], wide[...])
    x_in = (both[:, :tokens] * scale_main).astype(BF16).astype(F32)
    tail = (both[:, tokens:] * scale_tail).astype(BF16).astype(F32)
    fresh = 1.0 - jnp.broadcast_to(starts_ref[...].astype(F32), (8, tokens))
    lane8 = iota((8, tokens), 1)
    lane = iota((channels, tokens), 1)
    convolved = taps_ref[:, taps : taps + 1] + taps_ref[:, taps - 1 : taps] * x_in
    mask = fresh
    for back in range(1, taps):
        if back > 1:
            mask = mask * jnp.where(lane8 < back - 1, 1.0, pltpu.roll(fresh, back - 1, 1))
        behind = pltpu.roll(jnp.where(lane >= tokens - back, tail, x_in), back, 1)
        tap = taps_ref[:, taps - 1 - back : taps - back]
        convolved = convolved + jnp.where(mask[:1] > 0.5, tap * behind, 0.0)
    act = (convolved * (1.0 / (1.0 + jnp.exp(-convolved)))).astype(BF16)
    act_ref[...] = act
    low_ref[...] = dot(proj_ref[...], act).astype(BF16)


def join(state, length, lanes):
    states, channels = state.shape
    spare = lanes - channels
    pieces = channels // spare
    length_high = length.astype(BF16).astype(F32)
    line = iota((states, spare), 0)
    ends = jnp.zeros((states, spare), F32)
    for piece in range(pieces):
        high = length_high[:, piece * spare : piece * spare + spare]
        rest = length[:, piece * spare : piece * spare + spare] - high
        ends = jnp.where(line == piece, high, ends)
        ends = jnp.where(line == piece + pieces, rest, ends)
    return jnp.concatenate([state, ends], axis=1).astype(BF16)


def part(message, channels):
    message = message.astype(F32)
    pieces = channels // (message.shape[1] - channels)
    ends = message[:pieces, channels:] + message[pieces : 2 * pieces, channels:]
    length = jnp.concatenate([ends[piece : piece + 1] for piece in range(pieces)], axis=1)
    return message[:, :channels], length


def state_body(
    rank, in_ref, act_ref, dtw_ref, rate_ref, rows_ref, first_ref,
    send_ref, decay_step, drive_step, maps_ref,
):
    tokens = in_ref.shape[2]
    states, channels = rate_ref.shape
    low = in_ref[0].astype(F32)
    for peer in range(1, in_ref.shape[0]):
        low = low + in_ref[peer].astype(F32)
    dt_low = low[:rank].astype(BF16)
    in_map = low[rank : rank + states]
    maps_ref[...] = low[rank:]
    raw = dot(dt_low, dtw_ref[...], TN) + rows_ref[0:1, :]
    small = jnp.exp(-jnp.abs(raw))
    series = small * (1.0 - small * (0.5 - small * (1.0 / 3.0 - small * 0.25)))
    step = jnp.maximum(raw, 0.0) + jnp.where(small < 0.01, series, jnp.log(1.0 + small))
    drive_step[...] = step * jnp.transpose(act_ref[...].astype(F32))
    step = jnp.where(first_ref[...] > 0.5, FAR, step)
    decay_step[...] = step
    last = jnp.sum(step, axis=0, keepdims=True)
    rate = rate_ref[...] * (-LOG2E)
    state = jnp.zeros((states, channels), F32)
    for t in range(tokens):
        decay = jnp.exp2(decay_step[t : t + 1, :] * rate)
        state = decay * state + drive_step[t : t + 1, :] * in_map[:, t : t + 1]
    message = join(state, last, send_ref.shape[2])
    for peer in range(send_ref.shape[0]):
        send_ref[peer] = message


def row_body(me, in_ref, rate_ref, send_ref, before_ref, length_ref):
    states, channels = rate_ref.shape
    rate = rate_ref[...] * (-LOG2E)
    whole = jnp.zeros((states, channels), F32)
    before = whole
    whole_length = jnp.zeros((1, channels), F32)
    before_length = whole_length
    for peer in range(in_ref.shape[0]):
        final, length = part(in_ref[peer], channels)
        earlier = peer < me[0]
        through = jnp.exp2(length * rate)
        whole = through * whole + final
        before = jnp.where(earlier, whole, before)
        whole_length = whole_length + length
        before_length = jnp.where(earlier, whole_length, before_length)
    message = join(whole, whole_length, send_ref.shape[2])
    for peer in range(send_ref.shape[0]):
        send_ref[peer] = message
    before_ref[...] = before
    length_ref[...] = jnp.broadcast_to(before_length, length_ref.shape)


def side_body(
    features, in_ref, weight_hbm, act_ref, rate_ref, rows_ref, decay_step, drive_step, maps_ref, row_ref,
    out_ref, share_ref, wide, gate_weight, hidden, gate_token, sem,
):
    count = in_ref.shape[0]
    tokens = in_ref.shape[2]
    states, channels = rate_ref.shape
    fetch = pltpu.make_async_copy(weight_hbm.at[channels:], gate_weight, sem)
    fetch.start()
    sums = jnp.zeros((16, tokens), F32)
    for peer in range(count):
        wide[peer * features : (peer + 1) * features, :] = in_ref[peer, 0:features, :]
        sums = sums + in_ref[peer, features + 16 : features + 32, :].astype(F32)
    scale = lax.rsqrt((sums[0:1] + sums[1:2]) / (count * features) + EPSILON)
    in_map = maps_ref[0:states, :]
    out_map = maps_ref[states:, :]
    step = decay_step[...]
    high = step.astype(BF16)
    rest = (step - high.astype(F32)).astype(BF16)
    lower = jnp.where(iota((tokens, tokens), 0) >= iota((tokens, tokens), 1), 1.0, 0.0).astype(BF16)
    elapsed = dot(lower, high) + dot(lower, rest)
    spread = jnp.where((iota((states, tokens), 1) & (states - 1)) == iota((states, tokens), 0), 1.0, 0.0)
    maps = dot(out_map.astype(BF16), spread.astype(BF16), TN)
    own = (iota((tokens, tokens), 1) // states) == (iota((tokens, tokens), 0) & 7)
    maps = jnp.where(own, maps, 0.0).astype(BF16)
    out_ref[...] = rows_ref[1:2, :] * jnp.transpose(act_ref[...].astype(F32))
    fetch.wait()
    gate = dot(gate_weight[...], wide[...])
    gate = (gate * scale).astype(BF16).astype(F32)
    gate_token[...] = jnp.transpose(gate * (1.0 / (1.0 + jnp.exp(-gate))))
    rate = rate_ref[...] * (-LOG2E)
    by_token = jnp.transpose(out_map)
    for index in range(states):
        remains = jnp.exp2(elapsed * rate[index : index + 1, :]) * gate_token[...]
        share_ref[index] = (by_token[:, index : index + 1] * remains).astype(BF16)
    state = jnp.zeros((states, channels), F32)
    for block in range(tokens // 8):
        for inner in range(8):
            t = block * 8 + inner
            decay = jnp.exp2(decay_step[t : t + 1, :] * rate)
            state = decay * state + drive_step[t : t + 1, :] * in_map[:, t : t + 1]
            hidden[inner * states : (inner + 1) * states, :] = state.astype(BF16)
        out_ref[block * 8 : block * 8 + 8, :] += dot(maps[block * 8 : block * 8 + 8], hidden[...])
    out_ref[...] *= gate_token[...]


def finish_body(me, in_ref, rate_ref, before_ref, length_ref, out_in_ref, share_ref, mixed_ref):
    states, channels = rate_ref.shape
    rate = rate_ref[...] * (-LOG2E)
    state = jnp.zeros((states, channels), F32)
    for peer in range(in_ref.shape[0]):
        final, length = part(in_ref[peer], channels)
        earlier = peer < me[0]
        through = jnp.where(earlier, jnp.exp2(length * rate), 1.0)
        state = through * state + jnp.where(earlier, final, 0.0)
    state = jnp.exp2(length_ref[0:1, :] * rate) * state + before_ref[...]
    scanned = out_in_ref[...]
    for index in range(states):
        scanned = scanned + share_ref[index].astype(F32) * state[index : index + 1, :]
    mixed_ref[...] = jnp.transpose(scanned).astype(BF16)


def local(
    tokens, norm_gain, in_weight, conv_weight, conv_bias, proj_weight, dt_weight, dt_bias,
    decay_rate, skip_gain, doc_starts, group_target,
):
    rows_of, in_row = lax.axis_size("z"), lax.axis_size("x")
    peers = rows_of * in_row
    row_count, features = tokens.shape
    slots = group_target.shape[0]
    width = in_weight.shape[0]
    channels = in_weight.shape[2]
    rank = dt_weight.shape[0]
    states = decay_rate.shape[1]
    shape = jax.ShapeDtypeStruct
    me = lax.axis_index(("z", "x")).astype(jnp.int32).reshape(1)
    starts = doc_starts.reshape(1, row_count)
    my_gain = lax.dynamic_slice_in_dim(norm_gain, lax.axis_index("chan") * features, features)
    my_gain = jnp.broadcast_to(my_gain[:, None], (features, row_count))
    weight = jnp.transpose(in_weight, (1, 2, 0)).reshape(2 * channels, width)
    pieces, starts = call(
        functools.partial(pack_body, slots),
        (shape((peers, 16, row_count), BF16), shape((1, row_count), jnp.int32)),
        [SMEM, HBM, HBM, HBM],
        (me, in_hbm(group_target), in_hbm(tokens.T), in_hbm(starts)),
        [
            pltpu.SMEM((slots,), jnp.int32),
            pltpu.VMEM((features, row_count), BF16),
            pltpu.VMEM((2 * peers + 1, 16, row_count), F32),
            pltpu.SemaphoreType.DMA((3,)),
        ],
    )
    weight = in_hbm(weight)
    sources = (proj_weight.T, dt_weight, decay_rate.T, conv_weight, conv_bias, dt_bias, skip_gain)
    scan_weight, proj, dtw, rate, cols, rows, first = call(
        fetch_body,
        (
            shape((channels, width), BF16),
            shape((rank + 2 * states, channels), BF16),
            shape((rank, channels), BF16),
            shape((states, channels), F32),
            shape((channels, 8), F32),
            shape((8, channels), F32),
            shape((row_count, channels), F32),
        ),
        [HBM] * 8 + [VMEM],
        (weight, *(in_hbm(source) for source in sources), starts),
        [
            pltpu.VMEM(conv_weight.shape, F32),
            pltpu.VMEM((channels,), F32),
            pltpu.VMEM((channels,), F32),
            pltpu.VMEM((channels,), F32),
            pltpu.SemaphoreType.DMA((8,)),
        ],
    )
    arrived = lax.all_to_all(pieces, ("z", "x"), 0, 0, tiled=True)
    payload = call(
        place_body,
        shape((features + 32, row_count), BF16),
        [VMEM, VMEM],
        (arrived, my_gain),
    )
    gathered = lax.all_gather(payload, "chan", axis=0)
    low, act = call(
        functools.partial(project_body, features, conv_weight.shape[0]),
        (shape((rank + 2 * states, row_count), BF16), shape((channels, row_count), BF16)),
        [VMEM] * 5,
        (gathered, scan_weight, cols, proj, starts),
        [pltpu.VMEM((width, 2 * row_count), BF16)],
    )
    lows = lax.all_gather(low, "chan", axis=0)
    lanes = -(-channels // 128) * 128
    by_token = shape((row_count, channels), F32)
    send, decay_step, drive_step, maps = call(
        functools.partial(state_body, rank),
        (
            shape((in_row, states, lanes), BF16),
            by_token,
            by_token,
            shape((2 * states, row_count), F32),
        ),
        [VMEM] * 6,
        (lows, act, dtw, rate, rows, first),
    )
    in_row_ends = lax.all_to_all(send, "x", 0, 0, tiled=True)
    send, before, before_length = call(
        row_body,
        (
            shape((rows_of, states, lanes), BF16),
            shape((states, channels), F32),
            shape((8, channels), F32),
        ),
        [SMEM, VMEM, VMEM],
        (lax.axis_index("x").astype(jnp.int32).reshape(1), in_row_ends, rate),
    )
    out, share = call(
        functools.partial(side_body, features),
        (by_token, shape((states, row_count, channels), BF16)),
        [VMEM, HBM] + [VMEM] * 7,
        (gathered, weight, act, rate, rows, decay_step, drive_step, maps, before_length),
        [
            pltpu.VMEM((width, row_count), BF16),
            pltpu.VMEM((channels, width), BF16),
            pltpu.VMEM((8 * states, channels), BF16),
            pltpu.VMEM((row_count, channels), F32),
            pltpu.SemaphoreType.DMA,
        ],
    )
    ends = lax.all_to_all(send, "z", 0, 0, tiled=True)
    my_row = lax.axis_index("z").astype(jnp.int32).reshape(1)
    mixed = call(
        finish_body,
        shape((channels, row_count), BF16),
        [SMEM] + [VMEM] * 6,
        (my_row, ends, rate, before, before_length, out, share),
    )
    return mixed.T


def solution(mesh):
    peers, chans = mesh.devices.shape
    in_row = 4 if peers % 4 == 0 else 1
    grid = mesh.devices.reshape(peers // in_row, in_row, chans)
    mesh = jax.sharding.Mesh(grid, ("z", "x", "chan"))
    return jax.shard_map(
        local,
        mesh=mesh,
        in_specs=(
            P(("z", "x"), "chan"),
            P(),
            P(None, None, "chan"),
            P(None, "chan"),
            P("chan"),
            P("chan", None),
            P(None, "chan"),
            P("chan"),
            P("chan", None),
            P("chan"),
            P(("z", "x")),
            P(("z", "x")),
        ),
        out_specs=P(("z", "x"), "chan"),
        check_vma=False,
    )
```

```python
import functools
import math

import jax
import jax.numpy as jnp
from jax import lax
from jax.experimental import pallas as pl
from jax.experimental.pallas import tpu as pltpu
from jax.sharding import PartitionSpec as P

EPSILON = 1e-05
LOG2E = math.log2(math.e)
FAR = 1e30
F32 = jnp.float32
BF16 = jnp.bfloat16

VMEM = pl.BlockSpec(memory_space=pltpu.VMEM)
SMEM = pl.BlockSpec(memory_space=pltpu.SMEM)
HBM = pl.BlockSpec(memory_space=pltpu.HBM)

NN = (((1,), (0,)), ((), ()))
NT = (((1,), (1,)), ((), ()))
TN = (((0,), (0,)), ((), ()))


def dot(a, b, dims=NN):
    return lax.dot_general(a, b, dims, preferred_element_type=F32)


def in_hbm(value):
    return pltpu.with_memory_space_constraint(value, pltpu.HBM)


def iota(shape, dim):
    return lax.broadcasted_iota(jnp.int32, shape, dim)


def call(body, outs, specs, args, scratch=(), limit=24):
    return pl.pallas_call(
        body,
        out_shape=outs,
        in_specs=specs,
        out_specs=jax.tree.map(lambda _: VMEM, outs),
        scratch_shapes=list(scratch),
        compiler_params=pltpu.CompilerParams(vmem_limit_bytes=limit << 20),
    )(*args)


def swap_blocks(slabs):
    lanes = 128
    block = iota((16, lanes), 1) >> 3
    slabs = list(slabs) + [None] * (16 - len(slabs))
    for step in (8, 4, 2, 1):
        keep = (block & step) == 0
        for low in range(16):
            if low & step:
                continue
            a, b = slabs[low], slabs[low | step]
            if a is None and b is None:
                continue
            zero = jnp.zeros((16, lanes), F32)
            up = zero if b is None else pltpu.roll(b, 8 * step, 1)
            down = zero if a is None else pltpu.roll(a, lanes - 8 * step, 1)
            slabs[low] = jnp.where(keep, zero if a is None else a, up)
            slabs[low | step] = jnp.where(keep, down, zero if b is None else b)
    return slabs


def pack_body(slots, me, target_hbm, tok_hbm, starts_hbm, out_ref, starts_ref, target, tok_ref, pieces, sems):
    copies = [
        pltpu.make_async_copy(target_hbm, target, sems.at[0]),
        pltpu.make_async_copy(starts_hbm, starts_ref, sems.at[1]),
        pltpu.make_async_copy(tok_hbm, tok_ref, sems.at[2]),
    ]
    for copy in copies:
        copy.start()
    features, tokens = tok_ref.shape
    peers = out_ref.shape[0]
    parts = features // 16
    pieces[...] = jnp.zeros(pieces.shape, F32)
    lane = iota((16, tokens), 1)
    source = iota((tokens, tokens), 0)
    place = iota((tokens, tokens), 1)
    late = (source < features // 2) & ((source & 7) >= 5)
    to_tail = jnp.where(
        late & (place == features // 2 + 3 * (source >> 3) + (source & 7) - 5), 1.0, 0.0
    ).astype(BF16)
    copies[2].wait()
    groups = swap_blocks(
        [tok_ref[16 * piece : 16 * piece + 16, :].astype(F32) for piece in range(parts)]
    )
    tails = dot(jnp.concatenate(groups, axis=0).astype(BF16), to_tail)
    copies[0].wait()
    copies[1].wait()
    fresh = 1.0 - jnp.broadcast_to(starts_ref[...].astype(F32), (16, tokens))
    one = pltpu.roll(fresh, (114 - (tokens - 1)) % tokens, 1)
    two = pltpu.roll(fresh, (113 - (tokens - 1)) % tokens, 1)
    flags = jnp.where(
        lane == 115, 1.0, jnp.where(lane == 114, one, jnp.where(lane == 113, one * two, 0.0))
    )
    for group in range(slots):
        where_to = target[group]
        dev = lax.shift_right_logical(where_to, slots.bit_length() - 1)
        slot = where_to & (slots - 1)
        pieces[dev] = jnp.where(lane == 112, (slot + 1).astype(F32), groups[group])
        follows = (slot == slots - 1) & (dev + 1 < peers)
        pieces[jnp.where(follows, peers + dev + 1, 2 * peers)] = tails[16 * group : 16 * group + 16]
    after = me[0] + 1
    for peer in range(peers):
        whole = pieces[peer] + pieces[peers + peer] + jnp.where(after == peer, flags, 0.0)
        out_ref[peer] = whole.astype(BF16)


def fetch_body(
    weight_hbm, proj_hbm, dtw_hbm, rate_hbm, taps_hbm, conv_bias_hbm, dt_bias_hbm, skip_hbm, starts_ref,
    weight_ref, proj_ref, dtw_ref, rate_ref, cols_ref, rows_ref, first_ref,
    taps_in, conv_bias, dt_bias, skip, sems,
):
    taps, channels = taps_in.shape
    pairs = (
        (taps_hbm, taps_in),
        (conv_bias_hbm, conv_bias),
        (dt_bias_hbm, dt_bias),
        (skip_hbm, skip),
        (weight_hbm.at[0:channels], weight_ref),
        (proj_hbm, proj_ref),
        (dtw_hbm, dtw_ref),
        (rate_hbm, rate_ref),
    )
    copies = [
        pltpu.make_async_copy(source, target, sems.at[index])
        for index, (source, target) in enumerate(pairs)
    ]
    for copy in copies:
        copy.start()
    for copy in copies[:4]:
        copy.wait()
    bias = conv_bias[...].reshape(1, channels)
    blank = jnp.zeros((8 - taps - 1, channels), F32)
    cols_ref[...] = jnp.transpose(jnp.concatenate([taps_in[...], bias, blank], axis=0))
    tokens = starts_ref.shape[1]
    first = jnp.transpose(jnp.broadcast_to(starts_ref[...].astype(F32), (tokens, tokens)))
    first_ref[...] = jnp.broadcast_to(first[:, :1], first_ref.shape)
    rows_ref[0:1, :] = dt_bias[...].reshape(1, channels)
    rows_ref[1:2, :] = skip[...].reshape(1, channels)
    for copy in copies[4:]:
        copy.wait()


def place_body(in_ref, gain_ref, out_ref):
    peers, _, tokens = in_ref.shape
    features = gain_ref.shape[0]
    rows = 16 * peers
    slots = tokens // 8
    parts = features // 16
    arrived = in_ref[...].reshape(rows, tokens)
    spot = jnp.where(iota((16, tokens), 1) == 112, 1.0, 0.0).astype(BF16)
    label = dot(spot, arrived, NT)[:1]
    key = label * 16.0 + (iota((1, rows), 1) & 15).astype(F32)
    want = (iota((16 * slots, rows), 0) + 16).astype(F32)
    pick = jnp.where(key == want, 1.0, 0.0).astype(BF16)
    ordered = dot(pick, arrived)
    total = jnp.sum(in_ref[...].astype(F32), axis=0)
    lane = iota((16, tokens), 1)
    open_tail = jnp.where(lane >= tokens - 3, pltpu.roll(total, tokens - 3 - 113, 1), 0.0)
    mains = swap_blocks([ordered[16 * slot : 16 * slot + 16] for slot in range(slots)])[:parts]
    tails = []
    for piece in range(parts):
        shift = (tokens - 3 - features // 2 - 3 * piece) % tokens
        tails.append((total if shift == 0 else pltpu.roll(total, shift, 1)) * open_tail)
    x_main = jnp.concatenate(mains, axis=0)
    x_tail = jnp.concatenate(tails, axis=0)
    gain = gain_ref[...]
    main_sq = jnp.sum(x_main * x_main, axis=0, keepdims=True)
    tail_sq = jnp.sum(x_tail * x_tail, axis=0, keepdims=True)
    out_ref[0:features, :] = (x_main * gain).astype(BF16)
    x_tail = x_tail * gain
    packed = jnp.zeros((16, tokens), F32)
    for part in range(features // 16):
        shift = (8 * part - (tokens - 8)) % tokens
        packed = packed + pltpu.roll(x_tail[16 * part : 16 * part + 16], shift, 1)
    out_ref[features : features + 16, :] = packed.astype(BF16)
    main_high = main_sq.astype(BF16).astype(F32)
    tail_high = tail_sq.astype(BF16).astype(F32)
    line = iota((16, tokens), 0)
    sums = jnp.where(
        line == 0,
        main_high,
        jnp.where(
            line == 1,
            main_sq - main_high,
            jnp.where(line == 2, tail_high, jnp.where(line == 3, tail_sq - tail_high, 0.0)),
        ),
    )
    out_ref[features + 16 : features + 32, :] = sums.astype(BF16)


def project_body(
    features, taps, in_ref, weight_ref, taps_ref, proj_ref, starts_ref, low_ref, act_ref, wide,
):
    count = in_ref.shape[0]
    tokens = in_ref.shape[2]
    channels = act_ref.shape[0]
    width = count * features
    sums = jnp.zeros((16, tokens), F32)
    for peer in range(count):
        base = peer * features
        wide[base : base + features, 0:tokens] = in_ref[peer, 0:features, :]
        packed = in_ref[peer, features : features + 16, :].astype(F32)
        sums = sums + in_ref[peer, features + 16 : features + 32, :].astype(F32)
        for part in range(features // 16):
            shift = (tokens - 8 - 8 * part) % tokens
            moved = packed if shift == 0 else pltpu.roll(packed, shift, 1)
            wide[base + 16 * part : base + 16 * part + 16, tokens:] = moved.astype(BF16)
    scale_main = lax.rsqrt((sums[0:1] + sums[1:2]) / width + EPSILON)
    scale_tail = lax.rsqrt((sums[2:3] + sums[3:4]) / width + EPSILON)
    both = dot(weight_ref[...], wide[...])
    x_in = (both[:, :tokens] * scale_main).astype(BF16).astype(F32)
    tail = (both[:, tokens:] * scale_tail).astype(BF16).astype(F32)
    fresh = 1.0 - jnp.broadcast_to(starts_ref[...].astype(F32), (8, tokens))
    lane8 = iota((8, tokens), 1)
    lane = iota((channels, tokens), 1)
    convolved = taps_ref[:, taps : taps + 1] + taps_ref[:, taps - 1 : taps] * x_in
    mask = fresh
    for back in range(1, taps):
        if back > 1:
            mask = mask * jnp.where(lane8 < back - 1, 1.0, pltpu.roll(fresh, back - 1, 1))
        behind = pltpu.roll(jnp.where(lane >= tokens - back, tail, x_in), back, 1)
        tap = taps_ref[:, taps - 1 - back : taps - back]
        convolved = convolved + jnp.where(mask[:1] > 0.5, tap * behind, 0.0)
    act = (convolved * (1.0 / (1.0 + jnp.exp(-convolved)))).astype(BF16)
    act_ref[...] = act
    low_ref[...] = dot(proj_ref[...], act).astype(BF16)


def join(state, length, lanes):
    states, channels = state.shape
    spare = lanes - channels
    pieces = channels // spare
    length_high = length.astype(BF16).astype(F32)
    line = iota((states, spare), 0)
    ends = jnp.zeros((states, spare), F32)
    for piece in range(pieces):
        high = length_high[:, piece * spare : piece * spare + spare]
        rest = length[:, piece * spare : piece * spare + spare] - high
        ends = jnp.where(line == piece, high, ends)
        ends = jnp.where(line == piece + pieces, rest, ends)
    return jnp.concatenate([state, ends], axis=1).astype(BF16)


def part(message, channels):
    message = message.astype(F32)
    pieces = channels // (message.shape[1] - channels)
    ends = message[:pieces, channels:] + message[pieces : 2 * pieces, channels:]
    length = jnp.concatenate([ends[piece : piece + 1] for piece in range(pieces)], axis=1)
    return message[:, :channels], length


def state_body(
    rank, in_ref, act_ref, dtw_ref, rate_ref, rows_ref, first_ref,
    send_ref, decay_step, drive_step, maps_ref,
):
    tokens = in_ref.shape[2]
    states, channels = rate_ref.shape
    low = in_ref[0].astype(F32)
    for peer in range(1, in_ref.shape[0]):
        low = low + in_ref[peer].astype(F32)
    dt_low = low[:rank].astype(BF16)
    in_map = low[rank : rank + states]
    maps_ref[...] = low[rank:]
    raw = dot(dt_low, dtw_ref[...], TN) + rows_ref[0:1, :]
    small = jnp.exp(-jnp.abs(raw))
    series = small * (1.0 - small * (0.5 - small * (1.0 / 3.0 - small * 0.25)))
    step = jnp.maximum(raw, 0.0) + jnp.where(small < 0.01, series, jnp.log(1.0 + small))
    drive_step[...] = step * jnp.transpose(act_ref[...].astype(F32))
    step = jnp.where(first_ref[...] > 0.5, FAR, step)
    decay_step[...] = step
    last = jnp.sum(step, axis=0, keepdims=True)
    rate = rate_ref[...] * (-LOG2E)
    state = jnp.zeros((states, channels), F32)
    for t in range(tokens):
        decay = jnp.exp2(decay_step[t : t + 1, :] * rate)
        state = decay * state + drive_step[t : t + 1, :] * in_map[:, t : t + 1]
    message = join(state, last, send_ref.shape[2])
    for peer in range(send_ref.shape[0]):
        send_ref[peer] = message


def row_body(me, in_ref, rate_ref, out_ref, send_ref, before_ref, length_ref):
    states, channels = rate_ref.shape
    rate = rate_ref[...] * (-LOG2E)
    whole = jnp.zeros((states, channels), F32)
    before = whole
    whole_length = jnp.zeros((1, channels), F32)
    before_length = whole_length
    for peer in range(in_ref.shape[0]):
        final, length = part(in_ref[peer], channels)
        earlier = peer < me[0]
        through = jnp.exp2(length * rate)
        whole = through * whole + final
        before = jnp.where(earlier, whole, before)
        whole_length = whole_length + length
        before_length = jnp.where(earlier, whole_length, before_length)
    message = join(whole, whole_length, send_ref.shape[2])
    for peer in range(send_ref.shape[0]):
        send_ref[peer] = message
    before_ref[...] = before
    length_ref[...] = jnp.broadcast_to(before_length, length_ref.shape)


def side_body(
    features, in_ref, weight_hbm, act_ref, rate_ref, rows_ref, decay_step, drive_step, maps_ref,
    out_ref, share_ref, wide, gate_weight, hidden, gate_token, sem,
):
    count = in_ref.shape[0]
    tokens = in_ref.shape[2]
    states, channels = rate_ref.shape
    fetch = pltpu.make_async_copy(weight_hbm.at[channels:], gate_weight, sem)
    fetch.start()
    sums = jnp.zeros((16, tokens), F32)
    for peer in range(count):
        wide[peer * features : (peer + 1) * features, :] = in_ref[peer, 0:features, :]
        sums = sums + in_ref[peer, features + 16 : features + 32, :].astype(F32)
    scale = lax.rsqrt((sums[0:1] + sums[1:2]) / (count * features) + EPSILON)
    in_map = maps_ref[0:states, :]
    out_map = maps_ref[states:, :]
    step = decay_step[...]
    high = step.astype(BF16)
    rest = (step - high.astype(F32)).astype(BF16)
    lower = jnp.where(iota((tokens, tokens), 0) >= iota((tokens, tokens), 1), 1.0, 0.0).astype(BF16)
    elapsed = dot(lower, high) + dot(lower, rest)
    spread = jnp.where((iota((states, tokens), 1) & (states - 1)) == iota((states, tokens), 0), 1.0, 0.0)
    maps = dot(out_map.astype(BF16), spread.astype(BF16), TN)
    own = (iota((tokens, tokens), 1) // states) == (iota((tokens, tokens), 0) & 7)
    maps = jnp.where(own, maps, 0.0).astype(BF16)
    out_ref[...] = rows_ref[1:2, :] * jnp.transpose(act_ref[...].astype(F32))
    fetch.wait()
    gate = dot(gate_weight[...], wide[...])
    gate = (gate * scale).astype(BF16).astype(F32)
    gate_token[...] = jnp.transpose(gate * (1.0 / (1.0 + jnp.exp(-gate))))
    rate = rate_ref[...] * (-LOG2E)
    by_token = jnp.transpose(out_map)
    for index in range(states):
        remains = jnp.exp2(elapsed * rate[index : index + 1, :]) * gate_token[...]
        share_ref[index] = (by_token[:, index : index + 1] * remains).astype(BF16)
    state = jnp.zeros((states, channels), F32)
    for block in range(tokens // 8):
        for inner in range(8):
            t = block * 8 + inner
            decay = jnp.exp2(decay_step[t : t + 1, :] * rate)
            state = decay * state + drive_step[t : t + 1, :] * in_map[:, t : t + 1]
            hidden[inner * states : (inner + 1) * states, :] = state.astype(BF16)
        out_ref[block * 8 : block * 8 + 8, :] += dot(maps[block * 8 : block * 8 + 8], hidden[...])
    out_ref[...] *= gate_token[...]


def finish_body(me, in_ref, rate_ref, before_ref, length_ref, out_in_ref, share_ref, mixed_ref):
    states, channels = rate_ref.shape
    rate = rate_ref[...] * (-LOG2E)
    state = jnp.zeros((states, channels), F32)
    for peer in range(in_ref.shape[0]):
        final, length = part(in_ref[peer], channels)
        earlier = peer < me[0]
        through = jnp.where(earlier, jnp.exp2(length * rate), 1.0)
        state = through * state + jnp.where(earlier, final, 0.0)
    state = jnp.exp2(length_ref[0:1, :] * rate) * state + before_ref[...]
    scanned = out_in_ref[...]
    for index in range(states):
        scanned = scanned + share_ref[index].astype(F32) * state[index : index + 1, :]
    mixed_ref[...] = jnp.transpose(scanned).astype(BF16)


def local(
    tokens, norm_gain, in_weight, conv_weight, conv_bias, proj_weight, dt_weight, dt_bias,
    decay_rate, skip_gain, doc_starts, group_target,
):
    rows_of, in_row = lax.axis_size("z"), lax.axis_size("x")
    peers = rows_of * in_row
    row_count, features = tokens.shape
    slots = group_target.shape[0]
    width = in_weight.shape[0]
    channels = in_weight.shape[2]
    rank = dt_weight.shape[0]
    states = decay_rate.shape[1]
    shape = jax.ShapeDtypeStruct
    me = lax.axis_index(("z", "x")).astype(jnp.int32).reshape(1)
    starts = doc_starts.reshape(1, row_count)
    my_gain = lax.dynamic_slice_in_dim(norm_gain, lax.axis_index("chan") * features, features)
    my_gain = jnp.broadcast_to(my_gain[:, None], (features, row_count))
    weight = jnp.transpose(in_weight, (1, 2, 0)).reshape(2 * channels, width)
    pieces, starts = call(
        functools.partial(pack_body, slots),
        (shape((peers, 16, row_count), BF16), shape((1, row_count), jnp.int32)),
        [SMEM, HBM, HBM, HBM],
        (me, in_hbm(group_target), in_hbm(tokens.T), in_hbm(starts)),
        [
            pltpu.SMEM((slots,), jnp.int32),
            pltpu.VMEM((features, row_count), BF16),
            pltpu.VMEM((2 * peers + 1, 16, row_count), F32),
            pltpu.SemaphoreType.DMA((3,)),
        ],
    )
    weight = in_hbm(weight)
    sources = (proj_weight.T, dt_weight, decay_rate.T, conv_weight, conv_bias, dt_bias, skip_gain)
    scan_weight, proj, dtw, rate, cols, rows, first = call(
        fetch_body,
        (
            shape((channels, width), BF16),
            shape((rank + 2 * states, channels), BF16),
            shape((rank, channels), BF16),
            shape((states, channels), F32),
            shape((channels, 8), F32),
            shape((8, channels), F32),
            shape((row_count, channels), F32),
        ),
        [HBM] * 8 + [VMEM],
        (weight, *(in_hbm(source) for source in sources), starts),
        [
            pltpu.VMEM(conv_weight.shape, F32),
            pltpu.VMEM((channels,), F32),
            pltpu.VMEM((channels,), F32),
            pltpu.VMEM((channels,), F32),
            pltpu.SemaphoreType.DMA((8,)),
        ],
    )
    arrived = lax.all_to_all(pieces, ("z", "x"), 0, 0, tiled=True)
    payload = call(
        place_body,
        shape((features + 32, row_count), BF16),
        [VMEM, VMEM],
        (arrived, my_gain),
    )
    gathered = lax.all_gather(payload, "chan", axis=0)
    low, act = call(
        functools.partial(project_body, features, conv_weight.shape[0]),
        (shape((rank + 2 * states, row_count), BF16), shape((channels, row_count), BF16)),
        [VMEM] * 5,
        (gathered, scan_weight, cols, proj, starts),
        [pltpu.VMEM((width, 2 * row_count), BF16)],
    )
    lows = lax.all_gather(low, "chan", axis=0)
    lanes = -(-channels // 128) * 128
    by_token = shape((row_count, channels), F32)
    send, decay_step, drive_step, maps = call(
        functools.partial(state_body, rank),
        (
            shape((in_row, states, lanes), BF16),
            by_token,
            by_token,
            shape((2 * states, row_count), F32),
        ),
        [VMEM] * 6,
        (lows, act, dtw, rate, rows, first),
    )
    in_row_ends = lax.all_to_all(send, "x", 0, 0, tiled=True)
    out, share = call(
        functools.partial(side_body, features),
        (by_token, shape((states, row_count, channels), BF16)),
        [VMEM, HBM] + [VMEM] * 6,
        (gathered, weight, act, rate, rows, decay_step, drive_step, maps),
        [
            pltpu.VMEM((width, row_count), BF16),
            pltpu.VMEM((channels, width), BF16),
            pltpu.VMEM((8 * states, channels), BF16),
            pltpu.VMEM((row_count, channels), F32),
            pltpu.SemaphoreType.DMA,
        ],
    )
    send, before, before_length = call(
        row_body,
        (
            shape((rows_of, states, lanes), BF16),
            shape((states, channels), F32),
            shape((8, channels), F32),
        ),
        [SMEM, VMEM, VMEM, VMEM],
        (lax.axis_index("x").astype(jnp.int32).reshape(1), in_row_ends, rate, out),
    )
    ends = lax.all_to_all(send, "z", 0, 0, tiled=True)
    my_row = lax.axis_index("z").astype(jnp.int32).reshape(1)
    mixed = call(
        finish_body,
        shape((channels, row_count), BF16),
        [SMEM] + [VMEM] * 6,
        (my_row, ends, rate, before, before_length, out, share),
    )
    return mixed.T


def solution(mesh):
    peers, chans = mesh.devices.shape
    in_row = 4 if peers % 4 == 0 else 1
    grid = mesh.devices.reshape(peers // in_row, in_row, chans)
    mesh = jax.sharding.Mesh(grid, ("z", "x", "chan"))
    return jax.shard_map(
        local,
        mesh=mesh,
        in_specs=(
            P(("z", "x"), "chan"),
            P(),
            P(None, None, "chan"),
            P(None, "chan"),
            P("chan"),
            P("chan", None),
            P(None, "chan"),
            P("chan"),
            P("chan", None),
            P("chan"),
            P(("z", "x")),
            P(("z", "x")),
        ),
        out_specs=P(("z", "x"), "chan"),
        check_vma=False,
    )
```

```python
import functools
import math

import jax
import jax.numpy as jnp
from jax import lax
from jax.experimental import pallas as pl
from jax.experimental.pallas import tpu as pltpu
from jax.sharding import PartitionSpec as P

EPSILON = 1e-05
LOG2E = math.log2(math.e)
FAR = 1e30
F32 = jnp.float32
BF16 = jnp.bfloat16

VMEM = pl.BlockSpec(memory_space=pltpu.VMEM)
SMEM = pl.BlockSpec(memory_space=pltpu.SMEM)
HBM = pl.BlockSpec(memory_space=pltpu.HBM)

NN = (((1,), (0,)), ((), ()))
NT = (((1,), (1,)), ((), ()))
TN = (((0,), (0,)), ((), ()))


def dot(a, b, dims=NN):
    return lax.dot_general(a, b, dims, preferred_element_type=F32)


def in_hbm(value):
    return pltpu.with_memory_space_constraint(value, pltpu.HBM)


def iota(shape, dim):
    return lax.broadcasted_iota(jnp.int32, shape, dim)


def call(body, outs, specs, args, scratch=(), limit=24):
    return pl.pallas_call(
        body,
        out_shape=outs,
        in_specs=specs,
        out_specs=jax.tree.map(lambda _: VMEM, outs),
        scratch_shapes=list(scratch),
        compiler_params=pltpu.CompilerParams(vmem_limit_bytes=limit << 20),
    )(*args)


def swap_blocks(slabs):
    lanes = 128
    block = iota((16, lanes), 1) >> 3
    slabs = list(slabs) + [None] * (16 - len(slabs))
    for step in (8, 4, 2, 1):
        keep = (block & step) == 0
        for low in range(16):
            if low & step:
                continue
            a, b = slabs[low], slabs[low | step]
            if a is None and b is None:
                continue
            zero = jnp.zeros((16, lanes), F32)
            up = zero if b is None else pltpu.roll(b, 8 * step, 1)
            down = zero if a is None else pltpu.roll(a, lanes - 8 * step, 1)
            slabs[low] = jnp.where(keep, zero if a is None else a, up)
            slabs[low | step] = jnp.where(keep, down, zero if b is None else b)
    return slabs


def pack_body(
    slots, me, chan, target_hbm, tok_hbm, starts_hbm,
    weight_hbm, proj_hbm, dtw_hbm, rate_hbm, taps_hbm, conv_bias_hbm, dt_bias_hbm, skip_hbm, gain_hbm,
    out_ref, starts_ref, weight_ref, proj_ref, dtw_ref, rate_ref, cols_ref, rows_ref, first_ref, gain_ref,
    target, tok_ref, pieces, taps_in, conv_bias, dt_bias, skip, gain, sems, more_sems,
):
    taps, channels = taps_in.shape
    pairs = (
        (taps_hbm, taps_in),
        (conv_bias_hbm, conv_bias),
        (dt_bias_hbm, dt_bias),
        (skip_hbm, skip),
        (gain_hbm, gain),
        (weight_hbm.at[0:channels], weight_ref),
        (proj_hbm, proj_ref),
        (dtw_hbm, dtw_ref),
        (rate_hbm, rate_ref),
    )
    fetches = [
        pltpu.make_async_copy(source, into, more_sems.at[index])
        for index, (source, into) in enumerate(pairs)
    ]
    copies = [
        pltpu.make_async_copy(target_hbm, target, sems.at[0]),
        pltpu.make_async_copy(starts_hbm, starts_ref, sems.at[1]),
        pltpu.make_async_copy(tok_hbm, tok_ref, sems.at[2]),
    ]
    for copy in copies + fetches:
        copy.start()
    features, tokens = tok_ref.shape
    peers = out_ref.shape[0]
    parts = features // 16
    pieces[...] = jnp.zeros(pieces.shape, F32)
    lane = iota((16, tokens), 1)
    source = iota((tokens, tokens), 0)
    place = iota((tokens, tokens), 1)
    late = (source < features // 2) & ((source & 7) >= 5)
    to_tail = jnp.where(
        late & (place == features // 2 + 3 * (source >> 3) + (source & 7) - 5), 1.0, 0.0
    ).astype(BF16)
    copies[2].wait()
    groups = swap_blocks(
        [tok_ref[16 * piece : 16 * piece + 16, :].astype(F32) for piece in range(parts)]
    )
    tails = dot(jnp.concatenate(groups, axis=0).astype(BF16), to_tail)
    copies[0].wait()
    copies[1].wait()
    fresh = 1.0 - jnp.broadcast_to(starts_ref[...].astype(F32), (16, tokens))
    one = pltpu.roll(fresh, (114 - (tokens - 1)) % tokens, 1)
    two = pltpu.roll(fresh, (113 - (tokens - 1)) % tokens, 1)
    flags = jnp.where(
        lane == 115, 1.0, jnp.where(lane == 114, one, jnp.where(lane == 113, one * two, 0.0))
    )
    for group in range(slots):
        where_to = target[group]
        dev = lax.shift_right_logical(where_to, slots.bit_length() - 1)
        slot = where_to & (slots - 1)
        pieces[dev] = jnp.where(lane == 112, (slot + 1).astype(F32), groups[group])
        follows = (slot == slots - 1) & (dev + 1 < peers)
        pieces[jnp.where(follows, peers + dev + 1, 2 * peers)] = tails[16 * group : 16 * group + 16]
    after = me[0] + 1
    for peer in range(peers):
        whole = pieces[peer] + pieces[peers + peer] + jnp.where(after == peer, flags, 0.0)
        out_ref[peer] = whole.astype(BF16)
    for fetch in fetches[:5]:
        fetch.wait()
    bias = conv_bias[...].reshape(1, channels)
    blank = jnp.zeros((8 - taps - 1, channels), F32)
    cols_ref[...] = jnp.transpose(jnp.concatenate([taps_in[...], bias, blank], axis=0))
    first = jnp.transpose(jnp.broadcast_to(starts_ref[...].astype(F32), (tokens, tokens)))
    first_ref[...] = jnp.broadcast_to(first[:, :1], first_ref.shape)
    rows_ref[0:1, :] = dt_bias[...].reshape(1, channels)
    rows_ref[1:2, :] = skip[...].reshape(1, channels)
    gains = gain[...].reshape(1, gain.shape[0])
    mine = jnp.zeros((1, features), F32)
    for index in range(gain.shape[0] // features):
        mine = jnp.where(chan[0] == index, gains[:, index * features : (index + 1) * features], mine)
    gain_ref[...] = jnp.transpose(jnp.broadcast_to(mine, (tokens, features)))
    for fetch in fetches[5:]:
        fetch.wait()


def place_body(in_ref, gain_ref, out_ref):
    peers, _, tokens = in_ref.shape
    features = gain_ref.shape[0]
    rows = 16 * peers
    slots = tokens // 8
    parts = features // 16
    arrived = in_ref[...].reshape(rows, tokens)
    spot = jnp.where(iota((16, tokens), 1) == 112, 1.0, 0.0).astype(BF16)
    label = dot(spot, arrived, NT)[:1]
    key = label * 16.0 + (iota((1, rows), 1) & 15).astype(F32)
    want = (iota((16 * slots, rows), 0) + 16).astype(F32)
    pick = jnp.where(key == want, 1.0, 0.0).astype(BF16)
    ordered = dot(pick, arrived)
    total = jnp.sum(in_ref[...].astype(F32), axis=0)
    lane = iota((16, tokens), 1)
    open_tail = jnp.where(lane >= tokens - 3, pltpu.roll(total, tokens - 3 - 113, 1), 0.0)
    mains = swap_blocks([ordered[16 * slot : 16 * slot + 16] for slot in range(slots)])[:parts]
    tails = []
    for piece in range(parts):
        shift = (tokens - 3 - features // 2 - 3 * piece) % tokens
        tails.append((total if shift == 0 else pltpu.roll(total, shift, 1)) * open_tail)
    x_main = jnp.concatenate(mains, axis=0)
    x_tail = jnp.concatenate(tails, axis=0)
    gain = gain_ref[...]
    main_sq = jnp.sum(x_main * x_main, axis=0, keepdims=True)
    tail_sq = jnp.sum(x_tail * x_tail, axis=0, keepdims=True)
    out_ref[0:features, :] = (x_main * gain).astype(BF16)
    x_tail = x_tail * gain
    packed = jnp.zeros((16, tokens), F32)
    for part in range(features // 16):
        shift = (8 * part - (tokens - 8)) % tokens
        packed = packed + pltpu.roll(x_tail[16 * part : 16 * part + 16], shift, 1)
    out_ref[features : features + 16, :] = packed.astype(BF16)
    main_high = main_sq.astype(BF16).astype(F32)
    tail_high = tail_sq.astype(BF16).astype(F32)
    line = iota((16, tokens), 0)
    sums = jnp.where(
        line == 0,
        main_high,
        jnp.where(
            line == 1,
            main_sq - main_high,
            jnp.where(line == 2, tail_high, jnp.where(line == 3, tail_sq - tail_high, 0.0)),
        ),
    )
    out_ref[features + 16 : features + 32, :] = sums.astype(BF16)


def project_body(
    features, taps, in_ref, weight_ref, taps_ref, proj_ref, starts_ref, low_ref, act_ref, wide,
):
    count = in_ref.shape[0]
    tokens = in_ref.shape[2]
    channels = act_ref.shape[0]
    width = count * features
    sums = jnp.zeros((16, tokens), F32)
    for peer in range(count):
        base = peer * features
        wide[base : base + features, 0:tokens] = in_ref[peer, 0:features, :]
        packed = in_ref[peer, features : features + 16, :].astype(F32)
        sums = sums + in_ref[peer, features + 16 : features + 32, :].astype(F32)
        for part in range(features // 16):
            shift = (tokens - 8 - 8 * part) % tokens
            moved = packed if shift == 0 else pltpu.roll(packed, shift, 1)
            wide[base + 16 * part : base + 16 * part + 16, tokens:] = moved.astype(BF16)
    scale_main = lax.rsqrt((sums[0:1] + sums[1:2]) / width + EPSILON)
    scale_tail = lax.rsqrt((sums[2:3] + sums[3:4]) / width + EPSILON)
    both = dot(weight_ref[...], wide[...])
    x_in = (both[:, :tokens] * scale_main).astype(BF16).astype(F32)
    tail = (both[:, tokens:] * scale_tail).astype(BF16).astype(F32)
    fresh = 1.0 - jnp.broadcast_to(starts_ref[...].astype(F32), (8, tokens))
    lane8 = iota((8, tokens), 1)
    lane = iota((channels, tokens), 1)
    convolved = taps_ref[:, taps : taps + 1] + taps_ref[:, taps - 1 : taps] * x_in
    mask = fresh
    for back in range(1, taps):
        if back > 1:
            mask = mask * jnp.where(lane8 < back - 1, 1.0, pltpu.roll(fresh, back - 1, 1))
        behind = pltpu.roll(jnp.where(lane >= tokens - back, tail, x_in), back, 1)
        tap = taps_ref[:, taps - 1 - back : taps - back]
        convolved = convolved + jnp.where(mask[:1] > 0.5, tap * behind, 0.0)
    act = (convolved * (1.0 / (1.0 + jnp.exp(-convolved)))).astype(BF16)
    act_ref[...] = act
    low_ref[...] = dot(proj_ref[...], act).astype(BF16)


def join(state, length, lanes):
    states, channels = state.shape
    spare = lanes - channels
    pieces = channels // spare
    length_high = length.astype(BF16).astype(F32)
    line = iota((states, spare), 0)
    ends = jnp.zeros((states, spare), F32)
    for piece in range(pieces):
        high = length_high[:, piece * spare : piece * spare + spare]
        rest = length[:, piece * spare : piece * spare + spare] - high
        ends = jnp.where(line == piece, high, ends)
        ends = jnp.where(line == piece + pieces, rest, ends)
    return jnp.concatenate([state, ends], axis=1).astype(BF16)


def part(message, channels):
    message = message.astype(F32)
    pieces = channels // (message.shape[1] - channels)
    ends = message[:pieces, channels:] + message[pieces : 2 * pieces, channels:]
    length = jnp.concatenate([ends[piece : piece + 1] for piece in range(pieces)], axis=1)
    return message[:, :channels], length


def state_body(
    rank, in_ref, act_ref, dtw_ref, rate_ref, rows_ref, first_ref,
    send_ref, decay_step, drive_step, maps_ref,
):
    tokens = in_ref.shape[2]
    states, channels = rate_ref.shape
    low = in_ref[0].astype(F32)
    for peer in range(1, in_ref.shape[0]):
        low = low + in_ref[peer].astype(F32)
    dt_low = low[:rank].astype(BF16)
    in_map = low[rank : rank + states]
    maps_ref[...] = low[rank:]
    raw = dot(dt_low, dtw_ref[...], TN) + rows_ref[0:1, :]
    small = jnp.exp(-jnp.abs(raw))
    series = small * (1.0 - small * (0.5 - small * (1.0 / 3.0 - small * 0.25)))
    step = jnp.maximum(raw, 0.0) + jnp.where(small < 0.01, series, jnp.log(1.0 + small))
    drive_step[...] = step * jnp.transpose(act_ref[...].astype(F32))
    step = jnp.where(first_ref[...] > 0.5, FAR, step)
    decay_step[...] = step
    last = jnp.sum(step, axis=0, keepdims=True)
    rate = rate_ref[...] * (-LOG2E)
    stretches = 4
    length = tokens // stretches
    parts = [jnp.zeros((states, channels), F32)] * stretches
    for offset in range(length):
        for index in range(stretches):
            t = index * length + offset
            decay = jnp.exp2(decay_step[t : t + 1, :] * rate)
            parts[index] = decay * parts[index] + drive_step[t : t + 1, :] * in_map[:, t : t + 1]
    state = parts[0]
    for index in range(1, stretches):
        spent = jnp.sum(step[index * length : (index + 1) * length], axis=0, keepdims=True)
        state = jnp.exp2(spent * rate) * state + parts[index]
    message = join(state, last, send_ref.shape[2])
    for peer in range(send_ref.shape[0]):
        send_ref[peer] = message


def row_body(me, in_ref, rate_ref, send_ref, before_ref, length_ref):
    states, channels = rate_ref.shape
    rate = rate_ref[...] * (-LOG2E)
    whole = jnp.zeros((states, channels), F32)
    before = whole
    whole_length = jnp.zeros((1, channels), F32)
    before_length = whole_length
    for peer in range(in_ref.shape[0]):
        final, length = part(in_ref[peer], channels)
        earlier = peer < me[0]
        through = jnp.exp2(length * rate)
        whole = through * whole + final
        before = jnp.where(earlier, whole, before)
        whole_length = whole_length + length
        before_length = jnp.where(earlier, whole_length, before_length)
    message = join(whole, whole_length, send_ref.shape[2])
    for peer in range(send_ref.shape[0]):
        send_ref[peer] = message
    before_ref[...] = before
    length_ref[...] = jnp.broadcast_to(before_length, length_ref.shape)


def side_body(
    features, in_ref, weight_hbm, act_ref, rate_ref, rows_ref, decay_step, drive_step, maps_ref, row_ref,
    out_ref, share_ref, wide, gate_weight, hidden, gate_token, sem,
):
    count = in_ref.shape[0]
    tokens = in_ref.shape[2]
    states, channels = rate_ref.shape
    fetch = pltpu.make_async_copy(weight_hbm.at[channels:], gate_weight, sem)
    fetch.start()
    sums = jnp.zeros((16, tokens), F32)
    for peer in range(count):
        wide[peer * features : (peer + 1) * features, :] = in_ref[peer, 0:features, :]
        sums = sums + in_ref[peer, features + 16 : features + 32, :].astype(F32)
    scale = lax.rsqrt((sums[0:1] + sums[1:2]) / (count * features) + EPSILON)
    in_map = maps_ref[0:states, :]
    out_map = maps_ref[states:, :]
    step = decay_step[...]
    high = step.astype(BF16)
    rest = (step - high.astype(F32)).astype(BF16)
    lower = jnp.where(iota((tokens, tokens), 0) >= iota((tokens, tokens), 1), 1.0, 0.0).astype(BF16)
    elapsed = dot(lower, high) + dot(lower, rest)
    spread = jnp.where((iota((states, tokens), 1) & (states - 1)) == iota((states, tokens), 0), 1.0, 0.0)
    maps = dot(out_map.astype(BF16), spread.astype(BF16), TN)
    own = (iota((tokens, tokens), 1) // states) == (iota((tokens, tokens), 0) & 7)
    maps = jnp.where(own, maps, 0.0).astype(BF16)
    out_ref[...] = rows_ref[1:2, :] * jnp.transpose(act_ref[...].astype(F32))
    fetch.wait()
    gate = dot(gate_weight[...], wide[...])
    gate = (gate * scale).astype(BF16).astype(F32)
    gate_token[...] = jnp.transpose(gate * (1.0 / (1.0 + jnp.exp(-gate))))
    rate = rate_ref[...] * (-LOG2E)
    by_token = jnp.transpose(out_map)
    for index in range(states):
        remains = jnp.exp2(elapsed * rate[index : index + 1, :]) * gate_token[...]
        share_ref[index] = (by_token[:, index : index + 1] * remains).astype(BF16)
    state = jnp.zeros((states, channels), F32)
    for block in range(tokens // 8):
        for inner in range(8):
            t = block * 8 + inner
            decay = jnp.exp2(decay_step[t : t + 1, :] * rate)
            state = decay * state + drive_step[t : t + 1, :] * in_map[:, t : t + 1]
            hidden[inner * states : (inner + 1) * states, :] = state.astype(BF16)
        out_ref[block * 8 : block * 8 + 8, :] += dot(maps[block * 8 : block * 8 + 8], hidden[...])
    out_ref[...] *= gate_token[...]


def finish_body(me, in_ref, rate_ref, before_ref, length_ref, out_in_ref, share_ref, mixed_ref):
    states, channels = rate_ref.shape
    rate = rate_ref[...] * (-LOG2E)
    state = jnp.zeros((states, channels), F32)
    for peer in range(in_ref.shape[0]):
        final, length = part(in_ref[peer], channels)
        earlier = peer < me[0]
        through = jnp.where(earlier, jnp.exp2(length * rate), 1.0)
        state = through * state + jnp.where(earlier, final, 0.0)
    state = jnp.exp2(length_ref[0:1, :] * rate) * state + before_ref[...]
    scanned = out_in_ref[...]
    for index in range(states):
        scanned = scanned + share_ref[index].astype(F32) * state[index : index + 1, :]
    mixed_ref[...] = jnp.transpose(scanned).astype(BF16)


def local(
    tokens, norm_gain, in_weight, conv_weight, conv_bias, proj_weight, dt_weight, dt_bias,
    decay_rate, skip_gain, doc_starts, group_target,
):
    rows_of, in_row = lax.axis_size("z"), lax.axis_size("x")
    peers = rows_of * in_row
    row_count, features = tokens.shape
    slots = group_target.shape[0]
    width = in_weight.shape[0]
    channels = in_weight.shape[2]
    rank = dt_weight.shape[0]
    states = decay_rate.shape[1]
    shape = jax.ShapeDtypeStruct
    me = lax.axis_index(("z", "x")).astype(jnp.int32).reshape(1)
    starts = doc_starts.reshape(1, row_count)
    chan = lax.axis_index("chan").astype(jnp.int32).reshape(1)
    weight = jnp.transpose(in_weight, (1, 2, 0)).reshape(2 * channels, width)
    weight = in_hbm(weight)
    sources = (
        proj_weight.T, dt_weight, decay_rate.T, conv_weight, conv_bias, dt_bias, skip_gain, norm_gain,
    )
    pieces, starts, scan_weight, proj, dtw, rate, cols, rows, first, my_gain = call(
        functools.partial(pack_body, slots),
        (
            shape((peers, 16, row_count), BF16),
            shape((1, row_count), jnp.int32),
            shape((channels, width), BF16),
            shape((rank + 2 * states, channels), BF16),
            shape((rank, channels), BF16),
            shape((states, channels), F32),
            shape((channels, 8), F32),
            shape((8, channels), F32),
            shape((row_count, channels), F32),
            shape((features, row_count), F32),
        ),
        [SMEM, SMEM] + [HBM] * 12,
        (
            me, chan, in_hbm(group_target), in_hbm(tokens.T), in_hbm(starts), weight,
            *(in_hbm(source) for source in sources),
        ),
        [
            pltpu.SMEM((slots,), jnp.int32),
            pltpu.VMEM((features, row_count), BF16),
            pltpu.VMEM((2 * peers + 1, 16, row_count), F32),
            pltpu.VMEM(conv_weight.shape, F32),
            pltpu.VMEM((channels,), F32),
            pltpu.VMEM((channels,), F32),
            pltpu.VMEM((channels,), F32),
            pltpu.VMEM((width,), F32),
            pltpu.SemaphoreType.DMA((3,)),
            pltpu.SemaphoreType.DMA((9,)),
        ],
    )
    arrived = lax.all_to_all(pieces, ("z", "x"), 0, 0, tiled=True)
    payload = call(
        place_body,
        shape((features + 32, row_count), BF16),
        [VMEM, VMEM],
        (arrived, my_gain),
    )
    gathered = lax.all_gather(payload, "chan", axis=0)
    low, act = call(
        functools.partial(project_body, features, conv_weight.shape[0]),
        (shape((rank + 2 * states, row_count), BF16), shape((channels, row_count), BF16)),
        [VMEM] * 5,
        (gathered, scan_weight, cols, proj, starts),
        [pltpu.VMEM((width, 2 * row_count), BF16)],
    )
    lows = lax.all_gather(low, "chan", axis=0)
    lanes = -(-channels // 128) * 128
    by_token = shape((row_count, channels), F32)
    send, decay_step, drive_step, maps = call(
        functools.partial(state_body, rank),
        (
            shape((in_row, states, lanes), BF16),
            by_token,
            by_token,
            shape((2 * states, row_count), F32),
        ),
        [VMEM] * 6,
        (lows, act, dtw, rate, rows, first),
    )
    in_row_ends = lax.all_to_all(send, "x", 0, 0, tiled=True)
    send, before, before_length = call(
        row_body,
        (
            shape((rows_of, states, lanes), BF16),
            shape((states, channels), F32),
            shape((8, channels), F32),
        ),
        [SMEM, VMEM, VMEM],
        (lax.axis_index("x").astype(jnp.int32).reshape(1), in_row_ends, rate),
    )
    out, share = call(
        functools.partial(side_body, features),
        (by_token, shape((states, row_count, channels), BF16)),
        [VMEM, HBM] + [VMEM] * 7,
        (gathered, weight, act, rate, rows, decay_step, drive_step, maps, before_length),
        [
            pltpu.VMEM((width, row_count), BF16),
            pltpu.VMEM((channels, width), BF16),
            pltpu.VMEM((8 * states, channels), BF16),
            pltpu.VMEM((row_count, channels), F32),
            pltpu.SemaphoreType.DMA,
        ],
    )
    ends = lax.all_to_all(send, "z", 0, 0, tiled=True)
    my_row = lax.axis_index("z").astype(jnp.int32).reshape(1)
    mixed = call(
        finish_body,
        shape((channels, row_count), BF16),
        [SMEM] + [VMEM] * 6,
        (my_row, ends, rate, before, before_length, out, share),
    )
    return mixed.T


def solution(mesh):
    peers, chans = mesh.devices.shape
    in_row = 4 if peers % 4 == 0 else 1
    grid = mesh.devices.reshape(peers // in_row, in_row, chans)
    mesh = jax.sharding.Mesh(grid, ("z", "x", "chan"))
    return jax.shard_map(
        local,
        mesh=mesh,
        in_specs=(
            P(("z", "x"), "chan"),
            P(),
            P(None, None, "chan"),
            P(None, "chan"),
            P("chan"),
            P("chan", None),
            P(None, "chan"),
            P("chan"),
            P("chan", None),
            P("chan"),
            P(("z", "x")),
            P(("z", "x")),
        ),
        out_specs=P(("z", "x"), "chan"),
        check_vma=False,
    )
```

```python
import functools
import math

import jax
import jax.numpy as jnp
from jax import lax
from jax.experimental import pallas as pl
from jax.experimental.pallas import tpu as pltpu
from jax.sharding import PartitionSpec as P

EPSILON = 1e-05
LOG2E = math.log2(math.e)
FAR = 1e30
F32 = jnp.float32
BF16 = jnp.bfloat16

VMEM = pl.BlockSpec(memory_space=pltpu.VMEM)
SMEM = pl.BlockSpec(memory_space=pltpu.SMEM)
HBM = pl.BlockSpec(memory_space=pltpu.HBM)

NN = (((1,), (0,)), ((), ()))
NT = (((1,), (1,)), ((), ()))
TN = (((0,), (0,)), ((), ()))


def dot(a, b, dims=NN):
    return lax.dot_general(a, b, dims, preferred_element_type=F32)


def in_hbm(value):
    return pltpu.with_memory_space_constraint(value, pltpu.HBM)


def iota(shape, dim):
    return lax.broadcasted_iota(jnp.int32, shape, dim)


def call(body, outs, specs, args, scratch=(), limit=24):
    return pl.pallas_call(
        body,
        out_shape=outs,
        in_specs=specs,
        out_specs=jax.tree.map(lambda _: VMEM, outs),
        scratch_shapes=list(scratch),
        compiler_params=pltpu.CompilerParams(vmem_limit_bytes=limit << 20),
    )(*args)


def swap_blocks(slabs):
    lanes = 128
    block = iota((16, lanes), 1) >> 3
    slabs = list(slabs) + [None] * (16 - len(slabs))
    for step in (8, 4, 2, 1):
        keep = (block & step) == 0
        for low in range(16):
            if low & step:
                continue
            a, b = slabs[low], slabs[low | step]
            if a is None and b is None:
                continue
            zero = jnp.zeros((16, lanes), F32)
            up = zero if b is None else pltpu.roll(b, 8 * step, 1)
            down = zero if a is None else pltpu.roll(a, lanes - 8 * step, 1)
            slabs[low] = jnp.where(keep, zero if a is None else a, up)
            slabs[low | step] = jnp.where(keep, down, zero if b is None else b)
    return slabs


def pack_body(slots, me, target_hbm, tok_hbm, starts_hbm, out_ref, starts_ref, target, tok_ref, pieces, sems):
    copies = [
        pltpu.make_async_copy(target_hbm, target, sems.at[0]),
        pltpu.make_async_copy(starts_hbm, starts_ref, sems.at[1]),
        pltpu.make_async_copy(tok_hbm, tok_ref, sems.at[2]),
    ]
    for copy in copies:
        copy.start()
    features, tokens = tok_ref.shape
    peers = out_ref.shape[0]
    parts = features // 16
    pieces[...] = jnp.zeros(pieces.shape, F32)
    lane = iota((16, tokens), 1)
    source = iota((tokens, tokens), 0)
    place = iota((tokens, tokens), 1)
    late = (source < features // 2) & ((source & 7) >= 5)
    to_tail = jnp.where(
        late & (place == features // 2 + 3 * (source >> 3) + (source & 7) - 5), 1.0, 0.0
    ).astype(BF16)
    copies[2].wait()
    groups = swap_blocks(
        [tok_ref[16 * piece : 16 * piece + 16, :].astype(F32) for piece in range(parts)]
    )
    tails = dot(jnp.concatenate(groups, axis=0).astype(BF16), to_tail)
    copies[0].wait()
    copies[1].wait()
    fresh = 1.0 - jnp.broadcast_to(starts_ref[...].astype(F32), (16, tokens))
    one = pltpu.roll(fresh, (114 - (tokens - 1)) % tokens, 1)
    two = pltpu.roll(fresh, (113 - (tokens - 1)) % tokens, 1)
    flags = jnp.where(
        lane == 115, 1.0, jnp.where(lane == 114, one, jnp.where(lane == 113, one * two, 0.0))
    )
    for group in range(slots):
        where_to = target[group]
        dev = lax.shift_right_logical(where_to, slots.bit_length() - 1)
        slot = where_to & (slots - 1)
        pieces[dev] = jnp.where(lane == 112, (slot + 1).astype(F32), groups[group])
        follows = (slot == slots - 1) & (dev + 1 < peers)
        pieces[jnp.where(follows, peers + dev + 1, 2 * peers)] = tails[16 * group : 16 * group + 16]
    after = me[0] + 1
    for peer in range(peers):
        whole = pieces[peer] + pieces[peers + peer] + jnp.where(after == peer, flags, 0.0)
        out_ref[peer] = whole.astype(BF16)


def fetch_body(
    weight_hbm, proj_hbm, dtw_hbm, rate_hbm, taps_hbm, conv_bias_hbm, dt_bias_hbm, skip_hbm, starts_ref,
    weight_ref, proj_ref, dtw_ref, rate_ref, cols_ref, rows_ref, first_ref,
    taps_in, conv_bias, dt_bias, skip, sems,
):
    taps, channels = taps_in.shape
    pairs = (
        (taps_hbm, taps_in),
        (conv_bias_hbm, conv_bias),
        (dt_bias_hbm, dt_bias),
        (skip_hbm, skip),
        (weight_hbm.at[0:channels], weight_ref),
        (proj_hbm, proj_ref),
        (dtw_hbm, dtw_ref),
        (rate_hbm, rate_ref),
    )
    copies = [
        pltpu.make_async_copy(source, target, sems.at[index])
        for index, (source, target) in enumerate(pairs)
    ]
    for copy in copies:
        copy.start()
    for copy in copies[:4]:
        copy.wait()
    bias = conv_bias[...].reshape(1, channels)
    blank = jnp.zeros((8 - taps - 1, channels), F32)
    cols_ref[...] = jnp.transpose(jnp.concatenate([taps_in[...], bias, blank], axis=0))
    tokens = starts_ref.shape[1]
    first = jnp.transpose(jnp.broadcast_to(starts_ref[...].astype(F32), (tokens, tokens)))
    first_ref[...] = jnp.broadcast_to(first[:, :1], first_ref.shape)
    rows_ref[0:1, :] = dt_bias[...].reshape(1, channels)
    rows_ref[1:2, :] = skip[...].reshape(1, channels)
    for copy in copies[4:]:
        copy.wait()


def place_body(in_ref, gain_ref, out_ref):
    peers, _, tokens = in_ref.shape
    features = gain_ref.shape[0]
    rows = 16 * peers
    slots = tokens // 8
    parts = features // 16
    arrived = in_ref[...].reshape(rows, tokens)
    spot = jnp.where(iota((16, tokens), 1) == 112, 1.0, 0.0).astype(BF16)
    label = dot(spot, arrived, NT)[:1]
    key = label * 16.0 + (iota((1, rows), 1) & 15).astype(F32)
    want = (iota((16 * slots, rows), 0) + 16).astype(F32)
    pick = jnp.where(key == want, 1.0, 0.0).astype(BF16)
    ordered = dot(pick, arrived)
    total = jnp.sum(in_ref[...].astype(F32), axis=0)
    lane = iota((16, tokens), 1)
    open_tail = jnp.where(lane >= tokens - 3, pltpu.roll(total, tokens - 3 - 113, 1), 0.0)
    mains = swap_blocks([ordered[16 * slot : 16 * slot + 16] for slot in range(slots)])[:parts]
    tails = []
    for piece in range(parts):
        shift = (tokens - 3 - features // 2 - 3 * piece) % tokens
        tails.append((total if shift == 0 else pltpu.roll(total, shift, 1)) * open_tail)
    x_main = jnp.concatenate(mains, axis=0)
    x_tail = jnp.concatenate(tails, axis=0)
    gain = gain_ref[...]
    main_sq = jnp.sum(x_main * x_main, axis=0, keepdims=True)
    tail_sq = jnp.sum(x_tail * x_tail, axis=0, keepdims=True)
    out_ref[0:features, :] = (x_main * gain).astype(BF16)
    x_tail = x_tail * gain
    packed = jnp.zeros((16, tokens), F32)
    for part in range(features // 16):
        shift = (8 * part - (tokens - 8)) % tokens
        packed = packed + pltpu.roll(x_tail[16 * part : 16 * part + 16], shift, 1)
    line = iota((16, tokens), 0)
    first_lane = features // 2
    spare = (lane >= first_lane) & (lane < first_lane + 32)
    main_high = main_sq.astype(BF16).astype(F32)
    tail_high = tail_sq.astype(BF16).astype(F32)
    rows = [(main_high, part) for part in range(4)] + [(main_sq - main_high, part) for part in range(4)]
    rows += [(tail_high, 3), (tail_sq - tail_high, 3)]
    for index, (value, part) in enumerate(rows):
        moved = pltpu.roll(jnp.broadcast_to(value, (16, tokens)), (first_lane - 32 * part) % tokens, 1)
        packed = jnp.where(spare & (line == index), moved, packed)
    out_ref[features : features + 16, :] = packed.astype(BF16)


def square_sums(total, features):
    tokens = total.shape[1]
    first_lane = features // 2
    lane = iota((8, tokens), 1)
    main = jnp.zeros((8, tokens), F32)
    for part in range(4):
        row = jnp.broadcast_to(total[part : part + 1] + total[part + 4 : part + 5], (8, tokens))
        moved = pltpu.roll(row, (32 * part - first_lane) % tokens, 1)
        main = jnp.where((lane >> 5) == part, moved, main)
    row = jnp.broadcast_to(total[8:9] + total[9:10], (8, tokens))
    tail = pltpu.roll(row, (96 - first_lane) % tokens, 1)
    return main[:1], jnp.where(lane >= 96, tail, 0.0)[:1]


def project_body(
    features, taps, in_ref, weight_ref, taps_ref, proj_ref, starts_ref, low_ref, act_ref, wide,
):
    count = in_ref.shape[0]
    tokens = in_ref.shape[2]
    channels = act_ref.shape[0]
    width = count * features
    sums = jnp.zeros((16, tokens), F32)
    for peer in range(count):
        base = peer * features
        wide[base : base + features, 0:tokens] = in_ref[peer, 0:features, :]
        packed = in_ref[peer, features : features + 16, :].astype(F32)
        sums = sums + packed
        for part in range(features // 16):
            shift = (tokens - 8 - 8 * part) % tokens
            moved = packed if shift == 0 else pltpu.roll(packed, shift, 1)
            wide[base + 16 * part : base + 16 * part + 16, tokens:] = moved.astype(BF16)
    main_sq, tail_sq = square_sums(sums, features)
    scale_main = lax.rsqrt(main_sq / width + EPSILON)
    scale_tail = lax.rsqrt(tail_sq / width + EPSILON)
    both = dot(weight_ref[...], wide[...])
    x_in = (both[:, :tokens] * scale_main).astype(BF16).astype(F32)
    tail = (both[:, tokens:] * scale_tail).astype(BF16).astype(F32)
    fresh = 1.0 - jnp.broadcast_to(starts_ref[...].astype(F32), (8, tokens))
    lane8 = iota((8, tokens), 1)
    lane = iota((channels, tokens), 1)
    convolved = taps_ref[:, taps : taps + 1] + taps_ref[:, taps - 1 : taps] * x_in
    mask = fresh
    for back in range(1, taps):
        if back > 1:
            mask = mask * jnp.where(lane8 < back - 1, 1.0, pltpu.roll(fresh, back - 1, 1))
        behind = pltpu.roll(jnp.where(lane >= tokens - back, tail, x_in), back, 1)
        tap = taps_ref[:, taps - 1 - back : taps - back]
        convolved = convolved + jnp.where(mask[:1] > 0.5, tap * behind, 0.0)
    act = (convolved * (1.0 / (1.0 + jnp.exp(-convolved)))).astype(BF16)
    act_ref[...] = act
    low_ref[...] = dot(proj_ref[...], act).astype(BF16)


def join(state, length, lanes):
    states, channels = state.shape
    spare = lanes - channels
    pieces = channels // spare
    length_high = length.astype(BF16).astype(F32)
    line = iota((states, spare), 0)
    ends = jnp.zeros((states, spare), F32)
    for piece in range(pieces):
        high = length_high[:, piece * spare : piece * spare + spare]
        rest = length[:, piece * spare : piece * spare + spare] - high
        ends = jnp.where(line == piece, high, ends)
        ends = jnp.where(line == piece + pieces, rest, ends)
    return jnp.concatenate([state, ends], axis=1).astype(BF16)


def part(message, channels):
    message = message.astype(F32)
    pieces = channels // (message.shape[1] - channels)
    ends = message[:pieces, channels:] + message[pieces : 2 * pieces, channels:]
    length = jnp.concatenate([ends[piece : piece + 1] for piece in range(pieces)], axis=1)
    return message[:, :channels], length


def state_body(
    rank, in_ref, act_ref, dtw_ref, rate_ref, rows_ref, first_ref,
    send_ref, decay_step, drive_step, maps_ref,
):
    tokens = in_ref.shape[2]
    states, channels = rate_ref.shape
    low = in_ref[0].astype(F32)
    for peer in range(1, in_ref.shape[0]):
        low = low + in_ref[peer].astype(F32)
    dt_low = low[:rank].astype(BF16)
    in_map = low[rank : rank + states]
    maps_ref[...] = low[rank:]
    raw = dot(dt_low, dtw_ref[...], TN) + rows_ref[0:1, :]
    small = jnp.exp(-jnp.abs(raw))
    series = small * (1.0 - small * (0.5 - small * (1.0 / 3.0 - small * 0.25)))
    step = jnp.maximum(raw, 0.0) + jnp.where(small < 0.01, series, jnp.log(1.0 + small))
    drive_step[...] = step * jnp.transpose(act_ref[...].astype(F32))
    step = jnp.where(first_ref[...] > 0.5, FAR, step)
    decay_step[...] = step
    last = jnp.sum(step, axis=0, keepdims=True)
    rate = rate_ref[...] * (-LOG2E)
    stretches = 4
    length = tokens // stretches
    parts = [jnp.zeros((states, channels), F32)] * stretches
    for offset in range(length):
        for index in range(stretches):
            t = index * length + offset
            decay = jnp.exp2(decay_step[t : t + 1, :] * rate)
            parts[index] = decay * parts[index] + drive_step[t : t + 1, :] * in_map[:, t : t + 1]
    state = parts[0]
    for index in range(1, stretches):
        spent = jnp.sum(step[index * length : (index + 1) * length], axis=0, keepdims=True)
        state = jnp.exp2(spent * rate) * state + parts[index]
    message = join(state, last, send_ref.shape[2])
    for peer in range(send_ref.shape[0]):
        send_ref[peer] = message


def row_body(me, in_ref, rate_ref, send_ref, before_ref, length_ref):
    states, channels = rate_ref.shape
    rate = rate_ref[...] * (-LOG2E)
    whole = jnp.zeros((states, channels), F32)
    before = whole
    whole_length = jnp.zeros((1, channels), F32)
    before_length = whole_length
    for peer in range(in_ref.shape[0]):
        final, length = part(in_ref[peer], channels)
        earlier = peer < me[0]
        through = jnp.exp2(length * rate)
        whole = through * whole + final
        before = jnp.where(earlier, whole, before)
        whole_length = whole_length + length
        before_length = jnp.where(earlier, whole_length, before_length)
    message = join(whole, whole_length, send_ref.shape[2])
    for peer in range(send_ref.shape[0]):
        send_ref[peer] = message
    before_ref[...] = before
    length_ref[...] = jnp.broadcast_to(before_length, length_ref.shape)


def side_body(
    features, in_ref, weight_hbm, act_ref, rate_ref, rows_ref, decay_step, drive_step, maps_ref, row_ref,
    out_ref, share_ref, wide, gate_weight, hidden, gate_token, sem,
):
    count = in_ref.shape[0]
    tokens = in_ref.shape[2]
    states, channels = rate_ref.shape
    fetch = pltpu.make_async_copy(weight_hbm.at[channels:], gate_weight, sem)
    fetch.start()
    sums = jnp.zeros((16, tokens), F32)
    for peer in range(count):
        wide[peer * features : (peer + 1) * features, :] = in_ref[peer, 0:features, :]
        sums = sums + in_ref[peer, features : features + 16, :].astype(F32)
    scale = lax.rsqrt(square_sums(sums, features)[0] / (count * features) + EPSILON)
    in_map = maps_ref[0:states, :]
    out_map = maps_ref[states:, :]
    step = decay_step[...]
    high = step.astype(BF16)
    rest = (step - high.astype(F32)).astype(BF16)
    lower = jnp.where(iota((tokens, tokens), 0) >= iota((tokens, tokens), 1), 1.0, 0.0).astype(BF16)
    elapsed = dot(lower, high) + dot(lower, rest)
    spread = jnp.where((iota((states, tokens), 1) & (states - 1)) == iota((states, tokens), 0), 1.0, 0.0)
    maps = dot(out_map.astype(BF16), spread.astype(BF16), TN)
    own = (iota((tokens, tokens), 1) // states) == (iota((tokens, tokens), 0) & 7)
    maps = jnp.where(own, maps, 0.0).astype(BF16)
    out_ref[...] = rows_ref[1:2, :] * jnp.transpose(act_ref[...].astype(F32))
    fetch.wait()
    gate = dot(gate_weight[...], wide[...])
    gate = (gate * scale).astype(BF16).astype(F32)
    gate_token[...] = jnp.transpose(gate * (1.0 / (1.0 + jnp.exp(-gate))))
    rate = rate_ref[...] * (-LOG2E)
    by_token = jnp.transpose(out_map)
    for index in range(states):
        remains = jnp.exp2(elapsed * rate[index : index + 1, :]) * gate_token[...]
        share_ref[index] = (by_token[:, index : index + 1] * remains).astype(BF16)
    state = jnp.zeros((states, channels), F32)
    for block in range(tokens // 8):
        for inner in range(8):
            t = block * 8 + inner
            decay = jnp.exp2(decay_step[t : t + 1, :] * rate)
            state = decay * state + drive_step[t : t + 1, :] * in_map[:, t : t + 1]
            hidden[inner * states : (inner + 1) * states, :] = state.astype(BF16)
        out_ref[block * 8 : block * 8 + 8, :] += dot(maps[block * 8 : block * 8 + 8], hidden[...])
    out_ref[...] *= gate_token[...]


def finish_body(me, in_ref, rate_ref, before_ref, length_ref, out_in_ref, share_ref, mixed_ref):
    states, channels = rate_ref.shape
    rate = rate_ref[...] * (-LOG2E)
    state = jnp.zeros((states, channels), F32)
    for peer in range(in_ref.shape[0]):
        final, length = part(in_ref[peer], channels)
        earlier = peer < me[0]
        through = jnp.where(earlier, jnp.exp2(length * rate), 1.0)
        state = through * state + jnp.where(earlier, final, 0.0)
    state = jnp.exp2(length_ref[0:1, :] * rate) * state + before_ref[...]
    scanned = out_in_ref[...]
    for index in range(states):
        scanned = scanned + share_ref[index].astype(F32) * state[index : index + 1, :]
    mixed_ref[...] = jnp.transpose(scanned).astype(BF16)


def local(
    tokens, norm_gain, in_weight, conv_weight, conv_bias, proj_weight, dt_weight, dt_bias,
    decay_rate, skip_gain, doc_starts, group_target,
):
    rows_of, in_row = lax.axis_size("z"), lax.axis_size("x")
    peers = rows_of * in_row
    row_count, features = tokens.shape
    slots = group_target.shape[0]
    width = in_weight.shape[0]
    channels = in_weight.shape[2]
    rank = dt_weight.shape[0]
    states = decay_rate.shape[1]
    shape = jax.ShapeDtypeStruct
    me = lax.axis_index(("z", "x")).astype(jnp.int32).reshape(1)
    starts = doc_starts.reshape(1, row_count)
    my_gain = lax.dynamic_slice_in_dim(norm_gain, lax.axis_index("chan") * features, features)
    my_gain = jnp.broadcast_to(my_gain[:, None], (features, row_count))
    weight = jnp.transpose(in_weight, (1, 2, 0)).reshape(2 * channels, width)
    pieces, starts = call(
        functools.partial(pack_body, slots),
        (shape((peers, 16, row_count), BF16), shape((1, row_count), jnp.int32)),
        [SMEM, HBM, HBM, HBM],
        (me, in_hbm(group_target), in_hbm(tokens.T), in_hbm(starts)),
        [
            pltpu.SMEM((slots,), jnp.int32),
            pltpu.VMEM((features, row_count), BF16),
            pltpu.VMEM((2 * peers + 1, 16, row_count), F32),
            pltpu.SemaphoreType.DMA((3,)),
        ],
    )
    weight = in_hbm(weight)
    sources = (proj_weight.T, dt_weight, decay_rate.T, conv_weight, conv_bias, dt_bias, skip_gain)
    scan_weight, proj, dtw, rate, cols, rows, first = call(
        fetch_body,
        (
            shape((channels, width), BF16),
            shape((rank + 2 * states, channels), BF16),
            shape((rank, channels), BF16),
            shape((states, channels), F32),
            shape((channels, 8), F32),
            shape((8, channels), F32),
            shape((row_count, channels), F32),
        ),
        [HBM] * 8 + [VMEM],
        (weight, *(in_hbm(source) for source in sources), starts),
        [
            pltpu.VMEM(conv_weight.shape, F32),
            pltpu.VMEM((channels,), F32),
            pltpu.VMEM((channels,), F32),
            pltpu.VMEM((channels,), F32),
            pltpu.SemaphoreType.DMA((8,)),
        ],
    )
    arrived = lax.all_to_all(pieces, ("z", "x"), 0, 0, tiled=True)
    payload = call(
        place_body,
        shape((features + 16, row_count), BF16),
        [VMEM, VMEM],
        (arrived, my_gain),
    )
    gathered = lax.all_gather(payload, "chan", axis=0)
    low, act = call(
        functools.partial(project_body, features, conv_weight.shape[0]),
        (shape((rank + 2 * states, row_count), BF16), shape((channels, row_count), BF16)),
        [VMEM] * 5,
        (gathered, scan_weight, cols, proj, starts),
        [pltpu.VMEM((width, 2 * row_count), BF16)],
    )
    lows = lax.all_gather(low, "chan", axis=0)
    lanes = -(-channels // 128) * 128
    by_token = shape((row_count, channels), F32)
    send, decay_step, drive_step, maps = call(
        functools.partial(state_body, rank),
        (
            shape((in_row, states, lanes), BF16),
            by_token,
            by_token,
            shape((2 * states, row_count), F32),
        ),
        [VMEM] * 6,
        (lows, act, dtw, rate, rows, first),
    )
    in_row_ends = lax.all_to_all(send, "x", 0, 0, tiled=True)
    send, before, before_length = call(
        row_body,
        (
            shape((rows_of, states, lanes), BF16),
            shape((states, channels), F32),
            shape((8, channels), F32),
        ),
        [SMEM, VMEM, VMEM],
        (lax.axis_index("x").astype(jnp.int32).reshape(1), in_row_ends, rate),
    )
    out, share = call(
        functools.partial(side_body, features),
        (by_token, shape((states, row_count, channels), BF16)),
        [VMEM, HBM] + [VMEM] * 7,
        (gathered, weight, act, rate, rows, decay_step, drive_step, maps, before_length),
        [
            pltpu.VMEM((width, row_count), BF16),
            pltpu.VMEM((channels, width), BF16),
            pltpu.VMEM((8 * states, channels), BF16),
            pltpu.VMEM((row_count, channels), F32),
            pltpu.SemaphoreType.DMA,
        ],
    )
    ends = lax.all_to_all(send, "z", 0, 0, tiled=True)
    my_row = lax.axis_index("z").astype(jnp.int32).reshape(1)
    mixed = call(
        finish_body,
        shape((channels, row_count), BF16),
        [SMEM] + [VMEM] * 6,
        (my_row, ends, rate, before, before_length, out, share),
    )
    return mixed.T


def solution(mesh):
    peers, chans = mesh.devices.shape
    in_row = 4 if peers % 4 == 0 else 1
    grid = mesh.devices.reshape(peers // in_row, in_row, chans)
    mesh = jax.sharding.Mesh(grid, ("z", "x", "chan"))
    return jax.shard_map(
        local,
        mesh=mesh,
        in_specs=(
            P(("z", "x"), "chan"),
            P(),
            P(None, None, "chan"),
            P(None, "chan"),
            P("chan"),
            P("chan", None),
            P(None, "chan"),
            P("chan"),
            P("chan", None),
            P("chan"),
            P(("z", "x")),
            P(("z", "x")),
        ),
        out_specs=P(("z", "x"), "chan"),
        check_vma=False,
    )
```

```python
import functools
import math

import jax
import jax.numpy as jnp
from jax import lax
from jax.experimental import pallas as pl
from jax.experimental.pallas import tpu as pltpu
from jax.sharding import PartitionSpec as P

EPSILON = 1e-05
LOG2E = math.log2(math.e)
FAR = 1e30
F32 = jnp.float32
BF16 = jnp.bfloat16

VMEM = pl.BlockSpec(memory_space=pltpu.VMEM)
SMEM = pl.BlockSpec(memory_space=pltpu.SMEM)
HBM = pl.BlockSpec(memory_space=pltpu.HBM)

NN = (((1,), (0,)), ((), ()))
NT = (((1,), (1,)), ((), ()))
TN = (((0,), (0,)), ((), ()))


def dot(a, b, dims=NN):
    return lax.dot_general(a, b, dims, preferred_element_type=F32)


def in_hbm(value):
    return pltpu.with_memory_space_constraint(value, pltpu.HBM)


def iota(shape, dim):
    return lax.broadcasted_iota(jnp.int32, shape, dim)


def call(body, outs, specs, args, scratch=(), limit=24):
    return pl.pallas_call(
        body,
        out_shape=outs,
        in_specs=specs,
        out_specs=jax.tree.map(lambda _: VMEM, outs),
        scratch_shapes=list(scratch),
        compiler_params=pltpu.CompilerParams(vmem_limit_bytes=limit << 20),
    )(*args)


def swap_blocks(slabs):
    lanes = 128
    block = iota((16, lanes), 1) >> 3
    slabs = list(slabs) + [None] * (16 - len(slabs))
    for step in (8, 4, 2, 1):
        keep = (block & step) == 0
        for low in range(16):
            if low & step:
                continue
            a, b = slabs[low], slabs[low | step]
            if a is None and b is None:
                continue
            zero = jnp.zeros((16, lanes), F32)
            up = zero if b is None else pltpu.roll(b, 8 * step, 1)
            down = zero if a is None else pltpu.roll(a, lanes - 8 * step, 1)
            slabs[low] = jnp.where(keep, zero if a is None else a, up)
            slabs[low | step] = jnp.where(keep, down, zero if b is None else b)
    return slabs


def pack_body(slots, me, target_hbm, tok_hbm, starts_hbm, out_ref, starts_ref, target, tok_ref, pieces, sems):
    copies = [
        pltpu.make_async_copy(target_hbm, target, sems.at[0]),
        pltpu.make_async_copy(starts_hbm, starts_ref, sems.at[1]),
        pltpu.make_async_copy(tok_hbm, tok_ref, sems.at[2]),
    ]
    for copy in copies:
        copy.start()
    features, tokens = tok_ref.shape
    peers = out_ref.shape[0]
    parts = features // 16
    pieces[...] = jnp.zeros(pieces.shape, F32)
    lane = iota((16, tokens), 1)
    source = iota((tokens, tokens), 0)
    place = iota((tokens, tokens), 1)
    late = (source < features // 2) & ((source & 7) >= 5)
    to_tail = jnp.where(
        late & (place == features // 2 + 3 * (source >> 3) + (source & 7) - 5), 1.0, 0.0
    ).astype(BF16)
    copies[2].wait()
    groups = swap_blocks(
        [tok_ref[16 * piece : 16 * piece + 16, :].astype(F32) for piece in range(parts)]
    )
    tails = dot(jnp.concatenate(groups, axis=0).astype(BF16), to_tail)
    copies[0].wait()
    copies[1].wait()
    fresh = 1.0 - jnp.broadcast_to(starts_ref[...].astype(F32), (16, tokens))
    one = pltpu.roll(fresh, (114 - (tokens - 1)) % tokens, 1)
    two = pltpu.roll(fresh, (113 - (tokens - 1)) % tokens, 1)
    flags = jnp.where(
        lane == 115, 1.0, jnp.where(lane == 114, one, jnp.where(lane == 113, one * two, 0.0))
    )
    for group in range(slots):
        where_to = target[group]
        dev = lax.shift_right_logical(where_to, slots.bit_length() - 1)
        slot = where_to & (slots - 1)
        pieces[dev] = jnp.where(lane == 112, (slot + 1).astype(F32), groups[group])
        follows = (slot == slots - 1) & (dev + 1 < peers)
        pieces[jnp.where(follows, peers + dev + 1, 2 * peers)] = tails[16 * group : 16 * group + 16]
    after = me[0] + 1
    for peer in range(peers):
        whole = pieces[peer] + pieces[peers + peer] + jnp.where(after == peer, flags, 0.0)
        out_ref[peer] = whole.astype(BF16)


def fetch_body(
    weight_hbm, proj_hbm, dtw_hbm, rate_hbm, taps_hbm, conv_bias_hbm, dt_bias_hbm, skip_hbm, starts_ref,
    weight_ref, proj_ref, dtw_ref, rate_ref, cols_ref, rows_ref, first_ref,
    taps_in, conv_bias, dt_bias, skip, sems,
):
    taps, channels = taps_in.shape
    pairs = (
        (taps_hbm, taps_in),
        (conv_bias_hbm, conv_bias),
        (dt_bias_hbm, dt_bias),
        (skip_hbm, skip),
        (weight_hbm.at[0:channels], weight_ref),
        (proj_hbm, proj_ref),
        (dtw_hbm, dtw_ref),
        (rate_hbm, rate_ref),
    )
    copies = [
        pltpu.make_async_copy(source, target, sems.at[index])
        for index, (source, target) in enumerate(pairs)
    ]
    for copy in copies:
        copy.start()
    for copy in copies[:4]:
        copy.wait()
    bias = conv_bias[...].reshape(1, channels)
    blank = jnp.zeros((8 - taps - 1, channels), F32)
    cols_ref[...] = jnp.transpose(jnp.concatenate([taps_in[...], bias, blank], axis=0))
    tokens = starts_ref.shape[1]
    first = jnp.transpose(jnp.broadcast_to(starts_ref[...].astype(F32), (tokens, tokens)))
    first_ref[...] = jnp.broadcast_to(first[:, :1], first_ref.shape)
    rows_ref[0:1, :] = dt_bias[...].reshape(1, channels)
    rows_ref[1:2, :] = skip[...].reshape(1, channels)
    for copy in copies[4:]:
        copy.wait()


def place_body(in_ref, gain_ref, out_ref):
    peers, _, tokens = in_ref.shape
    features = gain_ref.shape[0]
    rows = 16 * peers
    slots = tokens // 8
    parts = features // 16
    arrived = in_ref[...].reshape(rows, tokens)
    spot = jnp.where(iota((16, tokens), 1) == 112, 1.0, 0.0).astype(BF16)
    label = dot(spot, arrived, NT)[:1]
    key = label * 16.0 + (iota((1, rows), 1) & 15).astype(F32)
    want = (iota((16 * slots, rows), 0) + 16).astype(F32)
    pick = jnp.where(key == want, 1.0, 0.0).astype(BF16)
    ordered = dot(pick, arrived)
    total = jnp.sum(in_ref[...].astype(F32), axis=0)
    lane = iota((16, tokens), 1)
    open_tail = jnp.where(lane >= tokens - 3, pltpu.roll(total, tokens - 3 - 113, 1), 0.0)
    mains = swap_blocks([ordered[16 * slot : 16 * slot + 16] for slot in range(slots)])[:parts]
    tails = []
    for piece in range(parts):
        shift = (tokens - 3 - features // 2 - 3 * piece) % tokens
        tails.append((total if shift == 0 else pltpu.roll(total, shift, 1)) * open_tail)
    x_main = jnp.concatenate(mains, axis=0)
    x_tail = jnp.concatenate(tails, axis=0)
    gain = gain_ref[...]
    main_sq = jnp.sum(x_main * x_main, axis=0, keepdims=True)
    tail_sq = jnp.sum(x_tail * x_tail, axis=0, keepdims=True)
    out_ref[0:features, :] = (x_main * gain).astype(BF16)
    x_tail = x_tail * gain
    packed = jnp.zeros((16, tokens), F32)
    for part in range(features // 16):
        shift = (8 * part - (tokens - 8)) % tokens
        packed = packed + pltpu.roll(x_tail[16 * part : 16 * part + 16], shift, 1)
    line = iota((16, tokens), 0)
    first_lane = features // 2
    spare = (lane >= first_lane) & (lane < first_lane + 32)
    main_high = main_sq.astype(BF16).astype(F32)
    tail_high = tail_sq.astype(BF16).astype(F32)
    rows = [(main_high, part) for part in range(4)] + [(main_sq - main_high, part) for part in range(4)]
    rows += [(tail_high, 3), (tail_sq - tail_high, 3)]
    for index, (value, part) in enumerate(rows):
        moved = pltpu.roll(jnp.broadcast_to(value, (16, tokens)), (first_lane - 32 * part) % tokens, 1)
        packed = jnp.where(spare & (line == index), moved, packed)
    out_ref[features : features + 16, :] = packed.astype(BF16)


def square_sums(total, features):
    tokens = total.shape[1]
    first_lane = features // 2
    lane = iota((8, tokens), 1)
    main = jnp.zeros((8, tokens), F32)
    for part in range(4):
        row = jnp.broadcast_to(total[part : part + 1] + total[part + 4 : part + 5], (8, tokens))
        moved = pltpu.roll(row, (32 * part - first_lane) % tokens, 1)
        main = jnp.where((lane >> 5) == part, moved, main)
    row = jnp.broadcast_to(total[8:9] + total[9:10], (8, tokens))
    tail = pltpu.roll(row, (96 - first_lane) % tokens, 1)
    return main[:1], jnp.where(lane >= 96, tail, 0.0)[:1]


def project_body(
    features, taps, in_ref, weight_ref, taps_ref, proj_ref, starts_ref, low_ref, act_ref, wide,
):
    count = in_ref.shape[0]
    tokens = in_ref.shape[2]
    channels = act_ref.shape[0]
    width = count * features
    sums = jnp.zeros((16, tokens), F32)
    for peer in range(count):
        base = peer * features
        wide[base : base + features, 0:tokens] = in_ref[peer, 0:features, :]
        packed = in_ref[peer, features : features + 16, :].astype(F32)
        sums = sums + packed
        for part in range(features // 16):
            shift = (tokens - 8 - 8 * part) % tokens
            moved = packed if shift == 0 else pltpu.roll(packed, shift, 1)
            wide[base + 16 * part : base + 16 * part + 16, tokens:] = moved.astype(BF16)
    main_sq, tail_sq = square_sums(sums, features)
    scale_main = lax.rsqrt(main_sq / width + EPSILON)
    scale_tail = lax.rsqrt(tail_sq / width + EPSILON)
    both = dot(weight_ref[...], wide[...])
    x_in = (both[:, :tokens] * scale_main).astype(BF16).astype(F32)
    tail = (both[:, tokens:] * scale_tail).astype(BF16).astype(F32)
    fresh = 1.0 - jnp.broadcast_to(starts_ref[...].astype(F32), (8, tokens))
    lane8 = iota((8, tokens), 1)
    lane = iota((channels, tokens), 1)
    convolved = taps_ref[:, taps : taps + 1] + taps_ref[:, taps - 1 : taps] * x_in
    mask = fresh
    for back in range(1, taps):
        if back > 1:
            mask = mask * jnp.where(lane8 < back - 1, 1.0, pltpu.roll(fresh, back - 1, 1))
        behind = pltpu.roll(jnp.where(lane >= tokens - back, tail, x_in), back, 1)
        tap = taps_ref[:, taps - 1 - back : taps - back]
        convolved = convolved + jnp.where(mask[:1] > 0.5, tap * behind, 0.0)
    act = (convolved * (1.0 / (1.0 + jnp.exp(-convolved)))).astype(BF16)
    act_ref[...] = act
    low_ref[...] = dot(proj_ref[...], act).astype(BF16)


def join(state, length, lanes):
    states, channels = state.shape
    spare = lanes - channels
    pieces = channels // spare
    length_high = length.astype(BF16).astype(F32)
    line = iota((states, spare), 0)
    ends = jnp.zeros((states, spare), F32)
    for piece in range(pieces):
        high = length_high[:, piece * spare : piece * spare + spare]
        rest = length[:, piece * spare : piece * spare + spare] - high
        ends = jnp.where(line == piece, high, ends)
        ends = jnp.where(line == piece + pieces, rest, ends)
    return jnp.concatenate([state, ends], axis=1).astype(BF16)


def part(message, channels):
    message = message.astype(F32)
    pieces = channels // (message.shape[1] - channels)
    ends = message[:pieces, channels:] + message[pieces : 2 * pieces, channels:]
    length = jnp.concatenate([ends[piece : piece + 1] for piece in range(pieces)], axis=1)
    return message[:, :channels], length


def state_body(
    rank, in_ref, act_ref, dtw_ref, rate_ref, rows_ref, first_ref,
    send_ref, decay_step, drive_step, maps_ref,
):
    tokens = in_ref.shape[2]
    states, channels = rate_ref.shape
    low = in_ref[0].astype(F32)
    for peer in range(1, in_ref.shape[0]):
        low = low + in_ref[peer].astype(F32)
    dt_low = low[:rank].astype(BF16)
    in_map = low[rank : rank + states]
    maps_ref[...] = low[rank:]
    raw = dot(dt_low, dtw_ref[...], TN) + rows_ref[0:1, :]
    small = jnp.exp(-jnp.abs(raw))
    series = small * (1.0 - small * (0.5 - small * (1.0 / 3.0 - small * 0.25)))
    step = jnp.maximum(raw, 0.0) + jnp.where(small < 0.01, series, jnp.log(1.0 + small))
    drive_step[...] = step * jnp.transpose(act_ref[...].astype(F32))
    step = jnp.where(first_ref[...] > 0.5, FAR, step)
    decay_step[...] = step
    last = jnp.sum(step, axis=0, keepdims=True)
    rate = rate_ref[...] * (-LOG2E)
    stretches = 4
    length = tokens // stretches
    parts = [jnp.zeros((states, channels), F32)] * stretches
    for offset in range(length):
        for index in range(stretches):
            t = index * length + offset
            decay = jnp.exp2(decay_step[t : t + 1, :] * rate)
            parts[index] = decay * parts[index] + drive_step[t : t + 1, :] * in_map[:, t : t + 1]
    state = parts[0]
    for index in range(1, stretches):
        spent = jnp.sum(step[index * length : (index + 1) * length], axis=0, keepdims=True)
        state = jnp.exp2(spent * rate) * state + parts[index]
    message = join(state, last, send_ref.shape[2])
    for peer in range(send_ref.shape[0]):
        send_ref[peer] = message


def row_body(me, in_ref, rate_ref, send_ref, before_ref, length_ref):
    states, channels = rate_ref.shape
    rate = rate_ref[...] * (-LOG2E)
    whole = jnp.zeros((states, channels), F32)
    before = whole
    whole_length = jnp.zeros((1, channels), F32)
    before_length = whole_length
    for peer in range(in_ref.shape[0]):
        final, length = part(in_ref[peer], channels)
        earlier = peer < me[0]
        through = jnp.exp2(length * rate)
        whole = through * whole + final
        before = jnp.where(earlier, whole, before)
        whole_length = whole_length + length
        before_length = jnp.where(earlier, whole_length, before_length)
    message = join(whole, whole_length, send_ref.shape[2])
    for peer in range(send_ref.shape[0]):
        send_ref[peer] = message
    before_ref[...] = before
    length_ref[...] = jnp.broadcast_to(before_length, length_ref.shape)


def side_body(
    features, in_ref, weight_hbm, act_ref, rate_ref, rows_ref, decay_step, drive_step, maps_ref, row_ref,
    out_ref, share_ref, wide, gate_weight, hidden, gate_token, sem,
):
    count = in_ref.shape[0]
    tokens = in_ref.shape[2]
    states, channels = rate_ref.shape
    fetch = pltpu.make_async_copy(weight_hbm.at[channels:], gate_weight, sem)
    fetch.start()
    sums = jnp.zeros((16, tokens), F32)
    for peer in range(count):
        wide[peer * features : (peer + 1) * features, :] = in_ref[peer, 0:features, :]
        sums = sums + in_ref[peer, features : features + 16, :].astype(F32)
    scale = lax.rsqrt(square_sums(sums, features)[0] / (count * features) + EPSILON)
    in_map = maps_ref[0:states, :]
    out_map = maps_ref[states:, :]
    step = decay_step[...]
    high = step.astype(BF16)
    rest = (step - high.astype(F32)).astype(BF16)
    lower = jnp.where(iota((tokens, tokens), 0) >= iota((tokens, tokens), 1), 1.0, 0.0).astype(BF16)
    elapsed = dot(lower, high) + dot(lower, rest)
    spread = jnp.where((iota((states, tokens), 1) & (states - 1)) == iota((states, tokens), 0), 1.0, 0.0)
    maps = dot(out_map.astype(BF16), spread.astype(BF16), TN)
    own = (iota((tokens, tokens), 1) // states) == (iota((tokens, tokens), 0) & 7)
    maps = jnp.where(own, maps, 0.0).astype(BF16)
    out_ref[...] = rows_ref[1:2, :] * jnp.transpose(act_ref[...].astype(F32))
    fetch.wait()
    gate = dot(gate_weight[...], wide[...])
    gate = (gate * scale).astype(BF16).astype(F32)
    gate_token[...] = jnp.transpose(gate * (1.0 / (1.0 + jnp.exp(-gate))))
    rate = rate_ref[...] * (-LOG2E)
    by_token = jnp.transpose(out_map)
    for index in range(states):
        remains = jnp.exp2(elapsed * rate[index : index + 1, :]) * gate_token[...]
        share_ref[index] = (by_token[:, index : index + 1] * remains).astype(BF16)
    state = jnp.zeros((states, channels), F32)
    for block in range(tokens // 8):
        for inner in range(8):
            t = block * 8 + inner
            decay = jnp.exp2(decay_step[t : t + 1, :] * rate)
            state = decay * state + drive_step[t : t + 1, :] * in_map[:, t : t + 1]
            hidden[inner * states : (inner + 1) * states, :] = state.astype(BF16)
        out_ref[block * 8 : block * 8 + 8, :] += dot(maps[block * 8 : block * 8 + 8], hidden[...])
    out_ref[...] *= gate_token[...]


def finish_body(me, in_ref, rate_ref, before_ref, length_ref, out_in_ref, share_ref, mixed_ref):
    states, channels = rate_ref.shape
    rate = rate_ref[...] * (-LOG2E)
    state = jnp.zeros((states, channels), F32)
    for peer in range(in_ref.shape[0]):
        final, length = part(in_ref[peer], channels)
        earlier = peer < me[0]
        through = jnp.where(earlier, jnp.exp2(length * rate), 1.0)
        state = through * state + jnp.where(earlier, final, 0.0)
    state = jnp.exp2(length_ref[0:1, :] * rate) * state + before_ref[...]
    scanned = out_in_ref[...]
    for index in range(states):
        scanned = scanned + share_ref[index].astype(F32) * state[index : index + 1, :]
    mixed_ref[...] = jnp.transpose(scanned.astype(BF16))


def local(
    tokens, norm_gain, in_weight, conv_weight, conv_bias, proj_weight, dt_weight, dt_bias,
    decay_rate, skip_gain, doc_starts, group_target,
):
    rows_of, in_row = lax.axis_size("z"), lax.axis_size("x")
    peers = rows_of * in_row
    row_count, features = tokens.shape
    slots = group_target.shape[0]
    width = in_weight.shape[0]
    channels = in_weight.shape[2]
    rank = dt_weight.shape[0]
    states = decay_rate.shape[1]
    shape = jax.ShapeDtypeStruct
    me = lax.axis_index(("z", "x")).astype(jnp.int32).reshape(1)
    starts = doc_starts.reshape(1, row_count)
    my_gain = lax.dynamic_slice_in_dim(norm_gain, lax.axis_index("chan") * features, features)
    my_gain = jnp.broadcast_to(my_gain[:, None], (features, row_count))
    weight = jnp.transpose(in_weight, (1, 2, 0)).reshape(2 * channels, width)
    pieces, starts = call(
        functools.partial(pack_body, slots),
        (shape((peers, 16, row_count), BF16), shape((1, row_count), jnp.int32)),
        [SMEM, HBM, HBM, HBM],
        (me, in_hbm(group_target), in_hbm(tokens.T), in_hbm(starts)),
        [
            pltpu.SMEM((slots,), jnp.int32),
            pltpu.VMEM((features, row_count), BF16),
            pltpu.VMEM((2 * peers + 1, 16, row_count), F32),
            pltpu.SemaphoreType.DMA((3,)),
        ],
    )
    weight = in_hbm(weight)
    sources = (proj_weight.T, dt_weight, decay_rate.T, conv_weight, conv_bias, dt_bias, skip_gain)
    scan_weight, proj, dtw, rate, cols, rows, first = call(
        fetch_body,
        (
            shape((channels, width), BF16),
            shape((rank + 2 * states, channels), BF16),
            shape((rank, channels), BF16),
            shape((states, channels), F32),
            shape((channels, 8), F32),
            shape((8, channels), F32),
            shape((row_count, channels), F32),
        ),
        [HBM] * 8 + [VMEM],
        (weight, *(in_hbm(source) for source in sources), starts),
        [
            pltpu.VMEM(conv_weight.shape, F32),
            pltpu.VMEM((channels,), F32),
            pltpu.VMEM((channels,), F32),
            pltpu.VMEM((channels,), F32),
            pltpu.SemaphoreType.DMA((8,)),
        ],
    )
    arrived = lax.all_to_all(pieces, ("z", "x"), 0, 0, tiled=True)
    payload = call(
        place_body,
        shape((features + 16, row_count), BF16),
        [VMEM, VMEM],
        (arrived, my_gain),
    )
    gathered = lax.all_gather(payload, "chan", axis=0)
    low, act = call(
        functools.partial(project_body, features, conv_weight.shape[0]),
        (shape((rank + 2 * states, row_count), BF16), shape((channels, row_count), BF16)),
        [VMEM] * 5,
        (gathered, scan_weight, cols, proj, starts),
        [pltpu.VMEM((width, 2 * row_count), BF16)],
    )
    lows = lax.all_gather(low, "chan", axis=0)
    lanes = -(-channels // 128) * 128
    by_token = shape((row_count, channels), F32)
    send, decay_step, drive_step, maps = call(
        functools.partial(state_body, rank),
        (
            shape((in_row, states, lanes), BF16),
            by_token,
            by_token,
            shape((2 * states, row_count), F32),
        ),
        [VMEM] * 6,
        (lows, act, dtw, rate, rows, first),
    )
    in_row_ends = lax.all_to_all(send, "x", 0, 0, tiled=True)
    send, before, before_length = call(
        row_body,
        (
            shape((rows_of, states, lanes), BF16),
            shape((states, channels), F32),
            shape((8, channels), F32),
        ),
        [SMEM, VMEM, VMEM],
        (lax.axis_index("x").astype(jnp.int32).reshape(1), in_row_ends, rate),
    )
    out, share = call(
        functools.partial(side_body, features),
        (by_token, shape((states, row_count, channels), BF16)),
        [VMEM, HBM] + [VMEM] * 7,
        (gathered, weight, act, rate, rows, decay_step, drive_step, maps, before_length),
        [
            pltpu.VMEM((width, row_count), BF16),
            pltpu.VMEM((channels, width), BF16),
            pltpu.VMEM((8 * states, channels), BF16),
            pltpu.VMEM((row_count, channels), F32),
            pltpu.SemaphoreType.DMA,
        ],
    )
    ends = lax.all_to_all(send, "z", 0, 0, tiled=True)
    my_row = lax.axis_index("z").astype(jnp.int32).reshape(1)
    mixed = call(
        finish_body,
        shape((channels, row_count), BF16),
        [SMEM] + [VMEM] * 6,
        (my_row, ends, rate, before, before_length, out, share),
    )
    return mixed.T


def solution(mesh):
    peers, chans = mesh.devices.shape
    in_row = 4 if peers % 4 == 0 else 1
    grid = mesh.devices.reshape(peers // in_row, in_row, chans)
    mesh = jax.sharding.Mesh(grid, ("z", "x", "chan"))
    return jax.shard_map(
        local,
        mesh=mesh,
        in_specs=(
            P(("z", "x"), "chan"),
            P(),
            P(None, None, "chan"),
            P(None, "chan"),
            P("chan"),
            P("chan", None),
            P(None, "chan"),
            P("chan"),
            P("chan", None),
            P("chan"),
            P(("z", "x")),
            P(("z", "x")),
        ),
        out_specs=P(("z", "x"), "chan"),
        check_vma=False,
    )
```
